32 devices in a mesh: az: 8 (over z, x), ax: 4 (over y, core).
Axes of the slice: x: 2, y: 2, z: 4, core: 2. Of those that a mesh axis runs over, the one named last changes fastest.
Arguments:
- state: float32 [1536, 5, 512], P(('az', 'ax')), may hold values from -6 to 6
- velocity: float32 [1536, 3], P(('az', 'ax')), may hold values from -4 to 4
- interp_maps: float32 [1536, 3, 8, 8], P(('az', 'ax')), may hold values from -2 to 2
- neighbours: int32 [1536, 6], P(('az', 'ax')), may hold values from 0 to 479
- send_faces: int32 [1536], P(('az', 'ax')), may hold values from 0 to 287
- owner_device: int32 [1536, 1], P(('az', 'ax')), may hold values from 0 to 7; in each aligned block of 48 rows (0 to 47, 48 to 95, ...) at most 15 rows name the same one
- owner_block: int32 [1536], P(('az', 'ax')), may hold values from 0 to 7
Outputs:
- new_state: float32 [1536, 5, 512], P(('az', 'ax'))
- spectrum: float32 [2, 5, 1024, 128], P(None, None, ('az', 'ax'))
The draws below stay inside these ranges and needn't reach their ends.
Inputs may be any that keep to these rules, and one draw needn't show every extreme that they name: `owner_device`: in the rows of one device at most 15 elements name the same owner sector, and 15 is reached in some device.
All inputs are finite; a program needn't handle non-finite values.
Results may differ from the reference program's by a relative error of at most 0.0003.
Values sent between devices are 32-bit elements; how exact they have to be, the bound alone decides.
No kernel may reach another device: no remote copies, remote signals or barrier semaphores. Data moves between devices by JAX's collectives and lax.ppermute only.
A program may use at most 64 MiB of HBM per device.

```python
import math
import jax
import jax.numpy as jnp
import numpy as np
from jax import lax

E_DEV = 48
TB = 2
PB = 4
CB_DEV = 8
CAP = 15
E_TOTAL = 1536
NTH = 128
CYCLE_DEV = 32
CYCLES = 1024
FACE_SLOTS = 480
N_AZ = 8
N_AX = 4


def plant(array, rng, smallest, high):
    longest = array.shape.index(max(array.shape))
    spots = []
    for shift in (0, 1):
        where = [jax.random.randint(jax.random.fold_in(rng, axis), (), 0, length) for axis, length in enumerate(array.shape)]
        where[longest] = (where[longest] + shift) % array.shape[longest]
        spots.append(tuple(where))
    return array.at[spots[0]].set(smallest).at[spots[1]].set(high)


def block_levels(rng, extent, shards, least, high):
    gain = 1.0
    for axis_at, shards_of in shards:
        steps = jax.random.uniform(jax.random.fold_in(jax.random.fold_in(rng, 6), axis_at), (shards_of,), jnp.float32, least / len(shards), high / len(shards))
        gain = gain * jnp.repeat(jnp.exp(steps), extent[axis_at] // shards_of).reshape((-1,) + (1,) * (len(extent) - 1 - axis_at))
    return gain


def deal_out(key, own, number, rows, number_of, top, reach, skew):
    order = jax.random.permutation(key, number_of)
    crowded, usual = shares(number_of, rows * top, reach, skew, True), shares(number_of, rows * top, reach, skew, False)
    places = jnp.arange(number_of)

    def named(lengths, offset_by):
        used = int((lengths > 0).sum())
        fixed = max(1, used // 4)
        moved = fixed + (places - fixed + offset_by * (used - fixed)) % max(1, number_of - fixed)
        return jnp.zeros((number_of,), jnp.int32).at[order[jnp.where(places < fixed, places, moved)]].set(jnp.asarray(lengths, jnp.int32))

    lengths = jnp.where(number % 4 == 0, named(crowded, number // 4), named(usual, number - number // 4 - 1))
    mixed = jax.random.permutation(jax.random.fold_in(own, 3), number_of)
    source_of, sink = mixed[0:number_of // 2 * 2:2], mixed[1:number_of // 2 * 2:2]
    margin = jnp.minimum(lengths[source_of] - 1, reach - lengths[sink]) // 2
    margin = jnp.where((source_of == order[0]) | (sink == order[0]) | (lengths[sink] == 0), 0, jnp.maximum(margin, 0))
    moved = jax.random.randint(jax.random.fold_in(own, 4), (number_of // 2,), 0, 1 << 20) % (margin + 1)
    lengths = lengths.at[source_of].add(-moved).at[sink].add(moved)
    labels = jnp.searchsorted(jnp.cumsum(lengths), jnp.arange(rows * top), side="right").astype(jnp.int32)
    grid = labels.reshape(top, rows).T
    grid = grid[jax.random.permutation(jax.random.fold_in(own, 1), rows)]
    offset_by = jax.random.randint(jax.random.fold_in(own, 2), (rows, 1), 0, top)
    return jnp.take_along_axis(grid, (jnp.arange(top)[None, :] + offset_by) % top, axis=1)


def shares(amount, total, bound, skew, full):
    loads = [(1 << 20) // math.isqrt(grade ** skew) + 1 for grade in range(1, amount + 1)]
    largest = bound if full else min(bound, max(-(-total // amount), total * loads[0] // sum(loads)))
    least = 1 if total - largest >= amount - 1 else 0
    counts, rest = [largest] + [least] * (amount - 1), total - largest - least * (amount - 1)
    while rest > 0:
        candidates = [i for i in range(1, amount) if counts[i] < largest] or [i for i in range(1, amount) if counts[i] < bound]
        whole, left = sum([loads[i] for i in candidates]), rest
        for i in candidates:
            more = min(bound - counts[i], max(1, left * loads[i] // whole), rest)
            counts[i] = counts[i] + more
            rest = rest - more
    return np.array(counts)


def scatter_about(rng, dims, scale, limit, shards=(), kind=jnp.bfloat16):
    drawn = jax.random.normal(rng, dims, jnp.float32) * scale
    if len(shards) > 0:
        drawn = block_levels(rng, dims, shards, -0.22, 0.18) * drawn
    return jnp.clip(drawn, min=-limit, max=limit).astype(kind)


def setup_inputs(seed: int = 0) -> dict:
    seeds = jax.random.split(jax.random.key(seed), 8)
    state = scatter_about(seeds[0], (E_TOTAL, 5, 512), 1.0, 6.0, ((0, 32),), jnp.float32)
    velocity = scatter_about(seeds[1], (E_TOTAL, 3), 1.0, 4.0, ((0, 32),), jnp.float32)
    interp_maps = scatter_about(seeds[2], (E_TOTAL, 3, 8, 8), 8 ** -0.5, 2.0, ((0, 32),), jnp.float32)
    neighbours = plant(jax.random.randint(seeds[3], (E_TOTAL, 6), 0, FACE_SLOTS), jax.random.fold_in(seeds[3], 1), 0, FACE_SLOTS - 1).astype(jnp.int32)
    send_faces = plant(jax.random.randint(seeds[4], (E_TOTAL,), 0, 6 * E_DEV), jax.random.fold_in(seeds[4], 1), 0, (6 * E_DEV) - 1).astype(jnp.int32)
    owner_device_keys = jax.random.split(jax.random.fold_in(seeds[5], 1), E_TOTAL // E_DEV)
    owner_device_turns = jax.random.permutation(jax.random.fold_in(seeds[5], 3), E_TOTAL // E_DEV)
    owner_device = jax.vmap(lambda own, number: deal_out(jax.random.fold_in(seeds[5], 2), own, number, E_DEV, N_AZ, 1, CAP, 1))(owner_device_keys, owner_device_turns).reshape((E_TOTAL, 1))
    owner_block = plant(jax.random.randint(seeds[6], (E_TOTAL,), 0, CB_DEV), jax.random.fold_in(seeds[6], 1), 0, CB_DEV - 1).astype(jnp.int32)
    return dict(state=state, velocity=velocity, interp_maps=interp_maps, neighbours=neighbours, send_faces=send_faces, owner_device=owner_device, owner_block=owner_block)


time_step = 0.02
penalty = 5.0
highest = lax.Precision.HIGHEST


def spectral_derivative():
    points = np.cos(np.pi * np.arange(8) / 7.0)
    ends = (np.arange(8) == 0) | (np.arange(8) == 7)
    scales = np.where(ends, 2.0, 1.0)
    signs = np.where(np.arange(8) % 2 == 0, 1.0, -1.0)
    differ = points[:, None] - points[None, :]
    offdiag = (scales[:, None] / scales[None, :]) * signs[:, None] * signs[None, :] / np.where(np.eye(8) > 0, 1.0, differ)
    inner = -points / (2.0 * np.where(ends, 1.0, 1.0 - points * points))
    corner = (2.0 * 49.0 + 1.0) / 6.0
    diagonal = np.where(np.arange(8) == 0, corner, np.where(np.arange(8) == 7, -corner, inner))
    return np.where(np.eye(8) > 0, diagonal[:, None], offdiag)


def derivative_table():
    deriv = spectral_derivative()
    along_x = np.kron(deriv, np.eye(64))
    along_y = np.kron(np.eye(8), np.kron(deriv, np.eye(8)))
    along_z = np.kron(np.eye(64), deriv)
    return np.concatenate([along_x.T, along_y.T, along_z.T], axis=1)


def face_selector():
    node_grid = np.arange(512).reshape(8, 8, 8)
    face_lists = [node_grid[0], node_grid[7], node_grid[:, 0], node_grid[:, 7], node_grid[:, :, 0], node_grid[:, :, 7]]
    picked = np.concatenate([square.reshape(-1) for square in face_lists])
    return (np.arange(512)[:, None] == picked[None, :]).astype(np.float32)


def group_rate(state, velocity, neighbours, send_faces):
    slices = velocity.shape[0]
    elements = velocity.shape[1]
    deriv = jnp.asarray(derivative_table(), jnp.float32)
    selector = jnp.asarray(face_selector(), jnp.float32)
    flat_state = state.reshape(slices * elements * 5, 512)
    derivs = jnp.dot(flat_state, deriv, precision=highest, preferred_element_type=jnp.float32)
    derivs = derivs.reshape(slices, elements, 5, 3, 512)
    advect = -jnp.einsum('sed,secdn->secn', velocity, derivs, precision=highest)
    own_faces = jnp.dot(flat_state, selector, precision=highest, preferred_element_type=jnp.float32)
    own_faces = own_faces.reshape(slices, elements, 5, 6, 64)
    local_table = own_faces.transpose(0, 1, 3, 2, 4).reshape(slices, elements * 6, 320)
    shared = jnp.take_along_axis(local_table, send_faces.astype(jnp.int32)[:, :, None], axis=1)
    gathered = shared.reshape(slices * elements, 320)
    tables = jnp.concatenate([local_table, jnp.broadcast_to(gathered[None], (slices, slices * elements, 320))], axis=1)
    lookup = neighbours.astype(jnp.int32).reshape(slices, elements * 6)[:, :, None]
    facing = jnp.take_along_axis(tables, lookup, axis=1)
    facing = facing.reshape(slices, elements, 6, 5, 64).transpose(0, 1, 3, 2, 4)
    face_jump = penalty * (facing - own_faces)
    lifted = jnp.dot(face_jump.reshape(-1, 384), selector.T, precision=highest, preferred_element_type=jnp.float32)
    return advect + lifted.reshape(slices, elements, 5, 512)


def interpolate(flat_state, interp_maps):
    node_cube = flat_state.reshape(-1, 5, 8, 8, 8)
    partial_value = jnp.einsum('erx,ecxyz->ecryz', interp_maps[:, 1], node_cube, precision=highest)
    partial_value = jnp.einsum('ety,ecryz->ectrz', interp_maps[:, 0], partial_value, precision=highest)
    partial_value = jnp.einsum('eqz,ectrz->ectrq', interp_maps[:, 2], partial_value, precision=highest)
    return partial_value.reshape(-1, 5 * 512)


def reference(state, velocity, interp_maps, neighbours, send_faces, owner_device, owner_block):
    grouped = (state.reshape(N_AZ, N_AX, E_DEV, 5, 512), velocity.reshape(N_AZ, N_AX, E_DEV, 3),
               neighbours.reshape(N_AZ, N_AX, E_DEV, 6), send_faces.reshape(N_AZ, N_AX, E_DEV),
               interp_maps.reshape(N_AZ, N_AX * E_DEV, 3, 8, 8))

    def advance(group_data):
        block_state, block_velocity, block_neighbours, block_sends, block_maps = group_data
        first_section = block_state + time_step * group_rate(block_state, block_velocity, block_neighbours, block_sends)
        second = 0.5 * (block_state + first_section + time_step * group_rate(first_section, block_velocity, block_neighbours, block_sends))
        return second, interpolate(second.reshape(-1, 5, 512), block_maps)

    advanced, blocks = lax.map(advance, grouped)
    slice_index = jnp.arange(N_AX, dtype=jnp.int32)[None, :, None]
    owners = owner_device.astype(jnp.int32).reshape(N_AZ, N_AX, E_DEV)
    targets = (owners * N_AX + slice_index) * CB_DEV + owner_block.astype(jnp.int32).reshape(N_AZ, N_AX, E_DEV)
    cylinder = jax.ops.segment_sum(blocks.reshape(-1, 2560), targets.reshape(-1), num_segments=N_AZ * N_AX * CB_DEV)
    cylinder = cylinder.reshape(N_AZ, N_AX, TB, PB, 5, 8, 64)
    cycle_data = cylinder.transpose(1, 4, 3, 6, 0, 2, 5).reshape(N_AX, 5, PB * 64, NTH)
    coeffs = jnp.fft.fft(cycle_data, axis=-1)
    stacked = jnp.stack([jnp.real(coeffs), jnp.imag(coeffs)]) * (NTH ** -0.5)
    stacked = stacked.reshape(2, N_AX, 5, N_AZ, CYCLE_DEV, NTH).transpose(0, 2, 3, 1, 4, 5)
    spectrum = stacked.reshape(2, 5, CYCLES, NTH)
    return advanced.reshape(E_TOTAL, 5, 512), spectrum
```

```python
import functools
import math

import jax
import jax.numpy as jnp
import numpy as np
from jax import lax
from jax.experimental import pallas as pl
from jax.experimental.pallas import tpu as pltpu
from jax.sharding import PartitionSpec as P

TB = 2
PB = 4
FIELDS = 5
time_step = 0.02
penalty = 5.0
highest = lax.Precision.HIGHEST
f32 = jnp.float32
bf16 = jnp.bfloat16


def spectral_derivative():
    points = np.cos(np.pi * np.arange(8) / 7.0)
    ends = (np.arange(8) == 0) | (np.arange(8) == 7)
    scales = np.where(ends, 2.0, 1.0)
    signs = np.where(np.arange(8) % 2 == 0, 1.0, -1.0)
    differ = points[:, None] - points[None, :]
    offdiag = (
        scales[:, None]
        / scales[None, :]
        * signs[:, None]
        * signs[None, :]
        / np.where(np.eye(8) > 0, 1.0, differ)
    )
    inner = -points / (2.0 * np.where(ends, 1.0, 1.0 - points * points))
    corner = (2.0 * 49.0 + 1.0) / 6.0
    diagonal = np.where(np.arange(8) == 0, corner, np.where(np.arange(8) == 7, -corner, inner))
    return np.where(np.eye(8) > 0, diagonal[:, None], offdiag)


def np_split(table):
    table = np.asarray(table, np.float32)
    high = table.astype(jnp.bfloat16)
    low = (table - high.astype(np.float32)).astype(jnp.bfloat16)
    return high, low


def face_nodes():
    grid = np.arange(512).reshape(8, 8, 8)
    faces = [grid[0], grid[7], grid[:, 0], grid[:, 7], grid[:, :, 0], grid[:, :, 7]]
    return [square.reshape(-1) for square in faces]


def make_tables():
    deriv = spectral_derivative()
    along_x = np.kron(deriv, np.eye(64)).T
    in_tile_y = np.kron(np.eye(2), np.kron(deriv, np.eye(8))).T
    in_tile_z = np.kron(np.eye(16), deriv).T
    picks = face_nodes()
    nodes = np.arange(512)
    extract = np.concatenate(
        [nodes[:, None] == np.tile(square, 2)[None, :] for square in picks], axis=1
    ).astype(jnp.bfloat16)
    lift = np.concatenate(
        [square[:, None] == nodes[None, :] for square in picks], axis=0
    ).astype(jnp.bfloat16)
    count = lift.astype(np.float32).sum(axis=0)[None, :]
    x_high, x_low = np_split(along_x)
    yz_high, yz_low = np_split(np.concatenate([in_tile_y, in_tile_z], axis=1))
    return dict(
        x_high=x_high,
        x_low=x_low,
        yz_high=yz_high,
        yz_low=yz_low,
        extract=extract,
        lift=lift,
        count=count.astype(np.float32),
    )


def split(value):
    high = value.astype(bf16)
    return high, (value - high.astype(f32)).astype(bf16)


def dot(a, b):
    return jnp.dot(a, b, preferred_element_type=f32)


def low_half(shape):
    return lax.broadcasted_iota(jnp.int32, shape, len(shape) - 1) < 64


def local_key(elements):
    lane = lax.broadcasted_iota(jnp.int32, (1, 6 * elements), 1)
    face = jnp.zeros_like(lane)
    for f in range(1, 6):
        face = face + (lane >= f * elements).astype(jnp.int32)
    return 6 * (lane - face * elements) + face


def column(row_ref):
    return row_ref[...].astype(f32).T


def pick_rows(names, keys):
    return jnp.where(names == keys.astype(f32), 1.0, 0.0).astype(bf16)


def face_tables(fields, extract):
    elements = fields.shape[0] // FIELDS
    parts = []
    for part in split(fields):
        faces = dot(part, extract).astype(bf16)
        rows = [
            jnp.concatenate(
                [
                    faces[c * elements : (c + 1) * elements, f * 128 : (f + 1) * 128]
                    for c in range(FIELDS)
                ],
                axis=1,
            )
            for f in range(6)
        ]
        parts.append(jnp.concatenate(rows, axis=0))
    return parts


def share_rows(table_high, table_low, send_ref, out_ref):
    elements = send_ref.shape[1]
    picked = pick_rows(column(send_ref), local_key(elements))
    rows = dot(picked, table_high) + dot(picked, table_low)
    field = [rows[:, c * 128 : (c + 1) * 128] for c in range(FIELDS)]
    half = low_half((elements, 128))
    out_ref[0:elements, :] = jnp.where(half, field[0], field[1])
    out_ref[elements : 2 * elements, :] = jnp.where(half, field[2], field[3])
    middle = elements // 2
    out_ref[2 * elements :, :] = jnp.where(
        half[:middle], field[4][:middle], field[4][middle:]
    )


def unpack_rows(ref, elements):
    half = low_half((elements, 128))
    middle = elements // 2
    fields = []
    for first in range(2):
        both = ref[first * elements : (first + 1) * elements, :]
        turned = pltpu.roll(both, 64, 1)
        fields.append(jnp.where(half, both, turned))
        fields.append(jnp.where(half, turned, both))
    both = ref[2 * elements :, :]
    turned = pltpu.roll(both, 64, 1)
    fields.append(
        jnp.concatenate(
            [jnp.where(half[:middle], both, turned), jnp.where(half[:middle], turned, both)],
            axis=0,
        )
    )
    return jnp.concatenate(fields, axis=1)


def lift_rows(picked, tables, lift, elements):
    half = low_half((elements, 128))
    total = None
    for table in tables:
        facing = dot(picked, table)
        field_rows = []
        for c in range(FIELDS):
            blocks = [
                facing[f * elements : (f + 1) * elements, c * 128 : (c + 1) * 128]
                for f in range(6)
            ]
            pairs = [jnp.where(half, blocks[f], blocks[f + 1]) for f in range(0, 6, 2)]
            field_rows.append(jnp.concatenate(pairs, axis=1))
        part = dot(jnp.concatenate(field_rows, axis=0).astype(bf16), lift)
        total = part if total is None else total + part
    return total


def local_rate(fields, velocity_ref, neigh_ref, tables, x_high, x_low, yz_high, yz_low, lift, count):
    elements = neigh_ref.shape[1]
    high, low = split(fields)
    along_x = dot(high, x_high) + dot(low, x_high) + dot(high, x_low)
    speed = velocity_ref[...].T
    speeds = [
        jnp.concatenate(
            [jnp.broadcast_to(speed[:, d : d + 1], (elements, 128))] * FIELDS, axis=0
        )
        for d in range(3)
    ]
    tiles = []
    for j in range(4):
        lanes = slice(j * 128, (j + 1) * 128)
        both = dot(high[:, lanes], yz_high) + dot(low[:, lanes], yz_high) + dot(high[:, lanes], yz_low)
        tiles.append(
            speeds[0] * along_x[:, lanes] + speeds[1] * both[:, :128] + speeds[2] * both[:, 128:]
        )
    names = column(neigh_ref)
    keys = local_key(elements)
    picked = jnp.concatenate([pick_rows(names[:, f : f + 1], keys) for f in range(6)], axis=0)
    lifted = lift_rows(picked, tables, lift, elements)
    return penalty * (lifted - count * fields) - jnp.concatenate(tiles, axis=1)


def remote_terms(me, neigh_ref, shared_refs, lift):
    elements = neigh_ref.shape[1]
    names = column(neigh_ref)
    lane = lax.broadcasted_iota(jnp.int32, (1, elements), 1)
    keys = jnp.concatenate(
        [6 * elements + (me ^ m) * elements + lane for m in range(len(shared_refs))], axis=1
    )
    picked = jnp.concatenate([pick_rows(names[:, f : f + 1], keys) for f in range(6)], axis=0)
    table = jnp.concatenate([unpack_rows(ref, elements) for ref in shared_refs], axis=0)
    return lift_rows(picked, split(table), lift, elements)


def rows_of(ref):
    fields, elements, nodes = ref.shape
    return ref[...].reshape(fields * elements, nodes)


def share_kernel(state_ref, send_ref, extract_ref, high_ref, low_ref, shared_ref):
    high, low = face_tables(rows_of(state_ref), extract_ref[...])
    high_ref[...] = high
    low_ref[...] = low
    share_rows(high, low, send_ref, shared_ref)


def first_local_kernel(
    state_ref, velocity_ref, neigh_ref, high_ref, low_ref,
    x_high, x_low, yz_high, yz_low, lift, count, out_ref,
):
    fields = rows_of(state_ref)
    rate = local_rate(
        fields, velocity_ref, neigh_ref, (high_ref[...], low_ref[...]),
        x_high[...], x_low[...], yz_high[...], yz_low[...], lift[...], count[...],
    )
    out_ref[...] = (fields + time_step * rate).reshape(out_ref.shape)


def first_finish_kernel(base_ref, neigh_ref, send_ref, lift, extract, *refs):
    shared_refs, (first_ref, high_ref, low_ref, shared_ref) = refs[:-4], refs[-4:]
    me = lax.axis_index("ax")
    terms = remote_terms(me, neigh_ref, shared_refs, lift[...])
    first = rows_of(base_ref) + (time_step * penalty) * terms
    first_ref[...] = first.reshape(first_ref.shape)
    high, low = face_tables(first, extract[...])
    high_ref[...] = high
    low_ref[...] = low
    share_rows(high, low, send_ref, shared_ref)


def second_local_kernel(
    state_ref, first_ref, velocity_ref, neigh_ref, high_ref, low_ref,
    x_high, x_low, yz_high, yz_low, lift, count, out_ref,
):
    fields = rows_of(first_ref)
    rate = local_rate(
        fields, velocity_ref, neigh_ref, (high_ref[...], low_ref[...]),
        x_high[...], x_low[...], yz_high[...], yz_low[...], lift[...], count[...],
    )
    out_ref[...] = (0.5 * (rows_of(state_ref) + fields + time_step * rate)).reshape(out_ref.shape)


def maps_kernel(maps_ref, device_ref, block_ref, radial_ref, axial_ref, high_ref, low_ref):
    elements = maps_ref.shape[2]
    row = lax.broadcasted_iota(jnp.int32, (elements, 128), 0)
    lane = lax.broadcasted_iota(jnp.int32, (elements, 128), 1)
    twice = ((lane & 63) == row).astype(f32)
    radial_ref[...] = jnp.dot(maps_ref[1], twice, precision=highest, preferred_element_type=f32)
    axial = jnp.dot(maps_ref[2], twice, precision=highest, preferred_element_type=f32)
    row64 = lax.broadcasted_iota(jnp.int32, (64, 64), 0)
    lane64 = lax.broadcasted_iota(jnp.int32, (64, 64), 1)
    swap = ((row64 >> 3) + 8 * (row64 & 7) == lane64).astype(f32)
    axial_ref[...] = jnp.dot(swap, axial, precision=highest, preferred_element_type=f32)
    azimuthal = maps_ref[0].T
    row_t = lax.broadcasted_iota(jnp.int32, (64, 128), 0)
    lane_t = lax.broadcasted_iota(jnp.int32, (64, 128), 1)
    places = device_ref[...].astype(f32).T
    blocks = block_ref[...].astype(f32).T
    theta_lanes = high_ref.shape[1] // PB
    high_ref[...] = jnp.zeros_like(high_ref)
    low_ref[...] = jnp.zeros_like(low_ref)
    upper = (blocks >= PB).astype(f32)
    sector_key = places * TB + upper
    plane_key = blocks - PB * upper
    for y in range(8):
        tile_t = ((row_t >> 3) == (lane_t & 7)) & ((row_t & 7) == y)
        values = jnp.dot(
            azimuthal, tile_t.astype(f32), precision=highest, preferred_element_type=f32
        )
        value_high, value_low = split(values)
        rows = pl.ds((y // 2) * 128 + (y % 2) * 64, elements)
        for pb in range(PB):
            for tile in range(theta_lanes // 128):
                here = ((lane + tile * 128) >> 3).astype(f32)
                mine = (sector_key == here) & (plane_key == pb)
                lanes = pl.ds(pb * theta_lanes + tile * 128, 128)
                high_ref[rows, lanes] = jnp.where(mine, value_high.astype(f32), 0.0).astype(bf16)
                low_ref[rows, lanes] = jnp.where(mine, value_low.astype(f32), 0.0).astype(bf16)


def sample_kernel(base_ref, neigh_ref, lift, radial_ref, axial_ref, high_ref, low_ref, *refs):
    sectors = high_ref.shape[1] // (PB * TB * 8)
    shares = lax.axis_size("ax")
    shared_refs = refs[:shares]
    new_ref, out_refs = refs[shares], refs[shares + 1 : shares + 1 + sectors]
    turned_ref, mapped_ref, parts_ref = refs[shares + 1 + sectors :]
    elements = neigh_ref.shape[1]
    me = lax.axis_index("ax")
    terms = remote_terms(me, neigh_ref, shared_refs, lift[...])
    new_state = rows_of(base_ref) + (0.5 * time_step * penalty) * terms
    new_ref[...] = new_state.reshape(new_ref.shape)
    gap = jnp.zeros((64 - elements, 128), f32)
    for c in range(FIELDS):
        for j in range(4):
            part = new_state[c * elements : (c + 1) * elements, j * 128 : (j + 1) * 128]
            after = pltpu.roll(part, 120, 1)
            turned_ref[c, j] = jnp.concatenate([part, gap, after, gap], axis=0).T
    radial = radial_ref[...]
    axial = axial_ref[...]
    for c in range(FIELDS):
        for yy in range(4):
            inputs = []
            for x in range(8):
                start = (x % 2) * 64 + 16 * yy
                inputs.append(turned_ref[c, x // 2, start : start + 8, :])
            for r in range(8):
                mixed = radial[8 * r : 8 * r + 1, :] * inputs[0]
                for x in range(1, 8):
                    mixed = mixed + radial[8 * r + x : 8 * r + x + 1, :] * inputs[x]
                value = axial[0:8, :] * mixed[0:1, :]
                for z in range(1, 8):
                    value = value + axial[8 * z : 8 * z + 8, :] * mixed[z : z + 1, :]
                row = (c * 8 + r) * 8
                mapped_ref[row : row + 8, yy * 128 : (yy + 1) * 128] = value
    mapped_high, mapped_low = split(mapped_ref[...])
    theta_lanes = high_ref.shape[1] // PB
    groups = sectors // PB
    rows = 64 // groups
    for pb in range(PB):
        lanes = pl.ds(pb * theta_lanes, theta_lanes)
        weight_high = high_ref[:, lanes]
        total = (
            dot(mapped_high, weight_high)
            + dot(mapped_low, weight_high)
            + dot(mapped_high, low_ref[:, lanes])
        )
        for g in range(groups):
            for c in range(FIELDS):
                start = c * 64 + g * rows
                parts_ref[pb * groups + g, c * rows : (c + 1) * rows, :] = total[start : start + rows]
    owner = lax.axis_index("az")
    for m in range(sectors):
        out_refs[m][...] = parts_ref[owner ^ m]


def fourier_kernel(high_ref, low_ref, *refs):
    out_ref = refs[-1]
    total = refs[0][...]
    for ref in refs[1:-1]:
        total = total + ref[...]
    high, low = split(total)
    weight = high_ref[...]
    coeffs = dot(high, weight) + dot(low, weight) + dot(high, low_ref[...])
    width = total.shape[1]
    rows = total.shape[0] // FIELDS
    for k in range(2):
        for c in range(FIELDS):
            out_ref[k, c] = coeffs[c * rows : (c + 1) * rows, k * width : (k + 1) * width]


def shape(dims, dtype=f32):
    return jax.ShapeDtypeStruct(dims, dtype)


def call(kernel, outs, *args, scratch=(), flops=0):
    size = sum(math.prod(a.shape) * a.dtype.itemsize for a in list(args) + list(outs))
    return pl.pallas_call(
        kernel,
        out_shape=outs,
        scratch_shapes=list(scratch),
        cost_estimate=pl.CostEstimate(flops=flops, bytes_accessed=size, transcendentals=0),
        compiler_params=pltpu.CompilerParams(vmem_limit_bytes=48 * 1024 * 1024),
    )(*args)


def exchange(value, axis):
    size = lax.axis_size(axis)
    return [value] + [
        lax.ppermute(value, axis, [(i, i ^ m) for i in range(size)]) for m in range(size - 1, 0, -1)
    ][::-1]


def per_device(state, velocity, interp_maps, neighbours, send_faces, owner_device, owner_block):
    elements = state.shape[0]
    sectors = lax.axis_size("az")
    fields = state.transpose(1, 0, 2)
    speed = velocity.T
    names = neighbours.T
    maps = interp_maps.transpose(1, 2, 3, 0).reshape(3, 64, elements)
    sends = send_faces.reshape(1, elements)
    tables = {name: jnp.asarray(value) for name, value in make_tables().items()}
    rate_tables = [tables[k] for k in ("x_high", "x_low", "yz_high", "yz_low", "lift", "count")]
    cube = shape(fields.shape)
    face_rows = shape((6 * elements, FIELDS * 128), bf16)
    travel = shape((FIELDS * elements // 2, 128))
    high, low, shared = call(
        share_kernel, (face_rows, face_rows, travel), fields, sends, tables["extract"],
        flops=400_000_000,
    )
    others = exchange(shared, "ax")
    base = call(
        first_local_kernel, (cube,), fields, speed, names, high, low, *rate_tables,
        flops=1_000_000_000,
    )[0]
    first, high, low, shared = call(
        first_finish_kernel, (cube, face_rows, face_rows, travel),
        base, names, sends, tables["lift"], tables["extract"], *others,
        flops=600_000_000,
    )
    others = exchange(shared, "ax")
    base = call(
        second_local_kernel, (cube,), fields, first, speed, names, high, low, *rate_tables,
        flops=1_000_000_000,
    )[0]
    lanes = sectors * TB * 8
    weights = shape((512, PB * lanes), bf16)
    radial, axial, weight_high, weight_low = call(
        maps_kernel, (shape((64, 128)), shape((64, 128)), weights, weights),
        maps, owner_device.reshape(1, elements), owner_block.reshape(1, elements),
        flops=100_000_000,
    )
    rows = FIELDS * 64 * PB // sectors
    pieces = call(
        sample_kernel, (cube,) + (shape((rows, lanes)),) * sectors,
        base, names, tables["lift"], radial, axial, weight_high, weight_low, *others,
        scratch=(
            pltpu.VMEM((FIELDS, 4, 128, 128), f32),
            pltpu.VMEM((FIELDS * 64, 512), f32),
            pltpu.VMEM((sectors, rows, lanes), f32),
        ),
        flops=800_000_000,
    )
    new_state, pieces = pieces[0], pieces[1:]
    arrived = [pieces[0]] + [
        lax.ppermute(pieces[m], "az", [(i, i ^ m) for i in range(sectors)])
        for m in range(sectors - 1, 0, -1)
    ]
    angle = 2.0 * np.pi / lanes * (np.outer(np.arange(lanes), np.arange(lanes)) % lanes)
    table = np.concatenate([np.cos(angle), -np.sin(angle)], axis=1) * lanes**-0.5
    table_high, table_low = np_split(table)
    spectrum = call(
        fourier_kernel, (shape((2, FIELDS, rows // FIELDS, lanes)),),
        jnp.asarray(table_high), jnp.asarray(table_low), *arrived,
        flops=100_000_000,
    )[0]
    return new_state.transpose(1, 0, 2), spectrum


def solution(mesh):
    return jax.shard_map(
        per_device,
        mesh=mesh,
        in_specs=(
            P(("az", "ax"), None, None),
            P(("az", "ax"), None),
            P(("az", "ax"), None, None, None),
            P(("az", "ax"), None),
            P(("az", "ax")),
            P(("az", "ax"), None),
            P(("az", "ax")),
        ),
        out_specs=(P(("az", "ax"), None, None), P(None, None, ("az", "ax"), None)),
        check_vma=False,
    )
```

```python
import functools
import math

import jax
import jax.numpy as jnp
import numpy as np
from jax import lax
from jax.experimental import pallas as pl
from jax.experimental.pallas import tpu as pltpu
from jax.sharding import PartitionSpec as P

TB = 2
PB = 4
FIELDS = 5
time_step = 0.02
penalty = 5.0
highest = lax.Precision.HIGHEST
f32 = jnp.float32
bf16 = jnp.bfloat16


def spectral_derivative():
    points = np.cos(np.pi * np.arange(8) / 7.0)
    ends = (np.arange(8) == 0) | (np.arange(8) == 7)
    scales = np.where(ends, 2.0, 1.0)
    signs = np.where(np.arange(8) % 2 == 0, 1.0, -1.0)
    differ = points[:, None] - points[None, :]
    offdiag = (
        scales[:, None]
        / scales[None, :]
        * signs[:, None]
        * signs[None, :]
        / np.where(np.eye(8) > 0, 1.0, differ)
    )
    inner = -points / (2.0 * np.where(ends, 1.0, 1.0 - points * points))
    corner = (2.0 * 49.0 + 1.0) / 6.0
    diagonal = np.where(np.arange(8) == 0, corner, np.where(np.arange(8) == 7, -corner, inner))
    return np.where(np.eye(8) > 0, diagonal[:, None], offdiag)


def tile_tables():
    deriv = spectral_derivative()
    along_y = np.kron(np.eye(2), np.kron(deriv, np.eye(8))).T
    along_z = np.kron(np.eye(16), deriv).T
    return np.concatenate([along_y, along_z], axis=1)


def face_node(face, position):
    first, second = position >> 3, position & 7
    if face < 2:
        return 448 * face + position
    if face < 4:
        return 56 * (face - 2) + 64 * first + second
    return 7 * (face - 4) + 64 * first + 8 * second


def iota(dims, axis):
    return lax.broadcasted_iota(jnp.int32, dims, axis)


def face_counts():
    node = iota((1, 512), 1)
    count = jnp.zeros((1, 512), f32)
    for coordinate in (node >> 6, (node >> 3) & 7, node & 7):
        count = count + jnp.where((coordinate == 0) | (coordinate == 7), 1.0, 0.0)
    return count


def split(value):
    high = value.astype(bf16)
    return high, (value - high.astype(f32)).astype(bf16)


def dot(a, b):
    return jnp.dot(a, b, preferred_element_type=f32)


def low_half(shape):
    return lax.broadcasted_iota(jnp.int32, shape, len(shape) - 1) < 64


def local_key(elements):
    lane = lax.broadcasted_iota(jnp.int32, (1, 6 * elements), 1)
    face = jnp.zeros_like(lane)
    for f in range(1, 6):
        face = face + (lane >= f * elements).astype(jnp.int32)
    return 6 * (lane - face * elements) + face


def column(row_ref):
    return row_ref[...].astype(f32).T


def pick_rows(names, keys):
    return jnp.where(names == keys.astype(f32), 1.0, 0.0).astype(bf16)


def face_tables(fields, extract):
    elements = fields.shape[0] // FIELDS
    parts = []
    for part in split(fields):
        faces = dot(part, extract).astype(bf16)
        rows = [
            jnp.concatenate(
                [
                    faces[c * elements : (c + 1) * elements, f * 128 : (f + 1) * 128]
                    for c in range(FIELDS)
                ],
                axis=1,
            )
            for f in range(6)
        ]
        parts.append(jnp.concatenate(rows, axis=0))
    return parts


def share_rows(table_high, table_low, send_ref, out_ref):
    elements = send_ref.shape[1]
    picked = pick_rows(column(send_ref), local_key(elements))
    rows = dot(picked, table_high) + dot(picked, table_low)
    field = [rows[:, c * 128 : (c + 1) * 128] for c in range(FIELDS)]
    half = low_half((elements, 128))
    out_ref[0:elements, :] = jnp.where(half, field[0], field[1])
    out_ref[elements : 2 * elements, :] = jnp.where(half, field[2], field[3])
    middle = elements // 2
    out_ref[2 * elements :, :] = jnp.where(
        half[:middle], field[4][:middle], field[4][middle:]
    )


def unpack_rows(ref, elements):
    half = low_half((elements, 128))
    middle = elements // 2
    fields = []
    for first in range(2):
        both = ref[first * elements : (first + 1) * elements, :]
        turned = pltpu.roll(both, 64, 1)
        fields.append(jnp.where(half, both, turned))
        fields.append(jnp.where(half, turned, both))
    both = ref[2 * elements :, :]
    turned = pltpu.roll(both, 64, 1)
    fields.append(
        jnp.concatenate(
            [jnp.where(half[:middle], both, turned), jnp.where(half[:middle], turned, both)],
            axis=0,
        )
    )
    return jnp.concatenate(fields, axis=1)


def lift_rows(picked, tables, lift, elements):
    half = low_half((elements, 128))
    total = None
    for table in tables:
        facing = dot(picked, table)
        field_rows = []
        for c in range(FIELDS):
            blocks = [
                facing[f * elements : (f + 1) * elements, c * 128 : (c + 1) * 128]
                for f in range(6)
            ]
            pairs = [jnp.where(half, blocks[f], blocks[f + 1]) for f in range(0, 6, 2)]
            field_rows.append(jnp.concatenate(pairs, axis=1))
        part = dot(jnp.concatenate(field_rows, axis=0).astype(bf16), lift)
        total = part if total is None else total + part
    return total


def x_derivative(fields):
    deriv = spectral_derivative()
    half = low_half((1, 128))
    tiles = [fields[:, 128 * i : 128 * i + 128] for i in range(4)]
    turned = [pltpu.roll(tile, 64, 1) for tile in tiles]
    out = []
    for j in range(4):
        total = None
        for i in range(4):
            same = jnp.where(half, float(deriv[2 * j, 2 * i]), float(deriv[2 * j + 1, 2 * i + 1]))
            cross = jnp.where(half, float(deriv[2 * j, 2 * i + 1]), float(deriv[2 * j + 1, 2 * i]))
            part = same * tiles[i] + cross * turned[i]
            total = part if total is None else total + part
        out.append(total)
    return out


def local_rate(fields, velocity_ref, neigh_ref, tables, yz_high, yz_low, lift):
    elements = neigh_ref.shape[1]
    high, low = split(fields)
    speed = velocity_ref[...].T
    speeds = [jnp.broadcast_to(speed[:, d : d + 1], (elements, 128)) for d in range(3)]
    both = []
    for j in range(4):
        lanes = slice(j * 128, (j + 1) * 128)
        both.append(
            dot(high[:, lanes], yz_high) + dot(low[:, lanes], yz_high) + dot(high[:, lanes], yz_low)
        )
    chunk = elements // 2
    rows = []
    for c in range(FIELDS):
        for part in range(2):
            begin = c * elements + part * chunk
            along_x = x_derivative(fields[begin : begin + chunk])
            here = [speed_rows[part * chunk : (part + 1) * chunk] for speed_rows in speeds]
            tiles = [
                here[0] * along_x[j]
                + here[1] * both[j][begin : begin + chunk, :128]
                + here[2] * both[j][begin : begin + chunk, 128:]
                for j in range(4)
            ]
            rows.append(jnp.concatenate(tiles, axis=1))
    names = column(neigh_ref)
    keys = local_key(elements)
    picked = jnp.concatenate([pick_rows(names[:, f : f + 1], keys) for f in range(6)], axis=0)
    lifted = lift_rows(picked, tables, lift, elements)
    return penalty * (lifted - face_counts() * fields) - jnp.concatenate(rows, axis=0)


def remote_terms(me, neigh_ref, shared_refs, lift):
    elements = neigh_ref.shape[1]
    names = column(neigh_ref)
    lane = lax.broadcasted_iota(jnp.int32, (1, elements), 1)
    keys = jnp.concatenate(
        [6 * elements + (me ^ m) * elements + lane for m in range(len(shared_refs))], axis=1
    )
    picked = jnp.concatenate([pick_rows(names[:, f : f + 1], keys) for f in range(6)], axis=0)
    table = jnp.concatenate([unpack_rows(ref, elements) for ref in shared_refs], axis=0)
    return lift_rows(picked, split(table), lift, elements)


def rows_of(ref):
    fields, elements, nodes = ref.shape
    return ref[...].reshape(fields * elements, nodes)


def load_kernel(*refs):
    count = 8
    sources, loaded = refs[:count], refs[count : 2 * count]
    extract_ref, lift_ref, high_ref, low_ref, shared_ref, sems = refs[2 * count :]
    copies = [
        pltpu.make_async_copy(source, target, sems.at[i])
        for i, (source, target) in enumerate(zip(sources, loaded))
    ]
    for copy in copies:
        copy.start()
    row, lane = iota((512, 128), 0), iota((512, 128), 1)
    for f in range(6):
        here = row == face_node(f, lane & 63)
        extract_ref[:, f * 128 : (f + 1) * 128] = jnp.where(here, 1.0, 0.0).astype(bf16)
    row, lane = iota((64, 512), 0), iota((64, 512), 1)
    for f in range(6):
        here = face_node(f, row) == lane
        lift_ref[f * 64 : (f + 1) * 64, :] = jnp.where(here, 1.0, 0.0).astype(bf16)
    for copy in copies:
        copy.wait()
    high, low = face_tables(rows_of(loaded[0]), extract_ref[...])
    high_ref[...] = high
    low_ref[...] = low
    share_rows(high, low, loaded[1], shared_ref)


def first_local_kernel(
    state_ref, velocity_ref, neigh_ref, high_ref, low_ref, yz, lift, out_ref
):
    fields = rows_of(state_ref)
    rate = local_rate(
        fields, velocity_ref, neigh_ref, (high_ref[...], low_ref[...]),
        *split(yz[...]), lift[...],
    )
    out_ref[...] = (fields + time_step * rate).reshape(out_ref.shape)


def first_finish_kernel(base_ref, neigh_ref, send_ref, lift, extract, *refs):
    shared_refs, (first_ref, high_ref, low_ref, shared_ref) = refs[:-4], refs[-4:]
    me = lax.axis_index("ax")
    terms = remote_terms(me, neigh_ref, shared_refs, lift[...])
    first = rows_of(base_ref) + (time_step * penalty) * terms
    first_ref[...] = first.reshape(first_ref.shape)
    high, low = face_tables(first, extract[...])
    high_ref[...] = high
    low_ref[...] = low
    share_rows(high, low, send_ref, shared_ref)


def second_local_kernel(
    state_ref, first_ref, velocity_ref, neigh_ref, high_ref, low_ref, yz, lift, out_ref
):
    fields = rows_of(first_ref)
    rate = local_rate(
        fields, velocity_ref, neigh_ref, (high_ref[...], low_ref[...]),
        *split(yz[...]), lift[...],
    )
    out_ref[...] = (0.5 * (rows_of(state_ref) + fields + time_step * rate)).reshape(out_ref.shape)


def maps_kernel(maps_ref, device_ref, block_ref, radial_ref, axial_ref, high_ref, low_ref):
    elements = maps_ref.shape[2]
    row = lax.broadcasted_iota(jnp.int32, (elements, 128), 0)
    lane = lax.broadcasted_iota(jnp.int32, (elements, 128), 1)
    twice = ((lane & 63) == row).astype(f32)
    radial_ref[...] = jnp.dot(maps_ref[1], twice, precision=highest, preferred_element_type=f32)
    axial = jnp.dot(maps_ref[2], twice, precision=highest, preferred_element_type=f32)
    row64 = lax.broadcasted_iota(jnp.int32, (64, 64), 0)
    lane64 = lax.broadcasted_iota(jnp.int32, (64, 64), 1)
    swap = ((row64 >> 3) + 8 * (row64 & 7) == lane64).astype(f32)
    axial_ref[...] = jnp.dot(swap, axial, precision=highest, preferred_element_type=f32)
    azimuthal = maps_ref[0].T
    row_t = lax.broadcasted_iota(jnp.int32, (64, 128), 0)
    lane_t = lax.broadcasted_iota(jnp.int32, (64, 128), 1)
    places = device_ref[...].astype(f32).T
    blocks = block_ref[...].astype(f32).T
    theta_lanes = high_ref.shape[1] // PB
    high_ref[...] = jnp.zeros_like(high_ref)
    low_ref[...] = jnp.zeros_like(low_ref)
    upper = (blocks >= PB).astype(f32)
    sector_key = places * TB + upper
    plane_key = blocks - PB * upper
    for y in range(8):
        tile_t = ((row_t >> 3) == (lane_t & 7)) & ((row_t & 7) == y)
        values = jnp.dot(
            azimuthal, tile_t.astype(f32), precision=highest, preferred_element_type=f32
        )
        value_high, value_low = split(values)
        rows = pl.ds((y // 2) * 128 + (y % 2) * 64, elements)
        for pb in range(PB):
            for tile in range(theta_lanes // 128):
                here = ((lane + tile * 128) >> 3).astype(f32)
                mine = (sector_key == here) & (plane_key == pb)
                lanes = pl.ds(pb * theta_lanes + tile * 128, 128)
                high_ref[rows, lanes] = jnp.where(mine, value_high.astype(f32), 0.0).astype(bf16)
                low_ref[rows, lanes] = jnp.where(mine, value_low.astype(f32), 0.0).astype(bf16)


def sample_kernel(base_ref, neigh_ref, lift, radial_ref, axial_ref, high_ref, low_ref, *refs):
    sectors = high_ref.shape[1] // (PB * TB * 8)
    shares = lax.axis_size("ax")
    shared_refs = refs[:shares]
    new_ref, out_refs = refs[shares], refs[shares + 1 : shares + 1 + sectors]
    turned_ref, mapped_ref, parts_ref = refs[shares + 1 + sectors :]
    elements = neigh_ref.shape[1]
    me = lax.axis_index("ax")
    terms = remote_terms(me, neigh_ref, shared_refs, lift[...])
    new_state = rows_of(base_ref) + (0.5 * time_step * penalty) * terms
    new_ref[...] = new_state.reshape(new_ref.shape)
    gap = jnp.zeros((64 - elements, 128), f32)
    for c in range(FIELDS):
        for j in range(4):
            part = new_state[c * elements : (c + 1) * elements, j * 128 : (j + 1) * 128]
            after = pltpu.roll(part, 120, 1)
            turned_ref[c, j] = jnp.concatenate([part, gap, after, gap], axis=0).T
    radial = radial_ref[...]
    axial = axial_ref[...]
    for c in range(FIELDS):
        for yy in range(4):
            inputs = []
            for x in range(8):
                start = (x % 2) * 64 + 16 * yy
                inputs.append(turned_ref[c, x // 2, start : start + 8, :])
            for r in range(8):
                mixed = radial[8 * r : 8 * r + 1, :] * inputs[0]
                for x in range(1, 8):
                    mixed = mixed + radial[8 * r + x : 8 * r + x + 1, :] * inputs[x]
                value = axial[0:8, :] * mixed[0:1, :]
                for z in range(1, 8):
                    value = value + axial[8 * z : 8 * z + 8, :] * mixed[z : z + 1, :]
                row = (c * 8 + r) * 8
                mapped_ref[row : row + 8, yy * 128 : (yy + 1) * 128] = value
    mapped_high, mapped_low = split(mapped_ref[...])
    theta_lanes = high_ref.shape[1] // PB
    groups = sectors // PB
    rows = 64 // groups
    for pb in range(PB):
        lanes = pl.ds(pb * theta_lanes, theta_lanes)
        weight_high = high_ref[:, lanes]
        total = (
            dot(mapped_high, weight_high)
            + dot(mapped_low, weight_high)
            + dot(mapped_high, low_ref[:, lanes])
        )
        for g in range(groups):
            for c in range(FIELDS):
                start = c * 64 + g * rows
                parts_ref[pb * groups + g, c * rows : (c + 1) * rows, :] = total[start : start + rows]
    owner = lax.axis_index("az")
    for m in range(sectors):
        out_refs[m][...] = parts_ref[owner ^ m]


def fourier_kernel(table_ref, *refs):
    out_ref = refs[-1]
    total = refs[0][...]
    for ref in refs[1:-1]:
        total = total + ref[...]
    high, low = split(total)
    weight, weight_low = split(table_ref[...])
    coeffs = dot(high, weight) + dot(low, weight) + dot(high, weight_low)
    width = total.shape[1]
    rows = total.shape[0] // FIELDS
    for k in range(2):
        for c in range(FIELDS):
            out_ref[k, c] = coeffs[c * rows : (c + 1) * rows, k * width : (k + 1) * width]


def store_kernel(new_ref, out_ref, sem):
    copy = pltpu.make_async_copy(new_ref, out_ref, sem)
    copy.start()
    copy.wait()


def shape(dims, dtype=f32):
    return jax.ShapeDtypeStruct(dims, dtype)


def call(kernel, outs, *args, scratch=(), flops=0, in_space=pltpu.VMEM, out_space=pltpu.VMEM):
    size = sum(math.prod(a.shape) * a.dtype.itemsize for a in list(args) + list(outs))
    return pl.pallas_call(
        kernel,
        out_shape=outs,
        in_specs=[pl.BlockSpec(memory_space=in_space)] * len(args),
        out_specs=tuple([pl.BlockSpec(memory_space=out_space)] * len(outs)),
        scratch_shapes=list(scratch),
        cost_estimate=pl.CostEstimate(flops=flops, bytes_accessed=size, transcendentals=0),
        compiler_params=pltpu.CompilerParams(vmem_limit_bytes=48 * 1024 * 1024),
    )(*args)


def exchange(value, axis):
    size = lax.axis_size(axis)
    return [value] + [
        lax.ppermute(value, axis, [(i, i ^ m) for i in range(size)]) for m in range(size - 1, 0, -1)
    ][::-1]


def per_device(state, velocity, interp_maps, neighbours, send_faces, owner_device, owner_block):
    elements = state.shape[0]
    sectors = lax.axis_size("az")
    inputs = (
        state.transpose(1, 0, 2),
        send_faces.reshape(1, elements),
        velocity.T,
        neighbours.T,
        interp_maps.transpose(1, 2, 3, 0).reshape(3, 64, elements),
        owner_device.reshape(1, elements),
        owner_block.reshape(1, elements),
    )
    yz_table = jnp.asarray(tile_tables(), f32)
    face_rows = shape((6 * elements, FIELDS * 128), bf16)
    travel = shape((FIELDS * elements // 2, 128))
    sources = inputs + (yz_table,)
    sources = tuple(pltpu.with_memory_space_constraint(a, pltpu.HBM) for a in sources)
    loaded = call(
        load_kernel,
        tuple(shape(a.shape, a.dtype) for a in sources)
        + (shape((512, 768), bf16), shape((384, 512), bf16), face_rows, face_rows, travel),
        *sources,
        scratch=(pltpu.SemaphoreType.DMA((len(sources),)),),
        flops=400_000_000,
        in_space=pltpu.HBM,
    )
    fields, sends, speed, names, maps, places, blocks, yz, extract, lift, high, low, shared = loaded
    cube = shape(fields.shape)
    others = exchange(shared, "ax")
    base = call(
        first_local_kernel, (cube,), fields, speed, names, high, low, yz, lift,
        flops=1_000_000_000,
    )[0]
    lanes = sectors * TB * 8
    weights = shape((512, PB * lanes), bf16)
    radial, axial, weight_high, weight_low = call(
        maps_kernel, (shape((64, 128)), shape((64, 128)), weights, weights), maps, places, blocks,
        flops=100_000_000,
    )
    first, high, low, shared = call(
        first_finish_kernel, (cube, face_rows, face_rows, travel),
        base, names, sends, lift, extract, *others,
        flops=600_000_000,
    )
    others = exchange(shared, "ax")
    base = call(
        second_local_kernel, (cube,), fields, first, speed, names, high, low, yz, lift,
        flops=1_000_000_000,
    )[0]
    rows = FIELDS * 64 * PB // sectors
    pieces = call(
        sample_kernel, (cube,) + (shape((rows, lanes)),) * sectors,
        base, names, lift, radial, axial, weight_high, weight_low, *others,
        scratch=(
            pltpu.VMEM((FIELDS, 4, 128, 128), f32),
            pltpu.VMEM((FIELDS * 64, 512), f32),
            pltpu.VMEM((sectors, rows, lanes), f32),
        ),
        flops=800_000_000,
    )
    new_state, pieces = pieces[0], pieces[1:]
    stored = call(
        store_kernel, (cube,), new_state, scratch=(pltpu.SemaphoreType.DMA,), out_space=pltpu.HBM
    )[0]
    arrived = [pieces[0]] + [
        lax.ppermute(pieces[m], "az", [(i, i ^ m) for i in range(sectors)])
        for m in range(sectors - 1, 0, -1)
    ]
    angle = 2.0 * np.pi / lanes * (np.outer(np.arange(lanes), np.arange(lanes)) % lanes)
    table = np.concatenate([np.cos(angle), -np.sin(angle)], axis=1) * lanes**-0.5
    spectrum = call(
        fourier_kernel, (shape((2, FIELDS, rows // FIELDS, lanes)),),
        jnp.asarray(table, f32), *arrived,
        flops=100_000_000,
    )[0]
    return stored.transpose(1, 0, 2), spectrum


def solution(mesh):
    return jax.shard_map(
        per_device,
        mesh=mesh,
        in_specs=(
            P(("az", "ax"), None, None),
            P(("az", "ax"), None),
            P(("az", "ax"), None, None, None),
            P(("az", "ax"), None),
            P(("az", "ax")),
            P(("az", "ax"), None),
            P(("az", "ax")),
        ),
        out_specs=(P(("az", "ax"), None, None), P(None, None, ("az", "ax"), None)),
        check_vma=False,
    )
```

```python
import functools
import math

import jax
import jax.numpy as jnp
import numpy as np
from jax import lax
from jax.experimental import pallas as pl
from jax.experimental.pallas import tpu as pltpu
from jax.sharding import PartitionSpec as P

TB = 2
PB = 4
FIELDS = 5
time_step = 0.02
penalty = 5.0
highest = lax.Precision.HIGHEST
f32 = jnp.float32
bf16 = jnp.bfloat16


def spectral_derivative():
    points = np.cos(np.pi * np.arange(8) / 7.0)
    ends = (np.arange(8) == 0) | (np.arange(8) == 7)
    scales = np.where(ends, 2.0, 1.0)
    signs = np.where(np.arange(8) % 2 == 0, 1.0, -1.0)
    differ = points[:, None] - points[None, :]
    offdiag = (
        scales[:, None]
        / scales[None, :]
        * signs[:, None]
        * signs[None, :]
        / np.where(np.eye(8) > 0, 1.0, differ)
    )
    inner = -points / (2.0 * np.where(ends, 1.0, 1.0 - points * points))
    corner = (2.0 * 49.0 + 1.0) / 6.0
    diagonal = np.where(np.arange(8) == 0, corner, np.where(np.arange(8) == 7, -corner, inner))
    return np.where(np.eye(8) > 0, diagonal[:, None], offdiag)


def tile_tables():
    deriv = spectral_derivative()
    along_y = np.kron(np.eye(2), np.kron(deriv, np.eye(8))).T
    along_z = np.kron(np.eye(16), deriv).T
    return np.concatenate([along_y, along_z], axis=1)


def face_node(face, position):
    first, second = position >> 3, position & 7
    if face < 2:
        return 448 * face + position
    if face < 4:
        return 56 * (face - 2) + 64 * first + second
    return 7 * (face - 4) + 64 * first + 8 * second


def iota(dims, axis):
    return lax.broadcasted_iota(jnp.int32, dims, axis)


def face_counts():
    node = iota((1, 512), 1)
    count = jnp.zeros((1, 512), f32)
    for coordinate in (node >> 6, (node >> 3) & 7, node & 7):
        count = count + jnp.where((coordinate == 0) | (coordinate == 7), 1.0, 0.0)
    return count


def split(value):
    high = value.astype(bf16)
    return high, (value - high.astype(f32)).astype(bf16)


def dot(a, b):
    return jnp.dot(a, b, preferred_element_type=f32)


def low_half(shape):
    return lax.broadcasted_iota(jnp.int32, shape, len(shape) - 1) < 64


def local_key(elements):
    lane = lax.broadcasted_iota(jnp.int32, (1, 6 * elements), 1)
    face = jnp.zeros_like(lane)
    for f in range(1, 6):
        face = face + (lane >= f * elements).astype(jnp.int32)
    return 6 * (lane - face * elements) + face


def column(row_ref):
    return row_ref[...].astype(f32).T


def pick_rows(names, keys):
    return jnp.where(names == keys.astype(f32), 1.0, 0.0).astype(bf16)


def face_table(fields, extract):
    elements = fields.shape[0] // FIELDS
    faces = dot(fields.astype(bf16), extract).astype(bf16)
    rows = [
        jnp.concatenate(
            [
                faces[c * elements : (c + 1) * elements, f * 128 : (f + 1) * 128]
                for c in range(FIELDS)
            ],
            axis=1,
        )
        for f in range(6)
    ]
    return jnp.concatenate(rows, axis=0)


def share_rows(table, picked, out_ref):
    elements = picked.shape[0]
    rows = dot(picked, table)
    field = [rows[:, c * 128 : (c + 1) * 128] for c in range(FIELDS)]
    half = low_half((elements, 128))
    out_ref[0:elements, :] = jnp.where(half, field[0], field[1])
    out_ref[elements : 2 * elements, :] = jnp.where(half, field[2], field[3])
    middle = elements // 2
    out_ref[2 * elements : 2 * elements + middle, :] = jnp.where(
        half[:middle], field[4][:middle], field[4][middle:]
    )


def unpack_rows(ref, elements):
    half = low_half((elements, 128))
    middle = elements // 2
    fields = []
    for first in range(2):
        both = ref[first * elements : (first + 1) * elements, :]
        turned = pltpu.roll(both, 64, 1)
        fields.append(jnp.where(half, both, turned))
        fields.append(jnp.where(half, turned, both))
    both = ref[2 * elements : 2 * elements + middle, :]
    turned = pltpu.roll(both, 64, 1)
    fields.append(
        jnp.concatenate(
            [jnp.where(half[:middle], both, turned), jnp.where(half[:middle], turned, both)],
            axis=0,
        )
    )
    return jnp.concatenate(fields, axis=1)


def share_names(names_ref, picked, out_ref):
    elements = picked.shape[0]
    lane = iota((1, 6 * elements), 1)
    face = jnp.zeros_like(lane)
    for f in range(1, 6):
        face = face + (lane >= f * elements).astype(jnp.int32)
    tile = (iota((elements, 6 * elements), 0) == lane - face * elements).astype(f32)
    names = jnp.dot(
        names_ref[...].astype(f32), tile, precision=highest, preferred_element_type=f32
    )
    rows = jnp.concatenate([names, face.astype(f32), jnp.zeros((1, 6 * elements), f32)], axis=0)
    out_ref[-8:, :] = jnp.zeros((8, 128), f32)
    out_ref[-8:, :elements] = lax.dot_general(
        rows, picked.astype(f32), (((1,), (1,)), ((), ())),
        precision=highest, preferred_element_type=f32,
    )


def facing_pairs(picked, table, elements):
    half = low_half((elements, 128))
    facing = dot(picked, table)
    field_rows = []
    for c in range(FIELDS):
        blocks = [
            facing[f * elements : (f + 1) * elements, c * 128 : (c + 1) * 128] for f in range(6)
        ]
        pairs = [jnp.where(half, blocks[f], blocks[f + 1]) for f in range(0, 6, 2)]
        field_rows.append(jnp.concatenate(pairs, axis=1))
    return jnp.concatenate(field_rows, axis=0).astype(bf16)


def x_derivative(fields):
    deriv = spectral_derivative()
    half = low_half((1, 128))
    tiles = [fields[:, 128 * i : 128 * i + 128] for i in range(4)]
    turned = [pltpu.roll(tile, 64, 1) for tile in tiles]
    out = []
    for j in range(4):
        total = None
        for i in range(4):
            same = jnp.where(half, float(deriv[2 * j, 2 * i]), float(deriv[2 * j + 1, 2 * i + 1]))
            cross = jnp.where(half, float(deriv[2 * j, 2 * i + 1]), float(deriv[2 * j + 1, 2 * i]))
            part = same * tiles[i] + cross * turned[i]
            total = part if total is None else total + part
        out.append(total)
    return out


def local_rate(fields, velocity_ref, neigh_ref, table, yz_high, yz_low, lift):
    elements = neigh_ref.shape[1]
    high, low = split(fields)
    speed = velocity_ref[...].T
    speeds = [jnp.broadcast_to(speed[:, d : d + 1], (elements, 128)) for d in range(3)]
    both = []
    for j in range(4):
        lanes = slice(j * 128, (j + 1) * 128)
        both.append(
            dot(high[:, lanes], yz_high) + dot(low[:, lanes], yz_high) + dot(high[:, lanes], yz_low)
        )
    chunk = elements // 2
    rows = []
    for c in range(FIELDS):
        for part in range(2):
            begin = c * elements + part * chunk
            along_x = x_derivative(fields[begin : begin + chunk])
            here = [speed_rows[part * chunk : (part + 1) * chunk] for speed_rows in speeds]
            tiles = [
                here[0] * along_x[j]
                + here[1] * both[j][begin : begin + chunk, :128]
                + here[2] * both[j][begin : begin + chunk, 128:]
                for j in range(4)
            ]
            rows.append(jnp.concatenate(tiles, axis=1))
    picked = pick_faces(column(neigh_ref), local_key(elements))
    lifted = dot(facing_pairs(picked, table, elements), lift)
    return penalty * (lifted - face_counts() * fields) - jnp.concatenate(rows, axis=0)


def pick_faces(names, keys):
    return jnp.concatenate([pick_rows(names[:, f : f + 1], keys) for f in range(6)], axis=0)


def remote_keys(elements):
    me = lax.axis_index("ax")
    lane = iota((1, elements), 1)
    return jnp.concatenate(
        [6 * elements + (me ^ m) * elements + lane for m in range(lax.axis_size("ax"))], axis=1
    )


def shared_table(refs, elements):
    return jnp.concatenate([unpack_rows(ref, elements) for ref in refs], axis=0)


def rows_of(ref):
    fields, elements, nodes = ref.shape
    return ref[...].reshape(fields * elements, nodes)


def load_kernel(*refs):
    count = 8
    sources, loaded = refs[:count], refs[count : 2 * count]
    extract_ref, lift_ref, cross_ref, table_ref, shared_ref, sems = refs[2 * count :]
    copies = [
        pltpu.make_async_copy(source, target, sems.at[i])
        for i, (source, target) in enumerate(zip(sources, loaded))
    ]
    for copy in copies:
        copy.start()
    row, lane = iota((512, 128), 0), iota((512, 128), 1)
    for f in range(6):
        here = row == face_node(f, lane & 63)
        extract_ref[:, f * 128 : (f + 1) * 128] = jnp.where(here, 1.0, 0.0).astype(bf16)
    row, lane = iota((64, 512), 0), iota((64, 512), 1)
    for f in range(6):
        here = face_node(f, row) == lane
        lift_ref[f * 64 : (f + 1) * 64, :] = jnp.where(here, 1.0, 0.0).astype(bf16)
    row, lane = iota((64, 128), 0), iota((64, 128), 1)
    for f in range(6):
        for g in range(6):
            here = face_node(f, row) == face_node(g, lane & 63)
            cross_ref[f * 64 : (f + 1) * 64, g * 128 : (g + 1) * 128] = jnp.where(
                here, 1.0, 0.0
            ).astype(bf16)
    for copy in copies:
        copy.wait()
    table = face_table(rows_of(loaded[0]), extract_ref[...])
    table_ref[...] = table
    picked = pick_rows(column(loaded[1]), local_key(loaded[1].shape[1]))
    share_rows(table, picked, shared_ref)
    share_names(loaded[3], picked, shared_ref)


def first_local_kernel(
    state_ref, velocity_ref, neigh_ref, send_ref, table_ref, yz, lift, extract, out_ref, shared_ref
):
    fields = rows_of(state_ref)
    rate = local_rate(
        fields, velocity_ref, neigh_ref, table_ref[...], *split(yz[...]), lift[...]
    )
    base = fields + time_step * rate
    out_ref[...] = base.reshape(out_ref.shape)
    picked = pick_rows(column(send_ref), local_key(send_ref.shape[1]))
    share_rows(face_table(base, extract[...]), picked, shared_ref)


def second_local_kernel(
    state_ref, base_ref, velocity_ref, neigh_ref, yz, lift, extract, cross, *refs
):
    shared_refs, (out_ref, added_ref) = refs[:-2], refs[-2:]
    elements = neigh_ref.shape[1]
    table = shared_table(shared_refs, elements).astype(bf16)
    keys = remote_keys(elements)
    picked = pick_faces(column(neigh_ref), keys)
    terms = dot(facing_pairs(picked, table, elements), lift[...])
    first = rows_of(base_ref) + (time_step * penalty) * terms
    rate = local_rate(
        first, velocity_ref, neigh_ref, face_table(first, extract[...]), *split(yz[...]), lift[...]
    )
    second = 0.5 * (rows_of(state_ref) + first + time_step * rate)
    out_ref[...] = second.reshape(out_ref.shape)
    names = jnp.concatenate([ref[-8:, :].T[:elements] for ref in shared_refs], axis=0)
    pairs = facing_pairs(pick_faces(names, keys), table, names.shape[0])
    for c in range(FIELDS):
        rows = slice(c * names.shape[0], (c + 1) * names.shape[0])
        faces = dot(pairs[rows], cross[...])
        added = faces[:, :128]
        for f in range(1, 6):
            added = jnp.where(names[:, 6:7] == f, faces[:, f * 128 : (f + 1) * 128], added)
        added_ref[:, c * 128 : (c + 1) * 128] = (time_step * penalty) * added


def maps_kernel(maps_ref, device_ref, block_ref, radial_ref, axial_ref, high_ref, low_ref):
    elements = maps_ref.shape[2]
    row = lax.broadcasted_iota(jnp.int32, (elements, 128), 0)
    lane = lax.broadcasted_iota(jnp.int32, (elements, 128), 1)
    twice = ((lane & 63) == row).astype(f32)
    radial_ref[...] = jnp.dot(maps_ref[1], twice, precision=highest, preferred_element_type=f32)
    axial = jnp.dot(maps_ref[2], twice, precision=highest, preferred_element_type=f32)
    row64 = lax.broadcasted_iota(jnp.int32, (64, 64), 0)
    lane64 = lax.broadcasted_iota(jnp.int32, (64, 64), 1)
    swap = ((row64 >> 3) + 8 * (row64 & 7) == lane64).astype(f32)
    axial_ref[...] = jnp.dot(swap, axial, precision=highest, preferred_element_type=f32)
    azimuthal = maps_ref[0].T
    row_t = lax.broadcasted_iota(jnp.int32, (64, 128), 0)
    lane_t = lax.broadcasted_iota(jnp.int32, (64, 128), 1)
    places = device_ref[...].astype(f32).T
    blocks = block_ref[...].astype(f32).T
    theta_lanes = high_ref.shape[1] // PB
    high_ref[...] = jnp.zeros_like(high_ref)
    low_ref[...] = jnp.zeros_like(low_ref)
    upper = (blocks >= PB).astype(f32)
    sector_key = places * TB + upper
    plane_key = blocks - PB * upper
    for y in range(8):
        tile_t = ((row_t >> 3) == (lane_t & 7)) & ((row_t & 7) == y)
        values = jnp.dot(
            azimuthal, tile_t.astype(f32), precision=highest, preferred_element_type=f32
        )
        value_high, value_low = split(values)
        rows = pl.ds((y // 2) * 128 + (y % 2) * 64, elements)
        for pb in range(PB):
            for tile in range(theta_lanes // 128):
                here = ((lane + tile * 128) >> 3).astype(f32)
                mine = (sector_key == here) & (plane_key == pb)
                lanes = pl.ds(pb * theta_lanes + tile * 128, 128)
                high_ref[rows, lanes] = jnp.where(mine, value_high.astype(f32), 0.0).astype(bf16)
                low_ref[rows, lanes] = jnp.where(mine, value_low.astype(f32), 0.0).astype(bf16)


def exchange_plan(size):
    straight = [m for m in range(size // 2, 3 * size // 4) if m & 1]
    relayed = [m for m in range(size - 1, 0, -2) if m not in straight]
    return relayed, [m for m in range(size) if m not in relayed]


def sample_kernel(
    base_ref, neigh_ref, added_ref, lift, radial_ref, axial_ref, high_ref, low_ref, *refs
):
    sectors = high_ref.shape[1] // (PB * TB * 8)
    shares = lax.axis_size("ax")
    shared_refs = refs[:shares]
    new_ref, out_refs = refs[shares], refs[shares + 1 : -3]
    turned_ref, mapped_ref, parts_ref = refs[-3:]
    elements = neigh_ref.shape[1]
    table = (shared_table(shared_refs, elements) + added_ref[...]).astype(bf16)
    picked = pick_faces(column(neigh_ref), remote_keys(elements))
    terms = dot(facing_pairs(picked, table, elements), lift[...])
    new_state = rows_of(base_ref) + (0.5 * time_step * penalty) * terms
    new_ref[...] = new_state.reshape(new_ref.shape)
    gap = jnp.zeros((64 - elements, 128), f32)
    for c in range(FIELDS):
        for j in range(4):
            part = new_state[c * elements : (c + 1) * elements, j * 128 : (j + 1) * 128]
            after = pltpu.roll(part, 120, 1)
            turned_ref[c, j] = jnp.concatenate([part, gap, after, gap], axis=0).T
    radial = radial_ref[...]
    axial = axial_ref[...]
    for c in range(FIELDS):
        for yy in range(4):
            inputs = []
            for x in range(8):
                start = (x % 2) * 64 + 16 * yy
                inputs.append(turned_ref[c, x // 2, start : start + 8, :])
            for r in range(8):
                mixed = radial[8 * r : 8 * r + 1, :] * inputs[0]
                for x in range(1, 8):
                    mixed = mixed + radial[8 * r + x : 8 * r + x + 1, :] * inputs[x]
                value = axial[0:8, :] * mixed[0:1, :]
                for z in range(1, 8):
                    value = value + axial[8 * z : 8 * z + 8, :] * mixed[z : z + 1, :]
                row = (c * 8 + r) * 8
                mapped_ref[row : row + 8, yy * 128 : (yy + 1) * 128] = value
    mapped_high, mapped_low = split(mapped_ref[...])
    theta_lanes = high_ref.shape[1] // PB
    groups = sectors // PB
    rows = 64 // groups
    for pb in range(PB):
        lanes = pl.ds(pb * theta_lanes, theta_lanes)
        weight_high = high_ref[:, lanes]
        total = (
            dot(mapped_high, weight_high)
            + dot(mapped_low, weight_high)
            + dot(mapped_high, low_ref[:, lanes])
        )
        for g in range(groups):
            for c in range(FIELDS):
                start = c * 64 + g * rows
                parts_ref[pb * groups + g, c * rows : (c + 1) * rows, :] = total[start : start + rows]
    owner = lax.axis_index("az")
    relayed, kept = exchange_plan(sectors)
    for i, m in enumerate(relayed):
        out_refs[0][i] = parts_ref[owner ^ m]
    for i, m in enumerate(kept):
        out_refs[1 + i][...] = parts_ref[owner ^ m]


def fourier_kernel(table_ref, bundle_ref, *refs):
    out_ref = refs[-1]
    total = bundle_ref[bundle_ref.shape[0] - 1]
    for ref in refs[:-1]:
        total = total + ref[...]
    high, low = split(total)
    weight, weight_low = split(table_ref[...])
    coeffs = dot(high, weight) + dot(low, weight) + dot(high, weight_low)
    width = total.shape[1]
    rows = total.shape[0] // FIELDS
    for k in range(2):
        for c in range(FIELDS):
            out_ref[k, c] = coeffs[c * rows : (c + 1) * rows, k * width : (k + 1) * width]


def join_kernel(got_ref, *refs):
    count = len(refs) // 2
    for i in range(count):
        refs[count + i][...] = refs[i][...] + got_ref[i]


def store_kernel(new_ref, out_ref, sem):
    copy = pltpu.make_async_copy(new_ref, out_ref, sem)
    copy.start()
    copy.wait()


def shape(dims, dtype=f32):
    return jax.ShapeDtypeStruct(dims, dtype)


def call(kernel, outs, *args, scratch=(), flops=0, in_space=pltpu.VMEM, out_space=pltpu.VMEM, aliases={}):
    size = sum(math.prod(a.shape) * a.dtype.itemsize for a in list(args) + list(outs))
    return pl.pallas_call(
        kernel,
        out_shape=outs,
        in_specs=[pl.BlockSpec(memory_space=in_space)] * len(args),
        out_specs=tuple([pl.BlockSpec(memory_space=out_space)] * len(outs)),
        scratch_shapes=list(scratch),
        input_output_aliases=aliases,
        cost_estimate=pl.CostEstimate(flops=flops, bytes_accessed=size, transcendentals=0),
        compiler_params=pltpu.CompilerParams(vmem_limit_bytes=48 * 1024 * 1024),
    )(*args)


def exchange(value, axis):
    size = lax.axis_size(axis)
    return [value] + [
        lax.ppermute(value, axis, [(i, i ^ m) for i in range(size)]) for m in range(size - 1, 0, -1)
    ][::-1]


def per_device(state, velocity, interp_maps, neighbours, send_faces, owner_device, owner_block):
    elements = state.shape[0]
    sectors = lax.axis_size("az")
    inputs = (
        state.transpose(1, 0, 2),
        send_faces.reshape(1, elements),
        velocity.T,
        neighbours.T,
        interp_maps.transpose(1, 2, 3, 0).reshape(3, 64, elements),
        owner_device.reshape(1, elements),
        owner_block.reshape(1, elements),
    )
    yz_table = jnp.asarray(tile_tables(), f32)
    face_rows = shape((6 * elements, FIELDS * 128), bf16)
    travel = FIELDS * elements // 2
    sources = inputs + (yz_table,)
    sources = tuple(pltpu.with_memory_space_constraint(a, pltpu.HBM) for a in sources)
    loaded = call(
        load_kernel,
        tuple(shape(a.shape, a.dtype) for a in sources)
        + (shape((512, 768), bf16), shape((384, 512), bf16), shape((384, 768), bf16))
        + (face_rows, shape((travel + 8, 128))),
        *sources,
        scratch=(pltpu.SemaphoreType.DMA((len(sources),)),),
        flops=400_000_000,
        in_space=pltpu.HBM,
    )
    fields, sends, speed, names, maps, places, blocks, yz, extract, lift, cross, table, shared = loaded
    cube = shape(fields.shape)
    others = exchange(shared, "ax")
    base, shared = call(
        first_local_kernel, (cube, shape((travel, 128))),
        fields, speed, names, sends, table, yz, lift, extract,
        flops=1_000_000_000,
    )
    firsts = exchange(shared, "ax")
    lanes = sectors * TB * 8
    weights = shape((512, PB * lanes), bf16)
    radial, axial, weight_high, weight_low = call(
        maps_kernel, (shape((64, 128)), shape((64, 128)), weights, weights), maps, places, blocks,
        flops=100_000_000,
    )
    base, added = call(
        second_local_kernel, (cube, shape((lax.axis_size("ax") * elements, FIELDS * 128))),
        fields, base, speed, names, yz, lift, extract, cross, *others,
        flops=1_500_000_000,
    )
    rows = FIELDS * 64 * PB // sectors
    piece = shape((rows, lanes))
    relayed, kept = exchange_plan(sectors)
    sampled = call(
        sample_kernel, (cube, shape((len(relayed), rows, lanes))) + (piece,) * len(kept),
        base, names, added, lift, radial, axial, weight_high, weight_low, *firsts,
        scratch=(
            pltpu.VMEM((FIELDS, 4, 128, 128), f32),
            pltpu.VMEM((FIELDS * 64, 512), f32),
            pltpu.VMEM((sectors, rows, lanes), f32),
        ),
        flops=800_000_000,
    )
    new_state, bundle, pieces = sampled[0], sampled[1], dict(zip(kept, sampled[2:]))
    stored = call(
        store_kernel, (cube,), new_state, scratch=(pltpu.SemaphoreType.DMA,), out_space=pltpu.HBM
    )[0]

    def swap(value, mask):
        return lax.ppermute(value, "az", [(i, i ^ mask) for i in range(sectors)])

    bundle = swap(bundle, 1)
    joined = [m - 1 for m in relayed if m > 1]
    arrived = [swap(pieces[m], m) for m in kept if m and m not in joined]
    sums = call(
        join_kernel, (piece,) * len(joined), bundle, *[pieces[m] for m in joined]
    )
    arrived += [swap(value, m) for m, value in zip(joined, sums)]
    arrived.append(pieces[0])
    angle = 2.0 * np.pi / lanes * (np.outer(np.arange(lanes), np.arange(lanes)) % lanes)
    table = np.concatenate([np.cos(angle), -np.sin(angle)], axis=1) * lanes**-0.5
    spectrum = call(
        fourier_kernel, (shape((2, FIELDS, rows // FIELDS, lanes)),),
        jnp.asarray(table, f32), bundle, *arrived,
        flops=100_000_000,
    )[0]
    return stored.transpose(1, 0, 2), spectrum


def solution(mesh):
    return jax.shard_map(
        per_device,
        mesh=mesh,
        in_specs=(
            P(("az", "ax"), None, None),
            P(("az", "ax"), None),
            P(("az", "ax"), None, None, None),
            P(("az", "ax"), None),
            P(("az", "ax")),
            P(("az", "ax"), None),
            P(("az", "ax")),
        ),
        out_specs=(P(("az", "ax"), None, None), P(None, None, ("az", "ax"), None)),
        check_vma=False,
    )
```

```python
import functools
import math

import jax
import jax.numpy as jnp
import numpy as np
from jax import lax
from jax.experimental import pallas as pl
from jax.experimental.pallas import tpu as pltpu
from jax.sharding import PartitionSpec as P

TB = 2
PB = 4
FIELDS = 5
time_step = 0.02
penalty = 5.0
highest = lax.Precision.HIGHEST
f32 = jnp.float32
bf16 = jnp.bfloat16


def spectral_derivative():
    points = np.cos(np.pi * np.arange(8) / 7.0)
    ends = (np.arange(8) == 0) | (np.arange(8) == 7)
    scales = np.where(ends, 2.0, 1.0)
    signs = np.where(np.arange(8) % 2 == 0, 1.0, -1.0)
    differ = points[:, None] - points[None, :]
    offdiag = (
        scales[:, None]
        / scales[None, :]
        * signs[:, None]
        * signs[None, :]
        / np.where(np.eye(8) > 0, 1.0, differ)
    )
    inner = -points / (2.0 * np.where(ends, 1.0, 1.0 - points * points))
    corner = (2.0 * 49.0 + 1.0) / 6.0
    diagonal = np.where(np.arange(8) == 0, corner, np.where(np.arange(8) == 7, -corner, inner))
    return np.where(np.eye(8) > 0, diagonal[:, None], offdiag)


def tile_tables():
    deriv = spectral_derivative()
    along_y = np.kron(np.eye(2), np.kron(deriv, np.eye(8))).T
    along_z = np.kron(np.eye(16), deriv).T
    return np.concatenate([along_y, along_z], axis=1)


def face_node(face, position):
    first, second = position >> 3, position & 7
    if face < 2:
        return 448 * face + position
    if face < 4:
        return 56 * (face - 2) + 64 * first + second
    return 7 * (face - 4) + 64 * first + 8 * second


def iota(dims, axis):
    return lax.broadcasted_iota(jnp.int32, dims, axis)


def face_counts():
    node = iota((1, 512), 1)
    count = jnp.zeros((1, 512), f32)
    for coordinate in (node >> 6, (node >> 3) & 7, node & 7):
        count = count + jnp.where((coordinate == 0) | (coordinate == 7), 1.0, 0.0)
    return count


def split(value):
    high = value.astype(bf16)
    return high, (value - high.astype(f32)).astype(bf16)


def dot(a, b):
    return jnp.dot(a, b, preferred_element_type=f32)


def low_half(shape):
    return lax.broadcasted_iota(jnp.int32, shape, len(shape) - 1) < 64


def local_key(elements):
    lane = lax.broadcasted_iota(jnp.int32, (1, 6 * elements), 1)
    face = jnp.zeros_like(lane)
    for f in range(1, 6):
        face = face + (lane >= f * elements).astype(jnp.int32)
    return 6 * (lane - face * elements) + face


def column(row_ref):
    return row_ref[...].astype(f32).T


def pick_rows(names, keys):
    return jnp.where(names == keys.astype(f32), 1.0, 0.0).astype(bf16)


def face_table(fields, extract):
    elements = fields.shape[0] // FIELDS
    faces = dot(fields.astype(bf16), extract).astype(bf16)
    rows = [
        jnp.concatenate(
            [
                faces[c * elements : (c + 1) * elements, f * 128 : (f + 1) * 128]
                for c in range(FIELDS)
            ],
            axis=1,
        )
        for f in range(6)
    ]
    return jnp.concatenate(rows, axis=0)


def share_rows(table, picked, out_ref):
    elements = picked.shape[0]
    rows = dot(picked, table)
    field = [rows[:, c * 128 : (c + 1) * 128] for c in range(FIELDS)]
    half = low_half((elements, 128))
    out_ref[0:elements, :] = jnp.where(half, field[0], field[1])
    out_ref[elements : 2 * elements, :] = jnp.where(half, field[2], field[3])
    middle = elements // 2
    out_ref[2 * elements : 2 * elements + middle, :] = jnp.where(
        half[:middle], field[4][:middle], field[4][middle:]
    )


def unpack_rows(ref, elements):
    half = low_half((elements, 128))
    middle = elements // 2
    fields = []
    for first in range(2):
        both = ref[first * elements : (first + 1) * elements, :]
        turned = pltpu.roll(both, 64, 1)
        fields.append(jnp.where(half, both, turned))
        fields.append(jnp.where(half, turned, both))
    both = ref[2 * elements : 2 * elements + middle, :]
    turned = pltpu.roll(both, 64, 1)
    fields.append(
        jnp.concatenate(
            [jnp.where(half[:middle], both, turned), jnp.where(half[:middle], turned, both)],
            axis=0,
        )
    )
    return jnp.concatenate(fields, axis=1)


def share_names(names_ref, picked, out_ref):
    elements = picked.shape[0]
    lane = iota((1, 6 * elements), 1)
    face = jnp.zeros_like(lane)
    for f in range(1, 6):
        face = face + (lane >= f * elements).astype(jnp.int32)
    tile = (iota((elements, 6 * elements), 0) == lane - face * elements).astype(f32)
    names = jnp.dot(
        names_ref[...].astype(f32), tile, precision=highest, preferred_element_type=f32
    )
    rows = jnp.concatenate([names, face.astype(f32), jnp.zeros((1, 6 * elements), f32)], axis=0)
    out_ref[-8:, :] = jnp.zeros((8, 128), f32)
    out_ref[-8:, :elements] = lax.dot_general(
        rows, picked.astype(f32), (((1,), (1,)), ((), ())),
        precision=highest, preferred_element_type=f32,
    )


def facing_pairs(picked, table, elements):
    half = low_half((elements, 128))
    facing = dot(picked, table)
    field_rows = []
    for c in range(FIELDS):
        blocks = [
            facing[f * elements : (f + 1) * elements, c * 128 : (c + 1) * 128] for f in range(6)
        ]
        pairs = [jnp.where(half, blocks[f], blocks[f + 1]) for f in range(0, 6, 2)]
        field_rows.append(jnp.concatenate(pairs, axis=1))
    return jnp.concatenate(field_rows, axis=0).astype(bf16)


def x_derivative(fields):
    deriv = spectral_derivative()
    half = low_half((1, 128))
    tiles = [fields[:, 128 * i : 128 * i + 128] for i in range(4)]
    turned = [pltpu.roll(tile, 64, 1) for tile in tiles]
    out = []
    for j in range(4):
        total = None
        for i in range(4):
            same = jnp.where(half, float(deriv[2 * j, 2 * i]), float(deriv[2 * j + 1, 2 * i + 1]))
            cross = jnp.where(half, float(deriv[2 * j, 2 * i + 1]), float(deriv[2 * j + 1, 2 * i]))
            part = same * tiles[i] + cross * turned[i]
            total = part if total is None else total + part
        out.append(total)
    return out


def local_rate(fields, velocity_ref, neigh_ref, table, yz_high, yz_low, lift):
    elements = neigh_ref.shape[1]
    high, low = split(fields)
    speed = velocity_ref[...].T
    speeds = [jnp.broadcast_to(speed[:, d : d + 1], (elements, 128)) for d in range(3)]
    both = []
    for j in range(4):
        lanes = slice(j * 128, (j + 1) * 128)
        both.append(
            dot(high[:, lanes], yz_high) + dot(low[:, lanes], yz_high) + dot(high[:, lanes], yz_low)
        )
    chunk = elements // 2
    rows = []
    for c in range(FIELDS):
        for part in range(2):
            begin = c * elements + part * chunk
            along_x = x_derivative(fields[begin : begin + chunk])
            here = [speed_rows[part * chunk : (part + 1) * chunk] for speed_rows in speeds]
            tiles = [
                here[0] * along_x[j]
                + here[1] * both[j][begin : begin + chunk, :128]
                + here[2] * both[j][begin : begin + chunk, 128:]
                for j in range(4)
            ]
            rows.append(jnp.concatenate(tiles, axis=1))
    picked = pick_faces(column(neigh_ref), local_key(elements))
    lifted = dot(facing_pairs(picked, table, elements), lift)
    return penalty * (lifted - face_counts() * fields) - jnp.concatenate(rows, axis=0)


def pick_faces(names, keys):
    return jnp.concatenate([pick_rows(names[:, f : f + 1], keys) for f in range(6)], axis=0)


def remote_keys(elements):
    me = lax.axis_index("ax")
    lane = iota((1, elements), 1)
    return jnp.concatenate(
        [6 * elements + (me ^ m) * elements + lane for m in range(lax.axis_size("ax"))], axis=1
    )


def shared_table(refs, elements):
    return jnp.concatenate([unpack_rows(ref, elements) for ref in refs], axis=0)


def rows_of(ref):
    fields, elements, nodes = ref.shape
    return ref[...].reshape(fields * elements, nodes)


def load_kernel(*refs):
    count = 8
    sources, loaded = refs[:count], refs[count : 2 * count]
    extract_ref, lift_ref, cross_ref, table_ref, shared_ref, sems = refs[2 * count :]
    pairs = list(zip(sources, loaded))
    fields = [(pairs[0][0].at[c], pairs[0][1].at[c]) for c in range(FIELDS)]
    copies = [
        pltpu.make_async_copy(source, target, sems.at[i])
        for i, (source, target) in enumerate(pairs[1:4] + fields + pairs[4:])
    ]
    for copy in copies:
        copy.start()
    row, lane = iota((512, 128), 0), iota((512, 128), 1)
    for f in range(6):
        here = row == face_node(f, lane & 63)
        extract_ref[:, f * 128 : (f + 1) * 128] = jnp.where(here, 1.0, 0.0).astype(bf16)
    for copy in copies[:3]:
        copy.wait()
    picked = pick_rows(column(loaded[1]), local_key(loaded[1].shape[1]))
    share_names(loaded[3], picked, shared_ref)
    row, lane = iota((64, 512), 0), iota((64, 512), 1)
    for f in range(6):
        here = face_node(f, row) == lane
        lift_ref[f * 64 : (f + 1) * 64, :] = jnp.where(here, 1.0, 0.0).astype(bf16)
    row, lane = iota((64, 128), 0), iota((64, 128), 1)
    for f in range(6):
        for g in range(0, 6, 2):
            node = jnp.where(lane < 64, face_node(g, lane & 63), face_node(g + 1, lane & 63))
            cross_ref[f * 64 : (f + 1) * 64, g * 64 : (g + 2) * 64] = jnp.where(
                face_node(f, row) == node, 1.0, 0.0
            ).astype(bf16)
    for copy in copies[3:]:
        copy.wait()
    table = face_table(rows_of(loaded[0]), extract_ref[...])
    table_ref[...] = table
    share_rows(table, picked, shared_ref)


def first_local_kernel(
    state_ref, velocity_ref, neigh_ref, send_ref, table_ref, yz, lift, extract, out_ref, shared_ref
):
    fields = rows_of(state_ref)
    rate = local_rate(
        fields, velocity_ref, neigh_ref, table_ref[...], *split(yz[...]), lift[...]
    )
    base = fields + time_step * rate
    out_ref[...] = base.reshape(out_ref.shape)
    picked = pick_rows(column(send_ref), local_key(send_ref.shape[1]))
    share_rows(face_table(base, extract[...]), picked, shared_ref)


def fill_maps(
    maps_ref, device_ref, block_ref, radial_ref, axial_ref, high_ref, low_ref
):
    elements = maps_ref.shape[2]
    row, lane = iota((elements, 128), 0), iota((elements, 128), 1)
    twice = ((lane & 63) == row).astype(f32).astype(bf16)
    radial_ref[...] = exact_dot(maps_ref[1], twice)
    swap = ((iota((64, 64), 0) >> 3) + 8 * (iota((64, 64), 0) & 7) == iota((64, 64), 1)).astype(f32)
    axial = [dot(swap.astype(bf16), part).astype(bf16) for part in split(maps_ref[2])]
    axial_ref[...] = dot(axial[0], twice) + dot(axial[1], twice)
    tile_row, tile_lane = iota((64, 1024), 0), iota((64, 1024), 1)
    tile = ((tile_row >> 3) == (tile_lane & 7)) & ((tile_row & 7) == (tile_lane >> 7))
    tile = jnp.where(tile, 1.0, 0.0).astype(bf16)
    values = [dot(part, tile) for part in split(maps_ref[0].T)]
    places = device_ref[...].astype(f32).T
    blocks = block_ref[...].astype(f32).T
    theta_lanes = high_ref.shape[1] // PB
    upper = (blocks >= PB).astype(f32)
    sector_key = places * TB + upper
    plane_key = blocks - PB * upper
    gap = jnp.zeros((64 - elements, high_ref.shape[1]), bf16)
    for y in range(8):
        start = y * 64
        high_ref[start + elements : start + 64, :] = gap
        low_ref[start + elements : start + 64, :] = gap
    for pb in range(PB):
        for tile_at in range(theta_lanes // 128):
            here = ((lane + tile_at * 128) >> 3).astype(f32)
            mine = (sector_key == here) & (plane_key == pb)
            begin = pb * theta_lanes + tile_at * 128
            for ref, value in zip((high_ref, low_ref), values):
                for y in range(8):
                    ref[y * 64 : y * 64 + elements, begin : begin + 128] = jnp.where(
                        mine, value[:, y * 128 : (y + 1) * 128], 0.0
                    ).astype(bf16)


def exact_dot(value, choice):
    high, low = split(value)
    return dot(high, choice) + dot(low, choice)


def second_local_kernel(
    state_ref, base_ref, velocity_ref, neigh_ref, send_ref, yz, lift, extract, cross, *refs
):
    shared_refs, map_refs, (out_ref, added_ref) = refs[:-9], refs[-9:-6] + refs[-4:], refs[-6:-4]
    fill_maps(*map_refs)
    elements = neigh_ref.shape[1]
    table = shared_table(shared_refs, elements).astype(bf16)
    keys = remote_keys(elements)
    picked = pick_faces(column(neigh_ref), keys)
    terms = dot(facing_pairs(picked, table, elements), lift[...])
    first = rows_of(base_ref) + (time_step * penalty) * terms
    first_table = face_table(first, extract[...])
    rate = local_rate(
        first, velocity_ref, neigh_ref, first_table, *split(yz[...]), lift[...]
    )
    second = 0.5 * (rows_of(state_ref) + first + time_step * rate)
    out_ref[...] = second.reshape(out_ref.shape)
    own = pick_rows(column(send_ref), local_key(elements))
    added_ref[:elements, :] = dot(own, first_table)
    names = jnp.concatenate([ref[-8:, :].T[:elements] for ref in shared_refs[1:]], axis=0)
    count = names.shape[0]
    pairs = facing_pairs(pick_faces(names, keys), table, count)
    face = names[:, 6:7]
    half = low_half((count, 128))
    same = half != ((face == 1) | (face == 3) | (face == 5))
    for c in range(FIELDS):
        faces = dot(pairs[c * count : (c + 1) * count], cross[...])
        added = jnp.where(face >= 2, faces[:, 128:256], faces[:, :128])
        added = jnp.where(face >= 4, faces[:, 256:], added)
        added = jnp.where(same, added, pltpu.roll(added, 64, 1))
        added_ref[elements:, c * 128 : (c + 1) * 128] = (time_step * penalty) * added


def exchange_plan(size):
    straight = [m for m in range(size // 2, 3 * size // 4) if m & 1]
    relayed = [m for m in range(size - 1, 1, -2) if m not in straight]
    return relayed, [m for m in range(size) if m not in relayed]


def sample_kernel(
    base_ref, neigh_ref, added_ref, lift, radial_ref, axial_ref, high_ref, low_ref, *refs
):
    sectors = high_ref.shape[1] // (PB * TB * 8)
    shares = lax.axis_size("ax") - 1
    shared_refs = refs[:shares]
    new_ref, out_refs = refs[shares], refs[shares + 1 : -3]
    turned_ref, mapped_ref, parts_ref = refs[-3:]
    elements = neigh_ref.shape[1]
    added = added_ref[elements:, :] + shared_table(shared_refs, elements)
    table = jnp.concatenate([added_ref[:elements, :], added], axis=0).astype(bf16)
    picked = pick_faces(column(neigh_ref), remote_keys(elements))
    terms = dot(facing_pairs(picked, table, elements), lift[...])
    new_state = rows_of(base_ref) + (0.5 * time_step * penalty) * terms
    new_ref[...] = new_state.reshape(new_ref.shape)
    gap = jnp.zeros((64 - elements, 128), f32)
    for c in range(FIELDS):
        for j in range(4):
            part = new_state[c * elements : (c + 1) * elements, j * 128 : (j + 1) * 128]
            after = pltpu.roll(part, 120, 1)
            turned_ref[c, j] = jnp.concatenate([part, gap, after, gap], axis=0).T
    radial = radial_ref[...]
    axial = axial_ref[...]
    for c in range(FIELDS):
        for yy in range(4):
            inputs = []
            for x in range(8):
                start = (x % 2) * 64 + 16 * yy
                inputs.append(turned_ref[c, x // 2, start : start + 8, :])
            for r in range(8):
                mixed = radial[8 * r : 8 * r + 1, :] * inputs[0]
                for x in range(1, 8):
                    mixed = mixed + radial[8 * r + x : 8 * r + x + 1, :] * inputs[x]
                value = axial[0:8, :] * mixed[0:1, :]
                for z in range(1, 8):
                    value = value + axial[8 * z : 8 * z + 8, :] * mixed[z : z + 1, :]
                row = (c * 8 + r) * 8
                mapped_ref[row : row + 8, yy * 128 : (yy + 1) * 128] = value
    mapped_high, mapped_low = split(mapped_ref[...])
    theta_lanes = high_ref.shape[1] // PB
    groups = sectors // PB
    rows = 64 // groups
    for pb in range(PB):
        lanes = pl.ds(pb * theta_lanes, theta_lanes)
        weight_high = high_ref[:, lanes]
        total = (
            dot(mapped_high, weight_high)
            + dot(mapped_low, weight_high)
            + dot(mapped_high, low_ref[:, lanes])
        )
        for g in range(groups):
            for c in range(FIELDS):
                start = c * 64 + g * rows
                parts_ref[pb * groups + g, c * rows : (c + 1) * rows, :] = total[start : start + rows]
    owner = lax.axis_index("az")
    relayed, kept = exchange_plan(sectors)
    for i, m in enumerate(relayed):
        out_refs[0][i] = parts_ref[owner ^ m]
    for i, m in enumerate(kept):
        out_refs[1 + i][...] = parts_ref[owner ^ m]


def fourier_kernel(table_ref, *refs):
    out_ref = refs[-1]
    total = refs[0][...]
    for ref in refs[1:-1]:
        total = total + ref[...]
    high, low = split(total)
    weight, weight_low = split(table_ref[...])
    coeffs = dot(high, weight) + dot(low, weight) + dot(high, weight_low)
    width = total.shape[1]
    rows = total.shape[0] // FIELDS
    for k in range(2):
        for c in range(FIELDS):
            out_ref[k, c] = coeffs[c * rows : (c + 1) * rows, k * width : (k + 1) * width]


def join_kernel(got_ref, *refs):
    count = len(refs) // 2
    for i in range(count - 1):
        refs[count + i][...] = refs[i][...] + got_ref[i]
    refs[-1][...] = refs[count - 1][...]


def store_kernel(new_ref, out_ref, sem):
    copy = pltpu.make_async_copy(new_ref, out_ref, sem)
    copy.start()
    copy.wait()


def shape(dims, dtype=f32):
    return jax.ShapeDtypeStruct(dims, dtype)


def call(kernel, outs, *args, scratch=(), flops=0, in_space=pltpu.VMEM, out_space=pltpu.VMEM, aliases={}):
    size = sum(math.prod(a.shape) * a.dtype.itemsize for a in list(args) + list(outs))
    return pl.pallas_call(
        kernel,
        out_shape=outs,
        in_specs=[pl.BlockSpec(memory_space=in_space)] * len(args),
        out_specs=tuple([pl.BlockSpec(memory_space=out_space)] * len(outs)),
        scratch_shapes=list(scratch),
        input_output_aliases=aliases,
        cost_estimate=pl.CostEstimate(flops=flops, bytes_accessed=size, transcendentals=0),
        compiler_params=pltpu.CompilerParams(vmem_limit_bytes=48 * 1024 * 1024),
    )(*args)


def exchange(value, axis):
    size = lax.axis_size(axis)
    return [value] + [
        lax.ppermute(value, axis, [(i, i ^ m) for i in range(size)]) for m in range(size - 1, 0, -1)
    ][::-1]


def per_device(state, velocity, interp_maps, neighbours, send_faces, owner_device, owner_block):
    elements = state.shape[0]
    sectors = lax.axis_size("az")
    inputs = (
        state.transpose(1, 0, 2),
        send_faces.reshape(1, elements),
        velocity.T,
        neighbours.T,
        interp_maps.transpose(1, 2, 3, 0).reshape(3, 64, elements),
        owner_device.reshape(1, elements),
        owner_block.reshape(1, elements),
    )
    yz_table = jnp.asarray(tile_tables(), f32)
    face_rows = shape((6 * elements, FIELDS * 128), bf16)
    travel = FIELDS * elements // 2
    sources = inputs + (yz_table,)
    sources = tuple(pltpu.with_memory_space_constraint(a, pltpu.HBM) for a in sources)
    loaded = call(
        load_kernel,
        tuple(shape(a.shape, a.dtype) for a in sources)
        + (shape((512, 768), bf16), shape((384, 512), bf16), shape((384, 384), bf16))
        + (face_rows, shape((travel + 8, 128))),
        *sources,
        scratch=(pltpu.SemaphoreType.DMA((len(sources) - 1 + FIELDS,)),),
        flops=400_000_000,
        in_space=pltpu.HBM,
    )
    fields, sends, speed, names, maps, places, blocks, yz, extract, lift, cross, table, shared = loaded
    cube = shape(fields.shape)
    others = exchange(shared, "ax")
    base, shared = call(
        first_local_kernel, (cube, shape((travel, 128))),
        fields, speed, names, sends, table, yz, lift, extract,
        flops=1_000_000_000,
    )
    firsts = exchange(shared, "ax")
    lanes = sectors * TB * 8
    weights = shape((512, PB * lanes), bf16)
    base, added, radial, axial, weight_high, weight_low = call(
        second_local_kernel,
        (cube, shape((lax.axis_size("ax") * elements, FIELDS * 128)))
        + (shape((64, 128)), shape((64, 128)), weights, weights),
        fields, base, speed, names, sends, yz, lift, extract, cross, *others, maps, places, blocks,
        flops=1_500_000_000,
    )
    rows = FIELDS * 64 * PB // sectors
    piece = shape((rows, lanes))
    relayed, kept = exchange_plan(sectors)
    sampled = call(
        sample_kernel, (cube, shape((len(relayed), rows, lanes))) + (piece,) * len(kept),
        base, names, added, lift, radial, axial, weight_high, weight_low, *firsts[1:],
        scratch=(
            pltpu.VMEM((FIELDS, 4, 128, 128), f32),
            pltpu.VMEM((FIELDS * 64, 512), f32),
            pltpu.VMEM((sectors, rows, lanes), f32),
        ),
        flops=800_000_000,
    )
    new_state, bundle, pieces = sampled[0], sampled[1], dict(zip(kept, sampled[2:]))
    stored = call(
        store_kernel, (cube,), new_state, scratch=(pltpu.SemaphoreType.DMA,), out_space=pltpu.HBM
    )[0]

    def swap(value, mask):
        return lax.ppermute(value, "az", [(i, i ^ mask) for i in range(sectors)])

    bundle = swap(bundle, 1)
    joined = [m - 1 for m in relayed] + [1]
    arrived = [swap(pieces[m], m) for m in kept if m and m not in joined]
    sums = call(join_kernel, (piece,) * len(joined), bundle, *[pieces[m] for m in joined])
    arrived += [swap(value, m) for m, value in zip(joined, sums)]
    arrived.append(pieces[0])
    angle = 2.0 * np.pi / lanes * (np.outer(np.arange(lanes), np.arange(lanes)) % lanes)
    table = np.concatenate([np.cos(angle), -np.sin(angle)], axis=1) * lanes**-0.5
    spectrum = call(
        fourier_kernel, (shape((2, FIELDS, rows // FIELDS, lanes)),),
        jnp.asarray(table, f32), *arrived,
        flops=100_000_000,
    )[0]
    return stored.transpose(1, 0, 2), spectrum


def solution(mesh):
    return jax.shard_map(
        per_device,
        mesh=mesh,
        in_specs=(
            P(("az", "ax"), None, None),
            P(("az", "ax"), None),
            P(("az", "ax"), None, None, None),
            P(("az", "ax"), None),
            P(("az", "ax")),
            P(("az", "ax"), None),
            P(("az", "ax")),
        ),
        out_specs=(P(("az", "ax"), None, None), P(None, None, ("az", "ax"), None)),
        check_vma=False,
    )
```

```python
import functools
import math

import jax
import jax.numpy as jnp
import numpy as np
from jax import lax
from jax.experimental import pallas as pl
from jax.experimental.pallas import tpu as pltpu
from jax.sharding import PartitionSpec as P

TB = 2
PB = 4
FIELDS = 5
time_step = 0.02
penalty = 5.0
highest = lax.Precision.HIGHEST
f32 = jnp.float32
bf16 = jnp.bfloat16


def spectral_derivative():
    points = np.cos(np.pi * np.arange(8) / 7.0)
    ends = (np.arange(8) == 0) | (np.arange(8) == 7)
    scales = np.where(ends, 2.0, 1.0)
    signs = np.where(np.arange(8) % 2 == 0, 1.0, -1.0)
    differ = points[:, None] - points[None, :]
    offdiag = (
        scales[:, None]
        / scales[None, :]
        * signs[:, None]
        * signs[None, :]
        / np.where(np.eye(8) > 0, 1.0, differ)
    )
    inner = -points / (2.0 * np.where(ends, 1.0, 1.0 - points * points))
    corner = (2.0 * 49.0 + 1.0) / 6.0
    diagonal = np.where(np.arange(8) == 0, corner, np.where(np.arange(8) == 7, -corner, inner))
    return np.where(np.eye(8) > 0, diagonal[:, None], offdiag)


def tile_tables():
    deriv = spectral_derivative()
    along_y = np.kron(np.eye(2), np.kron(deriv, np.eye(8))).T
    along_z = np.kron(np.eye(16), deriv).T
    return np.concatenate([along_y, along_z], axis=1)


def face_node(face, position):
    first, second = position >> 3, position & 7
    if face < 2:
        return 448 * face + position
    if face < 4:
        return 56 * (face - 2) + 64 * first + second
    return 7 * (face - 4) + 64 * first + 8 * second


def iota(dims, axis):
    return lax.broadcasted_iota(jnp.int32, dims, axis)


def face_counts():
    node = iota((1, 512), 1)
    count = jnp.zeros((1, 512), f32)
    for coordinate in (node >> 6, (node >> 3) & 7, node & 7):
        count = count + jnp.where((coordinate == 0) | (coordinate == 7), 1.0, 0.0)
    return count


def split(value):
    high = value.astype(bf16)
    return high, (value - high.astype(f32)).astype(bf16)


def dot(a, b):
    return jnp.dot(a, b, preferred_element_type=f32)


def low_half(shape):
    return lax.broadcasted_iota(jnp.int32, shape, len(shape) - 1) < 64


def local_key(elements):
    lane = lax.broadcasted_iota(jnp.int32, (1, 6 * elements), 1)
    face = jnp.zeros_like(lane)
    for f in range(1, 6):
        face = face + (lane >= f * elements).astype(jnp.int32)
    return 6 * (lane - face * elements) + face


def column(row_ref):
    return row_ref[...].astype(f32).T


def pick_rows(names, keys):
    return jnp.where(names == keys.astype(f32), 1.0, 0.0).astype(bf16)


def face_table(fields, extract):
    elements = fields.shape[0] // FIELDS
    faces = dot(fields.astype(bf16), extract).astype(bf16)
    half = low_half((fields.shape[0], 128))
    ends = [fields[:, :128], fields[:, 384:]]
    turned = [pltpu.roll(end, 64, 1) for end in ends]
    ends = [jnp.where(half, ends[0], turned[0]), jnp.where(half, turned[1], ends[1])]
    blocks = [end.astype(bf16) for end in ends] + [
        faces[:, f * 128 : (f + 1) * 128] for f in range(4)
    ]
    rows = [
        jnp.concatenate(
            [block[c * elements : (c + 1) * elements] for c in range(FIELDS)], axis=1
        )
        for block in blocks
    ]
    return jnp.concatenate(rows, axis=0)


def share_rows(table, picked, out_ref):
    elements = picked.shape[0]
    rows = dot(picked, table)
    field = [rows[:, c * 128 : (c + 1) * 128] for c in range(FIELDS)]
    half = low_half((elements, 128))
    out_ref[0:elements, :] = jnp.where(half, field[0], field[1])
    out_ref[elements : 2 * elements, :] = jnp.where(half, field[2], field[3])
    middle = elements // 2
    out_ref[2 * elements : 2 * elements + middle, :] = jnp.where(
        half[:middle], field[4][:middle], field[4][middle:]
    )


def unpack_rows(ref, elements):
    half = low_half((elements, 128))
    middle = elements // 2
    fields = []
    for first in range(2):
        both = ref[first * elements : (first + 1) * elements, :]
        turned = pltpu.roll(both, 64, 1)
        fields.append(jnp.where(half, both, turned))
        fields.append(jnp.where(half, turned, both))
    both = ref[2 * elements : 2 * elements + middle, :]
    turned = pltpu.roll(both, 64, 1)
    fields.append(
        jnp.concatenate(
            [jnp.where(half[:middle], both, turned), jnp.where(half[:middle], turned, both)],
            axis=0,
        )
    )
    return jnp.concatenate(fields, axis=1)


def share_names(names_ref, picked, out_ref):
    elements = picked.shape[0]
    lane = iota((1, 6 * elements), 1)
    face = jnp.zeros_like(lane)
    for f in range(1, 6):
        face = face + (lane >= f * elements).astype(jnp.int32)
    tile = (iota((elements, 6 * elements), 0) == lane - face * elements).astype(f32)
    names = jnp.dot(
        names_ref[...].astype(f32), tile, precision=highest, preferred_element_type=f32
    )
    rows = jnp.concatenate([names, face.astype(f32), jnp.zeros((1, 6 * elements), f32)], axis=0)
    out_ref[-8:, :] = jnp.zeros((8, 128), f32)
    out_ref[-8:, :elements] = lax.dot_general(
        rows, picked.astype(f32), (((1,), (1,)), ((), ())),
        precision=highest, preferred_element_type=f32,
    )


def facing_pairs(picked, table, elements):
    half = low_half((elements, 128))
    facing = dot(picked, table)
    field_rows = []
    for c in range(FIELDS):
        blocks = [
            facing[f * elements : (f + 1) * elements, c * 128 : (c + 1) * 128] for f in range(6)
        ]
        pairs = [jnp.where(half, blocks[f], blocks[f + 1]) for f in range(0, 6, 2)]
        field_rows.append(jnp.concatenate(pairs, axis=1))
    return jnp.concatenate(field_rows, axis=0).astype(bf16)


def lift_rows(picked, table, lift, elements):
    half = low_half((elements, 128))
    facing = dot(picked, table)
    ends, inner = [], []
    for c in range(FIELDS):
        blocks = [
            facing[f * elements : (f + 1) * elements, c * 128 : (c + 1) * 128] for f in range(6)
        ]
        ends.append((jnp.where(half, blocks[0], 0.0), jnp.where(half, 0.0, blocks[1])))
        pairs = [jnp.where(half, blocks[f], blocks[f + 1]) for f in (2, 4)]
        inner.append(jnp.concatenate(pairs, axis=1))
    lifted = dot(jnp.concatenate(inner, axis=0).astype(bf16), lift)
    rows = []
    for c in range(FIELDS):
        part = lifted[c * elements : (c + 1) * elements]
        rows.append(
            jnp.concatenate(
                [part[:, :128] + ends[c][0], part[:, 128:384], part[:, 384:] + ends[c][1]], axis=1
            )
        )
    return jnp.concatenate(rows, axis=0)


def x_derivative(fields):
    deriv = spectral_derivative()
    half = low_half((1, 128))
    tiles = [fields[:, 128 * i : 128 * i + 128] for i in range(4)]
    turned = [pltpu.roll(tile, 64, 1) for tile in tiles]
    out = []
    for j in range(4):
        total = None
        for i in range(4):
            same = jnp.where(half, float(deriv[2 * j, 2 * i]), float(deriv[2 * j + 1, 2 * i + 1]))
            cross = jnp.where(half, float(deriv[2 * j, 2 * i + 1]), float(deriv[2 * j + 1, 2 * i]))
            part = same * tiles[i] + cross * turned[i]
            total = part if total is None else total + part
        out.append(total)
    return out


def local_rate(fields, velocity_ref, neigh_ref, table, yz_high, yz_low, lift):
    elements = neigh_ref.shape[1]
    high, low = split(fields)
    speed = velocity_ref[...].T
    speeds = [jnp.broadcast_to(speed[:, d : d + 1], (elements, 128)) for d in range(3)]
    yz_twice = jnp.concatenate([yz_high, yz_high], axis=0)
    both = []
    for j in range(4):
        lanes = slice(j * 128, (j + 1) * 128)
        parts = jnp.concatenate([high[:, lanes], low[:, lanes]], axis=1)
        both.append(dot(parts, yz_twice) + dot(high[:, lanes], yz_low))
    chunk = elements // 2
    rows = []
    for c in range(FIELDS):
        for part in range(2):
            begin = c * elements + part * chunk
            along_x = x_derivative(fields[begin : begin + chunk])
            here = [speed_rows[part * chunk : (part + 1) * chunk] for speed_rows in speeds]
            tiles = [
                here[0] * along_x[j]
                + here[1] * both[j][begin : begin + chunk, :128]
                + here[2] * both[j][begin : begin + chunk, 128:]
                for j in range(4)
            ]
            rows.append(jnp.concatenate(tiles, axis=1))
    picked = pick_faces(column(neigh_ref), local_key(elements))
    lifted = lift_rows(picked, table, lift, elements)
    return penalty * (lifted - face_counts() * fields) - jnp.concatenate(rows, axis=0)


def pick_faces(names, keys):
    return jnp.concatenate([pick_rows(names[:, f : f + 1], keys) for f in range(6)], axis=0)


def remote_keys(elements):
    me = lax.axis_index("ax")
    lane = iota((1, elements), 1)
    return jnp.concatenate(
        [6 * elements + (me ^ m) * elements + lane for m in range(lax.axis_size("ax"))], axis=1
    )


def shared_table(refs, elements):
    return jnp.concatenate([unpack_rows(ref, elements) for ref in refs], axis=0)


def rows_of(ref):
    fields, elements, nodes = ref.shape
    return ref[...].reshape(fields * elements, nodes)


def load_kernel(*refs):
    count = 8
    sources, loaded = refs[:count], refs[count : 2 * count]
    extract_ref, lift_ref, cross_ref, table_ref, shared_ref, sems = refs[2 * count :]
    pairs = list(zip(sources, loaded))
    fields = [(pairs[0][0].at[c], pairs[0][1].at[c]) for c in range(FIELDS)]
    copies = [
        pltpu.make_async_copy(source, target, sems.at[i])
        for i, (source, target) in enumerate(pairs[1:4] + fields + pairs[4:])
    ]
    for copy in copies:
        copy.start()
    row, lane = iota((512, 128), 0), iota((512, 128), 1)
    for f in range(4):
        here = row == face_node(f + 2, lane & 63)
        extract_ref[:, f * 128 : (f + 1) * 128] = jnp.where(here, 1.0, 0.0).astype(bf16)
    for copy in copies[:3]:
        copy.wait()
    picked = pick_rows(column(loaded[1]), local_key(loaded[1].shape[1]))
    share_names(loaded[3], picked, shared_ref)
    row, lane = iota((64, 512), 0), iota((64, 512), 1)
    for f in range(4):
        here = face_node(f + 2, row) == lane
        lift_ref[f * 64 : (f + 1) * 64, :] = jnp.where(here, 1.0, 0.0).astype(bf16)
    row, lane = iota((64, 128), 0), iota((64, 128), 1)
    for f in range(6):
        for g in range(0, 6, 2):
            node = jnp.where(lane < 64, face_node(g, lane & 63), face_node(g + 1, lane & 63))
            cross_ref[f * 64 : (f + 1) * 64, g * 64 : (g + 2) * 64] = jnp.where(
                face_node(f, row) == node, 1.0, 0.0
            ).astype(bf16)
    for copy in copies[3:]:
        copy.wait()
    table = face_table(rows_of(loaded[0]), extract_ref[...])
    table_ref[...] = table
    share_rows(table, picked, shared_ref)


def first_local_kernel(
    state_ref, velocity_ref, neigh_ref, send_ref, table_ref, yz, lift, extract, out_ref, shared_ref
):
    fields = rows_of(state_ref)
    rate = local_rate(
        fields, velocity_ref, neigh_ref, table_ref[...], *split(yz[...]), lift[...]
    )
    base = fields + time_step * rate
    out_ref[...] = base.reshape(out_ref.shape)
    picked = pick_rows(column(send_ref), local_key(send_ref.shape[1]))
    share_rows(face_table(base, extract[...]), picked, shared_ref)


def fill_maps(
    maps_ref, device_ref, block_ref, radial_ref, axial_ref, high_ref, low_ref
):
    elements = maps_ref.shape[2]
    row, lane = iota((elements, 128), 0), iota((elements, 128), 1)
    twice = ((lane & 63) == row).astype(f32).astype(bf16)
    radial_ref[...] = exact_dot(maps_ref[1], twice)
    swap = ((iota((64, 64), 0) >> 3) + 8 * (iota((64, 64), 0) & 7) == iota((64, 64), 1)).astype(f32)
    axial = [dot(swap.astype(bf16), part).astype(bf16) for part in split(maps_ref[2])]
    axial_ref[...] = dot(axial[0], twice) + dot(axial[1], twice)
    tile_row, tile_lane = iota((64, 1024), 0), iota((64, 1024), 1)
    tile = ((tile_row >> 3) == (tile_lane & 7)) & ((tile_row & 7) == (tile_lane >> 7))
    tile = jnp.where(tile, 1.0, 0.0).astype(bf16)
    values = [dot(part, tile) for part in split(maps_ref[0].T)]
    places = device_ref[...].astype(f32).T
    blocks = block_ref[...].astype(f32).T
    theta_lanes = high_ref.shape[1] // PB
    upper = (blocks >= PB).astype(f32)
    sector_key = places * TB + upper
    plane_key = blocks - PB * upper
    gap = jnp.zeros((64 - elements, high_ref.shape[1]), bf16)
    for y in range(8):
        start = y * 64
        high_ref[start + elements : start + 64, :] = gap
        low_ref[start + elements : start + 64, :] = gap
    for pb in range(PB):
        for tile_at in range(theta_lanes // 128):
            here = ((lane + tile_at * 128) >> 3).astype(f32)
            mine = (sector_key == here) & (plane_key == pb)
            begin = pb * theta_lanes + tile_at * 128
            for ref, value in zip((high_ref, low_ref), values):
                for y in range(8):
                    ref[y * 64 : y * 64 + elements, begin : begin + 128] = jnp.where(
                        mine, value[:, y * 128 : (y + 1) * 128], 0.0
                    ).astype(bf16)


def exact_dot(value, choice):
    high, low = split(value)
    return dot(high, choice) + dot(low, choice)


def second_local_kernel(
    state_ref, base_ref, velocity_ref, neigh_ref, send_ref, yz, lift, extract, cross, *refs
):
    shared_refs, map_refs, (out_ref, added_ref) = refs[:-9], refs[-9:-6] + refs[-4:], refs[-6:-4]
    fill_maps(*map_refs)
    elements = neigh_ref.shape[1]
    table = shared_table(shared_refs, elements).astype(bf16)
    keys = remote_keys(elements)
    picked = pick_faces(column(neigh_ref), keys)
    terms = lift_rows(picked, table, lift[...], elements)
    first = rows_of(base_ref) + (time_step * penalty) * terms
    first_table = face_table(first, extract[...])
    rate = local_rate(
        first, velocity_ref, neigh_ref, first_table, *split(yz[...]), lift[...]
    )
    second = 0.5 * (rows_of(state_ref) + first + time_step * rate)
    out_ref[...] = second.reshape(out_ref.shape)
    own = pick_rows(column(send_ref), local_key(elements))
    added_ref[:elements, :] = dot(own, first_table)
    names = jnp.concatenate([ref[-8:, :].T[:elements] for ref in shared_refs[1:]], axis=0)
    count = names.shape[0]
    pairs = facing_pairs(pick_faces(names, keys), table, count)
    face = names[:, 6:7]
    half = low_half((count, 128))
    same = half != ((face == 1) | (face == 3) | (face == 5))
    for c in range(FIELDS):
        faces = dot(pairs[c * count : (c + 1) * count], cross[...])
        added = jnp.where(face >= 2, faces[:, 128:256], faces[:, :128])
        added = jnp.where(face >= 4, faces[:, 256:], added)
        added = jnp.where(same, added, pltpu.roll(added, 64, 1))
        added_ref[elements:, c * 128 : (c + 1) * 128] = (time_step * penalty) * added


def exchange_plan(size):
    straight = [m for m in range(size // 2, 3 * size // 4) if m & 1]
    relayed = [m for m in range(size - 1, 1, -2) if m not in straight]
    return relayed, [m for m in range(size) if m not in relayed]


def sample_kernel(
    base_ref, neigh_ref, added_ref, lift, radial_ref, axial_ref, high_ref, low_ref, *refs
):
    sectors = high_ref.shape[1] // (PB * TB * 8)
    shares = lax.axis_size("ax") - 1
    shared_refs = refs[:shares]
    new_ref, out_refs = refs[shares], refs[shares + 1 : -2]
    turned_ref, parts_ref = refs[-2:]
    elements = neigh_ref.shape[1]
    added = added_ref[elements:, :] + shared_table(shared_refs, elements)
    table = jnp.concatenate([added_ref[:elements, :], added], axis=0).astype(bf16)
    picked = pick_faces(column(neigh_ref), remote_keys(elements))
    terms = lift_rows(picked, table, lift[...], elements)
    new_state = rows_of(base_ref) + (0.5 * time_step * penalty) * terms
    new_ref[...] = new_state.reshape(new_ref.shape)
    gap = jnp.zeros((64 - elements, 128), f32)
    for c in range(FIELDS):
        for j in range(4):
            part = new_state[c * elements : (c + 1) * elements, j * 128 : (j + 1) * 128]
            after = pltpu.roll(part, 120, 1)
            turned_ref[c, j] = jnp.concatenate([part, gap, after, gap], axis=0).T
    radial = radial_ref[...]
    axial = axial_ref[...]
    theta_lanes = high_ref.shape[1] // PB
    groups = sectors // PB
    rows = 64 // groups
    for pair in range(2):
        tiles = []
        for yy in (2 * pair, 2 * pair + 1):
            values = []
            for c in range(FIELDS):
                inputs = []
                for x in range(8):
                    start = (x % 2) * 64 + 16 * yy
                    inputs.append(turned_ref[c, x // 2, start : start + 8, :])
                for r in range(8):
                    mixed = radial[8 * r : 8 * r + 1, :] * inputs[0]
                    for x in range(1, 8):
                        mixed = mixed + radial[8 * r + x : 8 * r + x + 1, :] * inputs[x]
                    value = axial[0:8, :] * mixed[0:1, :]
                    for z in range(1, 8):
                        value = value + axial[8 * z : 8 * z + 8, :] * mixed[z : z + 1, :]
                    values.append(value)
            tiles.append(jnp.concatenate(values, axis=0))
        mapped_high, mapped_low = split(jnp.concatenate(tiles, axis=1))
        depth = slice(256 * pair, 256 * pair + 256)
        weight_high = high_ref[depth, :]
        part = (
            dot(mapped_high, weight_high)
            + dot(mapped_low, weight_high)
            + dot(mapped_high, low_ref[depth, :])
        )
        total = part if pair == 0 else total + part
    for pb in range(PB):
        for g in range(groups):
            for c in range(FIELDS):
                start = c * 64 + g * rows
                parts_ref[pb * groups + g, c * rows : (c + 1) * rows, :] = total[
                    start : start + rows, pb * theta_lanes : (pb + 1) * theta_lanes
                ]
    owner = lax.axis_index("az")
    relayed, kept = exchange_plan(sectors)
    for i, m in enumerate(relayed):
        out_refs[0][i] = parts_ref[owner ^ m]
    for i, m in enumerate(kept):
        out_refs[1 + i][...] = parts_ref[owner ^ m]


def fourier_kernel(table_ref, *refs):
    out_ref = refs[-1]
    total = refs[0][...]
    for ref in refs[1:-1]:
        total = total + ref[...]
    high, low = split(total)
    weight, weight_low = split(table_ref[...])
    coeffs = dot(high, weight) + dot(low, weight) + dot(high, weight_low)
    width = total.shape[1]
    rows = total.shape[0] // FIELDS
    for k in range(2):
        for c in range(FIELDS):
            out_ref[k, c] = coeffs[c * rows : (c + 1) * rows, k * width : (k + 1) * width]


def join_kernel(got_ref, *refs):
    count = len(refs) // 2
    for i in range(count - 1):
        refs[count + i][...] = refs[i][...] + got_ref[i]
    refs[-1][...] = refs[count - 1][...]


def store_kernel(new_ref, out_ref, sem):
    copy = pltpu.make_async_copy(new_ref, out_ref, sem)
    copy.start()
    copy.wait()


def shape(dims, dtype=f32):
    return jax.ShapeDtypeStruct(dims, dtype)


def call(kernel, outs, *args, scratch=(), flops=0, in_space=pltpu.VMEM, out_space=pltpu.VMEM, aliases={}):
    size = sum(math.prod(a.shape) * a.dtype.itemsize for a in list(args) + list(outs))
    return pl.pallas_call(
        kernel,
        out_shape=outs,
        in_specs=[pl.BlockSpec(memory_space=in_space)] * len(args),
        out_specs=tuple([pl.BlockSpec(memory_space=out_space)] * len(outs)),
        scratch_shapes=list(scratch),
        input_output_aliases=aliases,
        cost_estimate=pl.CostEstimate(flops=flops, bytes_accessed=size, transcendentals=0),
        compiler_params=pltpu.CompilerParams(vmem_limit_bytes=48 * 1024 * 1024),
    )(*args)


def exchange(value, axis):
    size = lax.axis_size(axis)
    return [value] + [
        lax.ppermute(value, axis, [(i, i ^ m) for i in range(size)]) for m in range(size - 1, 0, -1)
    ][::-1]


def per_device(state, velocity, interp_maps, neighbours, send_faces, owner_device, owner_block):
    elements = state.shape[0]
    sectors = lax.axis_size("az")
    inputs = (
        state.transpose(1, 0, 2),
        send_faces.reshape(1, elements),
        velocity.T,
        neighbours.T,
        interp_maps.transpose(1, 2, 3, 0).reshape(3, 64, elements),
        owner_device.reshape(1, elements),
        owner_block.reshape(1, elements),
    )
    yz_table = jnp.asarray(tile_tables(), f32)
    face_rows = shape((6 * elements, FIELDS * 128), bf16)
    travel = FIELDS * elements // 2
    sources = inputs + (yz_table,)
    sources = tuple(pltpu.with_memory_space_constraint(a, pltpu.HBM) for a in sources)
    loaded = call(
        load_kernel,
        tuple(shape(a.shape, a.dtype) for a in sources)
        + (shape((512, 512), bf16), shape((256, 512), bf16), shape((384, 384), bf16))
        + (face_rows, shape((travel + 8, 128))),
        *sources,
        scratch=(pltpu.SemaphoreType.DMA((len(sources) - 1 + FIELDS,)),),
        flops=400_000_000,
        in_space=pltpu.HBM,
    )
    fields, sends, speed, names, maps, places, blocks, yz, extract, lift, cross, table, shared = loaded
    cube = shape(fields.shape)
    others = exchange(shared, "ax")
    base, shared = call(
        first_local_kernel, (cube, shape((travel, 128))),
        fields, speed, names, sends, table, yz, lift, extract,
        flops=1_000_000_000,
    )
    firsts = exchange(shared, "ax")
    lanes = sectors * TB * 8
    weights = shape((512, PB * lanes), bf16)
    base, added, radial, axial, weight_high, weight_low = call(
        second_local_kernel,
        (cube, shape((lax.axis_size("ax") * elements, FIELDS * 128)))
        + (shape((64, 128)), shape((64, 128)), weights, weights),
        fields, base, speed, names, sends, yz, lift, extract, cross, *others, maps, places, blocks,
        flops=1_500_000_000,
    )
    rows = FIELDS * 64 * PB // sectors
    piece = shape((rows, lanes))
    relayed, kept = exchange_plan(sectors)
    sampled = call(
        sample_kernel, (cube, shape((len(relayed), rows, lanes))) + (piece,) * len(kept),
        base, names, added, lift, radial, axial, weight_high, weight_low, *firsts[1:],
        scratch=(
            pltpu.VMEM((FIELDS, 4, 128, 128), f32),
            pltpu.VMEM((sectors, rows, lanes), f32),
        ),
        flops=800_000_000,
    )
    new_state, bundle, pieces = sampled[0], sampled[1], dict(zip(kept, sampled[2:]))
    stored = call(
        store_kernel, (cube,), new_state, scratch=(pltpu.SemaphoreType.DMA,), out_space=pltpu.HBM
    )[0]

    def swap(value, mask):
        return lax.ppermute(value, "az", [(i, i ^ mask) for i in range(sectors)])

    bundle = swap(bundle, 1)
    joined = [m - 1 for m in relayed] + [1]
    arrived = [swap(pieces[m], m) for m in kept if m and m not in joined]
    sums = call(join_kernel, (piece,) * len(joined), bundle, *[pieces[m] for m in joined])
    arrived += [swap(value, m) for m, value in zip(joined, sums)]
    arrived.append(pieces[0])
    angle = 2.0 * np.pi / lanes * (np.outer(np.arange(lanes), np.arange(lanes)) % lanes)
    table = np.concatenate([np.cos(angle), -np.sin(angle)], axis=1) * lanes**-0.5
    spectrum = call(
        fourier_kernel, (shape((2, FIELDS, rows // FIELDS, lanes)),),
        jnp.asarray(table, f32), *arrived,
        flops=100_000_000,
    )[0]
    return stored.transpose(1, 0, 2), spectrum


def solution(mesh):
    return jax.shard_map(
        per_device,
        mesh=mesh,
        in_specs=(
            P(("az", "ax"), None, None),
            P(("az", "ax"), None),
            P(("az", "ax"), None, None, None),
            P(("az", "ax"), None),
            P(("az", "ax")),
            P(("az", "ax"), None),
            P(("az", "ax")),
        ),
        out_specs=(P(("az", "ax"), None, None), P(None, None, ("az", "ax"), None)),
        check_vma=False,
    )
```

```python
import functools
import math

import jax
import jax.numpy as jnp
import numpy as np
from jax import lax
from jax.experimental import pallas as pl
from jax.experimental.pallas import tpu as pltpu
from jax.sharding import PartitionSpec as P

TB = 2
PB = 4
FIELDS = 5
time_step = 0.02
penalty = 5.0
highest = lax.Precision.HIGHEST
f32 = jnp.float32
bf16 = jnp.bfloat16


def spectral_derivative():
    points = np.cos(np.pi * np.arange(8) / 7.0)
    ends = (np.arange(8) == 0) | (np.arange(8) == 7)
    scales = np.where(ends, 2.0, 1.0)
    signs = np.where(np.arange(8) % 2 == 0, 1.0, -1.0)
    differ = points[:, None] - points[None, :]
    offdiag = (
        scales[:, None]
        / scales[None, :]
        * signs[:, None]
        * signs[None, :]
        / np.where(np.eye(8) > 0, 1.0, differ)
    )
    inner = -points / (2.0 * np.where(ends, 1.0, 1.0 - points * points))
    corner = (2.0 * 49.0 + 1.0) / 6.0
    diagonal = np.where(np.arange(8) == 0, corner, np.where(np.arange(8) == 7, -corner, inner))
    return np.where(np.eye(8) > 0, diagonal[:, None], offdiag)


def tile_tables():
    deriv = spectral_derivative()
    along_y = np.kron(np.eye(2), np.kron(deriv, np.eye(8))).T
    along_z = np.kron(np.eye(16), deriv).T
    return np.concatenate([along_y, along_z], axis=1)


def face_node(face, position):
    first, second = position >> 3, position & 7
    if face < 2:
        return 448 * face + position
    if face < 4:
        return 56 * (face - 2) + 64 * first + second
    return 7 * (face - 4) + 64 * first + 8 * second


def iota(dims, axis):
    return lax.broadcasted_iota(jnp.int32, dims, axis)


def face_counts():
    node = iota((1, 512), 1)
    count = jnp.zeros((1, 512), f32)
    for coordinate in (node >> 6, (node >> 3) & 7, node & 7):
        count = count + jnp.where((coordinate == 0) | (coordinate == 7), 1.0, 0.0)
    return count


def split(value):
    high = value.astype(bf16)
    return high, (value - high.astype(f32)).astype(bf16)


def remainder(value):
    return value - value.astype(bf16).astype(f32)


def dot(a, b):
    return jnp.dot(a, b, preferred_element_type=f32)


def low_half(shape):
    return lax.broadcasted_iota(jnp.int32, shape, len(shape) - 1) < 64


def local_key(elements):
    lane = lax.broadcasted_iota(jnp.int32, (1, 6 * elements), 1)
    face = jnp.zeros_like(lane)
    for f in range(1, 6):
        face = face + (lane >= f * elements).astype(jnp.int32)
    return 6 * (lane - face * elements) + face


def column(row_ref):
    return row_ref[...].astype(f32).T


def pick_rows(names, keys):
    return jnp.where(names == keys.astype(f32), 1.0, 0.0).astype(bf16)


def face_table(fields, extract):
    elements = fields.shape[0] // FIELDS
    faces = dot(fields.astype(bf16), extract).astype(bf16)
    half = low_half((fields.shape[0], 128))
    ends = [fields[:, :128], fields[:, 384:]]
    turned = [pltpu.roll(end, 64, 1) for end in ends]
    ends = [jnp.where(half, ends[0], turned[0]), jnp.where(half, turned[1], ends[1])]
    blocks = [end.astype(bf16) for end in ends] + [
        faces[:, f * 128 : (f + 1) * 128] for f in range(4)
    ]
    rows = [
        jnp.concatenate(
            [block[c * elements : (c + 1) * elements] for c in range(FIELDS)], axis=1
        )
        for block in blocks
    ]
    return jnp.concatenate(rows, axis=0)


def share_rows(table, picked, out_ref):
    elements = picked.shape[0]
    rows = dot(picked, table)
    field = [rows[:, c * 128 : (c + 1) * 128] for c in range(FIELDS)]
    half = low_half((elements, 128))
    out_ref[0:elements, :] = jnp.where(half, field[0], field[1])
    out_ref[elements : 2 * elements, :] = jnp.where(half, field[2], field[3])
    middle = elements // 2
    out_ref[2 * elements : 2 * elements + middle, :] = jnp.where(
        half[:middle], field[4][:middle], field[4][middle:]
    )


def unpack_rows(ref, elements):
    half = low_half((elements, 128))
    middle = elements // 2
    fields = []
    for first in range(2):
        both = ref[first * elements : (first + 1) * elements, :]
        turned = pltpu.roll(both, 64, 1)
        fields.append(jnp.where(half, both, turned))
        fields.append(jnp.where(half, turned, both))
    both = ref[2 * elements : 2 * elements + middle, :]
    turned = pltpu.roll(both, 64, 1)
    fields.append(
        jnp.concatenate(
            [jnp.where(half[:middle], both, turned), jnp.where(half[:middle], turned, both)],
            axis=0,
        )
    )
    return jnp.concatenate(fields, axis=1)


def share_names(names_ref, picked, out_ref):
    elements = picked.shape[0]
    lane = iota((1, 6 * elements), 1)
    face = jnp.zeros_like(lane)
    for f in range(1, 6):
        face = face + (lane >= f * elements).astype(jnp.int32)
    tile = (iota((elements, 6 * elements), 0) == lane - face * elements).astype(f32)
    names = jnp.dot(
        names_ref[...].astype(f32), tile, precision=highest, preferred_element_type=f32
    )
    rows = jnp.concatenate([names, face.astype(f32), jnp.zeros((1, 6 * elements), f32)], axis=0)
    out_ref[-8:, :] = jnp.zeros((8, 128), f32)
    out_ref[-8:, :elements] = lax.dot_general(
        rows, picked.astype(f32), (((1,), (1,)), ((), ())),
        precision=highest, preferred_element_type=f32,
    )


def facing_pairs(picked, table, elements):
    half = low_half((elements, 128))
    facing = dot(picked, table)
    field_rows = []
    for c in range(FIELDS):
        blocks = [
            facing[f * elements : (f + 1) * elements, c * 128 : (c + 1) * 128] for f in range(6)
        ]
        pairs = [jnp.where(half, blocks[f], blocks[f + 1]) for f in range(0, 6, 2)]
        field_rows.append(jnp.concatenate(pairs, axis=1))
    return jnp.concatenate(field_rows, axis=0).astype(bf16)


def lift_rows(picked, table, lift, elements):
    half = low_half((elements, 128))
    facing = dot(picked, table)
    ends, inner = [], []
    for c in range(FIELDS):
        blocks = [
            facing[f * elements : (f + 1) * elements, c * 128 : (c + 1) * 128] for f in range(6)
        ]
        ends.append((jnp.where(half, blocks[0], 0.0), jnp.where(half, 0.0, blocks[1])))
        pairs = [jnp.where(half, blocks[f], blocks[f + 1]) for f in (2, 4)]
        inner.append(jnp.concatenate(pairs, axis=1))
    lifted = dot(jnp.concatenate(inner, axis=0).astype(bf16), lift)
    rows = []
    for c in range(FIELDS):
        part = lifted[c * elements : (c + 1) * elements]
        rows.append(
            jnp.concatenate(
                [part[:, :128] + ends[c][0], part[:, 128:384], part[:, 384:] + ends[c][1]], axis=1
            )
        )
    return jnp.concatenate(rows, axis=0)


def x_derivative(fields):
    deriv = spectral_derivative()
    half = low_half((1, 128))
    tiles = [fields[:, 128 * i : 128 * i + 128] for i in range(4)]
    turned = [pltpu.roll(tile, 64, 1) for tile in tiles]
    out = []
    for j in range(4):
        total = None
        for i in range(4):
            same = jnp.where(half, float(deriv[2 * j, 2 * i]), float(deriv[2 * j + 1, 2 * i + 1]))
            cross = jnp.where(half, float(deriv[2 * j, 2 * i + 1]), float(deriv[2 * j + 1, 2 * i]))
            part = same * tiles[i] + cross * turned[i]
            total = part if total is None else total + part
        out.append(total)
    return out


def local_rate(fields, velocity_ref, neigh_ref, table, yz_high, yz_low, lift):
    elements = neigh_ref.shape[1]
    high, low = split(fields)
    speed = velocity_ref[...].T
    speeds = [jnp.broadcast_to(speed[:, d : d + 1], (elements, 128)) for d in range(3)]
    yz_twice = jnp.concatenate([yz_high, yz_high], axis=0)
    both = []
    for j in range(4):
        lanes = slice(j * 128, (j + 1) * 128)
        parts = jnp.concatenate([high[:, lanes], low[:, lanes]], axis=1)
        both.append(dot(parts, yz_twice) + dot(high[:, lanes], yz_low))
    chunk = elements // 2
    rows = []
    for c in range(FIELDS):
        for part in range(2):
            begin = c * elements + part * chunk
            along_x = x_derivative(fields[begin : begin + chunk])
            here = [speed_rows[part * chunk : (part + 1) * chunk] for speed_rows in speeds]
            tiles = [
                here[0] * along_x[j]
                + here[1] * both[j][begin : begin + chunk, :128]
                + here[2] * both[j][begin : begin + chunk, 128:]
                for j in range(4)
            ]
            rows.append(jnp.concatenate(tiles, axis=1))
    picked = pick_faces(column(neigh_ref), local_key(elements))
    lifted = lift_rows(picked, table, lift, elements)
    return penalty * (lifted - face_counts() * fields) - jnp.concatenate(rows, axis=0)


def pick_faces(names, keys):
    return jnp.concatenate([pick_rows(names[:, f : f + 1], keys) for f in range(6)], axis=0)


def remote_keys(elements):
    me = lax.axis_index("ax")
    lane = iota((1, elements), 1)
    return jnp.concatenate(
        [6 * elements + (me ^ m) * elements + lane for m in range(lax.axis_size("ax"))], axis=1
    )


def shared_table(refs, elements):
    return jnp.concatenate([unpack_rows(ref, elements) for ref in refs], axis=0)


def rows_of(ref):
    fields, elements, nodes = ref.shape
    return ref[...].reshape(fields * elements, nodes)


def load_kernel(*refs):
    count = 8
    sources, loaded = refs[:count], refs[count : 2 * count]
    extract_ref, lift_ref, cross_ref, table_ref, shared_ref, sems = refs[2 * count :]
    pairs = list(zip(sources, loaded))
    fields = [(pairs[0][0].at[c], pairs[0][1].at[c]) for c in range(FIELDS)]
    copies = [
        pltpu.make_async_copy(source, target, sems.at[i])
        for i, (source, target) in enumerate(pairs[1:4] + fields + pairs[4:])
    ]
    for copy in copies:
        copy.start()
    row, lane = iota((512, 128), 0), iota((512, 128), 1)
    for f in range(4):
        here = row == face_node(f + 2, lane & 63)
        extract_ref[:, f * 128 : (f + 1) * 128] = jnp.where(here, 1.0, 0.0).astype(bf16)
    for copy in copies[:3]:
        copy.wait()
    picked = pick_rows(column(loaded[1]), local_key(loaded[1].shape[1]))
    share_names(loaded[3], picked, shared_ref)
    row, lane = iota((64, 512), 0), iota((64, 512), 1)
    for f in range(4):
        here = face_node(f + 2, row) == lane
        lift_ref[f * 64 : (f + 1) * 64, :] = jnp.where(here, 1.0, 0.0).astype(bf16)
    row, lane = iota((64, 128), 0), iota((64, 128), 1)
    for f in range(6):
        for g in range(0, 6, 2):
            node = jnp.where(lane < 64, face_node(g, lane & 63), face_node(g + 1, lane & 63))
            cross_ref[f * 64 : (f + 1) * 64, g * 64 : (g + 2) * 64] = jnp.where(
                face_node(f, row) == node, 1.0, 0.0
            ).astype(bf16)
    for copy in copies[3:]:
        copy.wait()
    table = face_table(rows_of(loaded[0]), extract_ref[...])
    table_ref[...] = table
    share_rows(table, picked, shared_ref)


def first_local_kernel(
    state_ref, velocity_ref, neigh_ref, send_ref, table_ref, yz, lift, extract, out_ref, shared_ref
):
    fields = rows_of(state_ref)
    rate = local_rate(
        fields, velocity_ref, neigh_ref, table_ref[...], *split(yz[...]), lift[...]
    )
    base = fields + time_step * rate
    out_ref[...] = base.reshape(out_ref.shape)
    picked = pick_rows(column(send_ref), local_key(send_ref.shape[1]))
    share_rows(face_table(base + remainder(fields), extract[...]), picked, shared_ref)


def fill_maps(
    maps_ref, device_ref, block_ref, radial_ref, axial_ref, high_ref, low_ref
):
    elements = maps_ref.shape[2]
    row, lane = iota((elements, 128), 0), iota((elements, 128), 1)
    twice = ((lane & 63) == row).astype(f32).astype(bf16)
    radial_ref[...] = exact_dot(maps_ref[1], twice)
    swap = ((iota((64, 64), 0) >> 3) + 8 * (iota((64, 64), 0) & 7) == iota((64, 64), 1)).astype(f32)
    axial = [dot(swap.astype(bf16), part).astype(bf16) for part in split(maps_ref[2])]
    axial_ref[...] = dot(axial[0], twice) + dot(axial[1], twice)
    tile_row, tile_lane = iota((64, 1024), 0), iota((64, 1024), 1)
    tile = ((tile_row >> 3) == (tile_lane & 7)) & ((tile_row & 7) == (tile_lane >> 7))
    tile = jnp.where(tile, 1.0, 0.0).astype(bf16)
    values = [dot(part, tile) for part in split(maps_ref[0].T)]
    places = device_ref[...].astype(f32).T
    blocks = block_ref[...].astype(f32).T
    theta_lanes = high_ref.shape[1] // PB
    upper = (blocks >= PB).astype(f32)
    sector_key = places * TB + upper
    plane_key = blocks - PB * upper
    gap = jnp.zeros((64 - elements, high_ref.shape[1]), bf16)
    for y in range(8):
        start = y * 64
        high_ref[start + elements : start + 64, :] = gap
        low_ref[start + elements : start + 64, :] = gap
    for pb in range(PB):
        for tile_at in range(theta_lanes // 128):
            here = ((lane + tile_at * 128) >> 3).astype(f32)
            mine = (sector_key == here) & (plane_key == pb)
            begin = pb * theta_lanes + tile_at * 128
            for ref, value in zip((high_ref, low_ref), values):
                for y in range(8):
                    ref[y * 64 : y * 64 + elements, begin : begin + 128] = jnp.where(
                        mine, value[:, y * 128 : (y + 1) * 128], 0.0
                    ).astype(bf16)


def exact_dot(value, choice):
    high, low = split(value)
    return dot(high, choice) + dot(low, choice)


def second_local_kernel(
    state_ref, base_ref, velocity_ref, neigh_ref, send_ref, yz, lift, extract, cross, *refs
):
    shared_refs, map_refs, (out_ref, added_ref) = refs[:-9], refs[-9:-6] + refs[-4:], refs[-6:-4]
    fill_maps(*map_refs)
    elements = neigh_ref.shape[1]
    table = shared_table(shared_refs, elements).astype(bf16)
    keys = remote_keys(elements)
    picked = pick_faces(column(neigh_ref), keys)
    terms = lift_rows(picked, table, lift[...], elements)
    first = rows_of(base_ref) + (time_step * penalty) * terms
    first_table = face_table(first + remainder(rows_of(state_ref)), extract[...])
    rate = local_rate(
        first, velocity_ref, neigh_ref, first_table, *split(yz[...]), lift[...]
    )
    second = 0.5 * (rows_of(state_ref) + first + time_step * rate)
    out_ref[...] = second.reshape(out_ref.shape)
    own = pick_rows(column(send_ref), local_key(elements))
    added_ref[:elements, :] = dot(own, first_table)
    names = jnp.concatenate([ref[-8:, :].T[:elements] for ref in shared_refs[1:]], axis=0)
    count = names.shape[0]
    pairs = facing_pairs(pick_faces(names, keys), table, count)
    face = names[:, 6:7]
    half = low_half((count, 128))
    same = half != ((face == 1) | (face == 3) | (face == 5))
    for c in range(FIELDS):
        faces = dot(pairs[c * count : (c + 1) * count], cross[...])
        added = jnp.where(face >= 2, faces[:, 128:256], faces[:, :128])
        added = jnp.where(face >= 4, faces[:, 256:], added)
        added = jnp.where(same, added, pltpu.roll(added, 64, 1))
        added_ref[elements:, c * 128 : (c + 1) * 128] = (time_step * penalty) * added


def exchange_plan(size):
    straight = [m for m in range(size // 2, 3 * size // 4) if m & 1]
    relayed = [m for m in range(size - 1, 1, -2) if m not in straight]
    return relayed, [m for m in range(size) if m not in relayed]


def sample_kernel(
    base_ref, neigh_ref, added_ref, lift, radial_ref, axial_ref, high_ref, low_ref, *refs
):
    sectors = high_ref.shape[1] // (PB * TB * 8)
    shares = lax.axis_size("ax") - 1
    shared_refs = refs[:shares]
    new_ref, out_refs = refs[shares], refs[shares + 1 : -2]
    turned_ref, parts_ref = refs[-2:]
    elements = neigh_ref.shape[1]
    added = added_ref[elements:, :] + shared_table(shared_refs, elements)
    table = jnp.concatenate([added_ref[:elements, :], added], axis=0).astype(bf16)
    picked = pick_faces(column(neigh_ref), remote_keys(elements))
    terms = lift_rows(picked, table, lift[...], elements)
    new_state = rows_of(base_ref) + (0.5 * time_step * penalty) * terms
    new_ref[...] = new_state.reshape(new_ref.shape)
    gap = jnp.zeros((64 - elements, 128), f32)
    for c in range(FIELDS):
        for j in range(4):
            part = new_state[c * elements : (c + 1) * elements, j * 128 : (j + 1) * 128]
            after = pltpu.roll(part, 120, 1)
            turned_ref[c, j] = jnp.concatenate([part, gap, after, gap], axis=0).T
    radial = radial_ref[...]
    axial = axial_ref[...]
    theta_lanes = high_ref.shape[1] // PB
    groups = sectors // PB
    rows = 64 // groups
    for pair in range(2):
        tiles = []
        for yy in (2 * pair, 2 * pair + 1):
            values = []
            for c in range(FIELDS):
                inputs = []
                for x in range(8):
                    start = (x % 2) * 64 + 16 * yy
                    value = axial[0:8, :] * turned_ref[c, x // 2, start : start + 1, :]
                    for z in range(1, 8):
                        row = turned_ref[c, x // 2, start + z : start + z + 1, :]
                        value = value + axial[8 * z : 8 * z + 8, :] * row
                    inputs.append(value)
                for r in range(8):
                    value = radial_ref[8 * r : 8 * r + 1, :] * inputs[0]
                    for x in range(1, 8):
                        value = value + radial_ref[8 * r + x : 8 * r + x + 1, :] * inputs[x]
                    values.append(value)
            tiles.append(jnp.concatenate(values, axis=0))
        mapped_high, mapped_low = split(jnp.concatenate(tiles, axis=1))
        depth = slice(256 * pair, 256 * pair + 256)
        weight_high = high_ref[depth, :]
        part = (
            dot(mapped_high, weight_high)
            + dot(mapped_low, weight_high)
            + dot(mapped_high, low_ref[depth, :])
        )
        total = part if pair == 0 else total + part
    for pb in range(PB):
        for g in range(groups):
            for c in range(FIELDS):
                start = c * 64 + g * rows
                parts_ref[pb * groups + g, c * rows : (c + 1) * rows, :] = total[
                    start : start + rows, pb * theta_lanes : (pb + 1) * theta_lanes
                ]
    owner = lax.axis_index("az")
    relayed, kept = exchange_plan(sectors)
    for i, m in enumerate(relayed):
        out_refs[0][i] = parts_ref[owner ^ m]
    for i, m in enumerate(kept):
        out_refs[1 + i][...] = parts_ref[owner ^ m]


def fourier_kernel(table_ref, *refs):
    out_ref = refs[-1]
    total = refs[0][...]
    for ref in refs[1:-1]:
        total = total + ref[...]
    high, low = split(total)
    weight, weight_low = split(table_ref[...])
    coeffs = dot(high, weight) + dot(low, weight) + dot(high, weight_low)
    width = total.shape[1]
    rows = total.shape[0] // FIELDS
    for k in range(2):
        for c in range(FIELDS):
            out_ref[k, c] = coeffs[c * rows : (c + 1) * rows, k * width : (k + 1) * width]


def join_kernel(got_ref, *refs):
    count = len(refs) // 2
    for i in range(count - 1):
        refs[count + i][...] = refs[i][...] + got_ref[i]
    refs[-1][...] = refs[count - 1][...]


def store_kernel(new_ref, out_ref, sem):
    copy = pltpu.make_async_copy(new_ref, out_ref, sem)
    copy.start()
    copy.wait()


def shape(dims, dtype=f32):
    return jax.ShapeDtypeStruct(dims, dtype)


def call(kernel, outs, *args, scratch=(), flops=0, in_space=pltpu.VMEM, out_space=pltpu.VMEM, aliases={}):
    size = sum(math.prod(a.shape) * a.dtype.itemsize for a in list(args) + list(outs))
    return pl.pallas_call(
        kernel,
        out_shape=outs,
        in_specs=[pl.BlockSpec(memory_space=in_space)] * len(args),
        out_specs=tuple([pl.BlockSpec(memory_space=out_space)] * len(outs)),
        scratch_shapes=list(scratch),
        input_output_aliases=aliases,
        cost_estimate=pl.CostEstimate(flops=flops, bytes_accessed=size, transcendentals=0),
        compiler_params=pltpu.CompilerParams(vmem_limit_bytes=48 * 1024 * 1024),
    )(*args)


def exchange(value, axis):
    size = lax.axis_size(axis)
    return [value] + [
        lax.ppermute(value, axis, [(i, i ^ m) for i in range(size)]) for m in range(size - 1, 0, -1)
    ][::-1]


def per_device(state, velocity, interp_maps, neighbours, send_faces, owner_device, owner_block):
    elements = state.shape[0]
    sectors = lax.axis_size("az")
    inputs = (
        state.transpose(1, 0, 2),
        send_faces.reshape(1, elements),
        velocity.T,
        neighbours.T,
        interp_maps.transpose(1, 2, 3, 0).reshape(3, 64, elements),
        owner_device.reshape(1, elements),
        owner_block.reshape(1, elements),
    )
    yz_table = jnp.asarray(tile_tables(), f32)
    face_rows = shape((6 * elements, FIELDS * 128), bf16)
    travel = FIELDS * elements // 2
    sources = inputs + (yz_table,)
    sources = tuple(pltpu.with_memory_space_constraint(a, pltpu.HBM) for a in sources)
    loaded = call(
        load_kernel,
        tuple(shape(a.shape, a.dtype) for a in sources)
        + (shape((512, 512), bf16), shape((256, 512), bf16), shape((384, 384), bf16))
        + (face_rows, shape((travel + 8, 128))),
        *sources,
        scratch=(pltpu.SemaphoreType.DMA((len(sources) - 1 + FIELDS,)),),
        flops=400_000_000,
        in_space=pltpu.HBM,
    )
    fields, sends, speed, names, maps, places, blocks, yz, extract, lift, cross, table, shared = loaded
    cube = shape(fields.shape)
    others = exchange(shared, "ax")
    base, shared = call(
        first_local_kernel, (cube, shape((travel, 128))),
        fields, speed, names, sends, table, yz, lift, extract,
        flops=1_000_000_000,
    )
    firsts = exchange(shared, "ax")
    lanes = sectors * TB * 8
    weights = shape((512, PB * lanes), bf16)
    base, added, radial, axial, weight_high, weight_low = call(
        second_local_kernel,
        (cube, shape((lax.axis_size("ax") * elements, FIELDS * 128)))
        + (shape((64, 128)), shape((64, 128)), weights, weights),
        fields, base, speed, names, sends, yz, lift, extract, cross, *others, maps, places, blocks,
        flops=1_500_000_000,
    )
    rows = FIELDS * 64 * PB // sectors
    piece = shape((rows, lanes))
    relayed, kept = exchange_plan(sectors)
    sampled = call(
        sample_kernel, (cube, shape((len(relayed), rows, lanes))) + (piece,) * len(kept),
        base, names, added, lift, radial, axial, weight_high, weight_low, *firsts[1:],
        scratch=(
            pltpu.VMEM((FIELDS, 4, 128, 128), f32),
            pltpu.VMEM((sectors, rows, lanes), f32),
        ),
        flops=800_000_000,
    )
    new_state, bundle, pieces = sampled[0], sampled[1], dict(zip(kept, sampled[2:]))
    stored = call(
        store_kernel, (cube,), new_state, scratch=(pltpu.SemaphoreType.DMA,), out_space=pltpu.HBM
    )[0]

    def swap(value, mask):
        return lax.ppermute(value, "az", [(i, i ^ mask) for i in range(sectors)])

    bundle = swap(bundle, 1)
    joined = [m - 1 for m in relayed] + [1]
    arrived = [swap(pieces[m], m) for m in kept if m and m not in joined]
    sums = call(join_kernel, (piece,) * len(joined), bundle, *[pieces[m] for m in joined])
    arrived += [swap(value, m) for m, value in zip(joined, sums)]
    arrived.append(pieces[0])
    angle = 2.0 * np.pi / lanes * (np.outer(np.arange(lanes), np.arange(lanes)) % lanes)
    table = np.concatenate([np.cos(angle), -np.sin(angle)], axis=1) * lanes**-0.5
    spectrum = call(
        fourier_kernel, (shape((2, FIELDS, rows // FIELDS, lanes)),),
        jnp.asarray(table, f32), *arrived,
        flops=100_000_000,
    )[0]
    return stored.transpose(1, 0, 2), spectrum


def solution(mesh):
    return jax.shard_map(
        per_device,
        mesh=mesh,
        in_specs=(
            P(("az", "ax"), None, None),
            P(("az", "ax"), None),
            P(("az", "ax"), None, None, None),
            P(("az", "ax"), None),
            P(("az", "ax")),
            P(("az", "ax"), None),
            P(("az", "ax")),
        ),
        out_specs=(P(("az", "ax"), None, None), P(None, None, ("az", "ax"), None)),
        check_vma=False,
    )
```

```python
import functools
import math

import jax
import jax.numpy as jnp
import numpy as np
from jax import lax
from jax.experimental import pallas as pl
from jax.experimental.pallas import tpu as pltpu
from jax.sharding import PartitionSpec as P

TB = 2
PB = 4
FIELDS = 5
time_step = 0.02
penalty = 5.0
highest = lax.Precision.HIGHEST
f32 = jnp.float32
bf16 = jnp.bfloat16


def spectral_derivative():
    points = np.cos(np.pi * np.arange(8) / 7.0)
    ends = (np.arange(8) == 0) | (np.arange(8) == 7)
    scales = np.where(ends, 2.0, 1.0)
    signs = np.where(np.arange(8) % 2 == 0, 1.0, -1.0)
    differ = points[:, None] - points[None, :]
    offdiag = (
        scales[:, None]
        / scales[None, :]
        * signs[:, None]
        * signs[None, :]
        / np.where(np.eye(8) > 0, 1.0, differ)
    )
    inner = -points / (2.0 * np.where(ends, 1.0, 1.0 - points * points))
    corner = (2.0 * 49.0 + 1.0) / 6.0
    diagonal = np.where(np.arange(8) == 0, corner, np.where(np.arange(8) == 7, -corner, inner))
    return np.where(np.eye(8) > 0, diagonal[:, None], offdiag)


def tile_tables():
    deriv = spectral_derivative()
    along_y = np.kron(np.eye(2), np.kron(deriv, np.eye(8))).T
    along_z = np.kron(np.eye(16), deriv).T
    return np.concatenate([along_y, along_z], axis=1)


def face_node(face, position):
    first, second = position >> 3, position & 7
    if face < 2:
        return 448 * face + position
    if face < 4:
        return 56 * (face - 2) + 64 * first + second
    return 7 * (face - 4) + 64 * first + 8 * second


def iota(dims, axis):
    return lax.broadcasted_iota(jnp.int32, dims, axis)


def face_counts():
    node = iota((1, 512), 1)
    count = jnp.zeros((1, 512), f32)
    for coordinate in (node >> 6, (node >> 3) & 7, node & 7):
        count = count + jnp.where((coordinate == 0) | (coordinate == 7), 1.0, 0.0)
    return count


def split(value):
    high = value.astype(bf16)
    return high, (value - high.astype(f32)).astype(bf16)


def remainder(value):
    return value - value.astype(bf16).astype(f32)


def dot(a, b):
    return jnp.dot(a, b, preferred_element_type=f32)


def low_half(shape):
    return lax.broadcasted_iota(jnp.int32, shape, len(shape) - 1) < 64


def local_key(elements):
    lane = lax.broadcasted_iota(jnp.int32, (1, 6 * elements), 1)
    face = jnp.zeros_like(lane)
    for f in range(1, 6):
        face = face + (lane >= f * elements).astype(jnp.int32)
    return 6 * (lane - face * elements) + face


def column(row_ref):
    return row_ref[...].astype(f32).T


def pick_rows(names, keys):
    return jnp.where(names == keys.astype(f32), 1.0, 0.0).astype(bf16)


def face_table(fields, extract):
    elements = fields.shape[0] // FIELDS
    faces = dot(fields.astype(bf16), extract).astype(bf16)
    half = low_half((fields.shape[0], 128))
    ends = [fields[:, :128], fields[:, 384:]]
    turned = [pltpu.roll(end, 64, 1) for end in ends]
    ends = [jnp.where(half, ends[0], turned[0]), jnp.where(half, turned[1], ends[1])]
    blocks = [end.astype(bf16) for end in ends] + [
        faces[:, f * 128 : (f + 1) * 128] for f in range(4)
    ]
    rows = [
        jnp.concatenate(
            [block[c * elements : (c + 1) * elements] for c in range(FIELDS)], axis=1
        )
        for block in blocks
    ]
    return jnp.concatenate(rows, axis=0)


def share_rows(table, picked, out_ref):
    elements = picked.shape[0]
    rows = dot(picked, table)
    field = [rows[:, c * 128 : (c + 1) * 128] for c in range(FIELDS)]
    half = low_half((elements, 128))
    out_ref[0:elements, :] = jnp.where(half, field[0], field[1])
    out_ref[elements : 2 * elements, :] = jnp.where(half, field[2], field[3])
    middle = elements // 2
    out_ref[2 * elements : 2 * elements + middle, :] = jnp.where(
        half[:middle], field[4][:middle], field[4][middle:]
    )


def unpack_rows(ref, elements):
    half = low_half((elements, 128))
    middle = elements // 2
    fields = []
    for first in range(2):
        both = ref[first * elements : (first + 1) * elements, :]
        turned = pltpu.roll(both, 64, 1)
        fields.append(jnp.where(half, both, turned))
        fields.append(jnp.where(half, turned, both))
    both = ref[2 * elements : 2 * elements + middle, :]
    turned = pltpu.roll(both, 64, 1)
    fields.append(
        jnp.concatenate(
            [jnp.where(half[:middle], both, turned), jnp.where(half[:middle], turned, both)],
            axis=0,
        )
    )
    return jnp.concatenate(fields, axis=1)


def share_names(names_ref, send_ref, out_ref):
    elements = send_ref.shape[1]
    sends = send_ref[...].astype(f32)
    element = jnp.floor((sends + 0.5) * (1.0 / 6.0))
    chosen = (iota((elements, elements), 0).astype(f32) == element).astype(f32).astype(bf16)
    names = jnp.concatenate([names_ref[...].astype(f32), jnp.zeros((2, elements), f32)], axis=0)
    out_ref[-8:, :] = jnp.zeros((8, 128), f32)
    out_ref[-8:, :elements] = exact_dot(names, chosen)
    out_ref[-2:-1, :elements] = sends - 6.0 * element


def facing_pairs(picked, table, elements):
    half = low_half((elements, 128))
    facing = dot(picked, table)
    field_rows = []
    for c in range(FIELDS):
        blocks = [
            facing[f * elements : (f + 1) * elements, c * 128 : (c + 1) * 128] for f in range(6)
        ]
        pairs = [jnp.where(half, blocks[f], blocks[f + 1]) for f in range(0, 6, 2)]
        field_rows.append(jnp.concatenate(pairs, axis=1))
    return jnp.concatenate(field_rows, axis=0).astype(bf16)


def lift_rows(picked, table, lift, elements):
    half = low_half((elements, 128))
    facing = dot(picked, table)
    ends, inner = [], []
    for c in range(FIELDS):
        blocks = [
            facing[f * elements : (f + 1) * elements, c * 128 : (c + 1) * 128] for f in range(6)
        ]
        ends.append((jnp.where(half, blocks[0], 0.0), jnp.where(half, 0.0, blocks[1])))
        pairs = [jnp.where(half, blocks[f], blocks[f + 1]) for f in (2, 4)]
        inner.append(jnp.concatenate(pairs, axis=1))
    lifted = dot(jnp.concatenate(inner, axis=0).astype(bf16), lift)
    rows = []
    for c in range(FIELDS):
        part = lifted[c * elements : (c + 1) * elements]
        rows.append(
            jnp.concatenate(
                [part[:, :128] + ends[c][0], part[:, 128:384], part[:, 384:] + ends[c][1]], axis=1
            )
        )
    return jnp.concatenate(rows, axis=0)


def x_derivative(fields):
    deriv = spectral_derivative()
    half = low_half((1, 128))
    tiles = [fields[:, 128 * i : 128 * i + 128] for i in range(4)]
    turned = [pltpu.roll(tile, 64, 1) for tile in tiles]
    out = []
    for j in range(4):
        total = None
        for i in range(4):
            same = jnp.where(half, float(deriv[2 * j, 2 * i]), float(deriv[2 * j + 1, 2 * i + 1]))
            cross = jnp.where(half, float(deriv[2 * j, 2 * i + 1]), float(deriv[2 * j + 1, 2 * i]))
            part = same * tiles[i] + cross * turned[i]
            total = part if total is None else total + part
        out.append(total)
    return out


def local_rate(fields, velocity_ref, neigh_ref, table, yz_high, yz_low, lift):
    elements = neigh_ref.shape[1]
    high, low = split(fields)
    speed = velocity_ref[...].T
    speeds = [jnp.broadcast_to(speed[:, d : d + 1], (elements, 128)) for d in range(3)]
    yz_twice = jnp.concatenate([yz_high, yz_high], axis=0)
    both = []
    for j in range(4):
        lanes = slice(j * 128, (j + 1) * 128)
        parts = jnp.concatenate([high[:, lanes], low[:, lanes]], axis=1)
        both.append(dot(parts, yz_twice) + dot(high[:, lanes], yz_low))
    chunk = elements // 2
    rows = []
    for c in range(FIELDS):
        for part in range(2):
            begin = c * elements + part * chunk
            along_x = x_derivative(fields[begin : begin + chunk])
            here = [speed_rows[part * chunk : (part + 1) * chunk] for speed_rows in speeds]
            tiles = [
                here[0] * along_x[j]
                + here[1] * both[j][begin : begin + chunk, :128]
                + here[2] * both[j][begin : begin + chunk, 128:]
                for j in range(4)
            ]
            rows.append(jnp.concatenate(tiles, axis=1))
    picked = pick_faces(column(neigh_ref), local_key(elements))
    lifted = lift_rows(picked, table, lift, elements)
    return penalty * (lifted - face_counts() * fields) - jnp.concatenate(rows, axis=0)


def pick_faces(names, keys):
    return jnp.concatenate([pick_rows(names[:, f : f + 1], keys) for f in range(6)], axis=0)


def remote_keys(elements):
    me = lax.axis_index("ax")
    lane = iota((1, elements), 1)
    return jnp.concatenate(
        [6 * elements + (me ^ m) * elements + lane for m in range(lax.axis_size("ax"))], axis=1
    )


def shared_table(refs, elements):
    return jnp.concatenate([unpack_rows(ref, elements) for ref in refs], axis=0)


def rows_of(ref):
    fields, elements, nodes = ref.shape
    return ref[...].reshape(fields * elements, nodes)


def load_kernel(*refs):
    count = 8
    sources, loaded = refs[:count], refs[count : 2 * count]
    extract_ref, lift_ref, cross_ref, table_ref, shared_ref, sems = refs[2 * count :]
    pairs = list(zip(sources, loaded))
    fields = [(pairs[0][0].at[c], pairs[0][1].at[c]) for c in range(FIELDS)]
    copies = [
        pltpu.make_async_copy(source, target, sems.at[i])
        for i, (source, target) in enumerate(pairs[1:2] + pairs[3:4] + fields + pairs[2:3] + pairs[4:])
    ]
    for copy in copies:
        copy.start()
    row, lane = iota((512, 128), 0), iota((512, 128), 1)
    for f in range(4):
        here = row == face_node(f + 2, lane & 63)
        extract_ref[:, f * 128 : (f + 1) * 128] = jnp.where(here, 1.0, 0.0).astype(bf16)
    for copy in copies[:2]:
        copy.wait()
    picked = pick_rows(column(loaded[1]), local_key(loaded[1].shape[1]))
    share_names(loaded[3], loaded[1], shared_ref)
    row, lane = iota((64, 512), 0), iota((64, 512), 1)
    for f in range(4):
        here = face_node(f + 2, row) == lane
        lift_ref[f * 64 : (f + 1) * 64, :] = jnp.where(here, 1.0, 0.0).astype(bf16)
    row, lane = iota((64, 128), 0), iota((64, 128), 1)
    for f in range(6):
        for g in range(0, 6, 2):
            node = jnp.where(lane < 64, face_node(g, lane & 63), face_node(g + 1, lane & 63))
            cross_ref[f * 64 : (f + 1) * 64, g * 64 : (g + 2) * 64] = jnp.where(
                face_node(f, row) == node, 1.0, 0.0
            ).astype(bf16)
    for copy in copies[2 : 2 + FIELDS]:
        copy.wait()
    table = face_table(rows_of(loaded[0]), extract_ref[...])
    table_ref[...] = table
    share_rows(table, picked, shared_ref)
    for copy in copies[2 + FIELDS :]:
        copy.wait()


def first_local_kernel(
    state_ref, velocity_ref, neigh_ref, send_ref, table_ref, yz, lift, extract, out_ref, shared_ref
):
    fields = rows_of(state_ref)
    rate = local_rate(
        fields, velocity_ref, neigh_ref, table_ref[...], *split(yz[...]), lift[...]
    )
    base = fields + time_step * rate
    out_ref[...] = base.reshape(out_ref.shape)
    picked = pick_rows(column(send_ref), local_key(send_ref.shape[1]))
    share_rows(face_table(base + remainder(fields), extract[...]), picked, shared_ref)


def fill_maps(
    maps_ref, device_ref, block_ref, radial_ref, axial_ref, high_ref, low_ref
):
    elements = maps_ref.shape[2]
    row, lane = iota((elements, 128), 0), iota((elements, 128), 1)
    twice = ((lane & 63) == row).astype(f32).astype(bf16)
    radial_ref[...] = exact_dot(maps_ref[1], twice)
    swap = ((iota((64, 64), 0) >> 3) + 8 * (iota((64, 64), 0) & 7) == iota((64, 64), 1)).astype(f32)
    axial = [dot(swap.astype(bf16), part).astype(bf16) for part in split(maps_ref[2])]
    axial_ref[...] = dot(axial[0], twice) + dot(axial[1], twice)
    tile_row, tile_lane = iota((64, 1024), 0), iota((64, 1024), 1)
    tile = ((tile_row >> 3) == (tile_lane & 7)) & ((tile_row & 7) == (tile_lane >> 7))
    tile = jnp.where(tile, 1.0, 0.0).astype(bf16)
    values = [dot(part, tile) for part in split(maps_ref[0].T)]
    places = device_ref[...].astype(f32).T
    blocks = block_ref[...].astype(f32).T
    theta_lanes = high_ref.shape[1] // PB
    upper = (blocks >= PB).astype(f32)
    sector_key = places * TB + upper
    plane_key = blocks - PB * upper
    gap = jnp.zeros((64 - elements, high_ref.shape[1]), bf16)
    for y in range(8):
        start = y * 64
        high_ref[start + elements : start + 64, :] = gap
        low_ref[start + elements : start + 64, :] = gap
    for pb in range(PB):
        for tile_at in range(theta_lanes // 128):
            here = ((lane + tile_at * 128) >> 3).astype(f32)
            mine = (sector_key == here) & (plane_key == pb)
            begin = pb * theta_lanes + tile_at * 128
            for ref, value in zip((high_ref, low_ref), values):
                for y in range(8):
                    ref[y * 64 : y * 64 + elements, begin : begin + 128] = jnp.where(
                        mine, value[:, y * 128 : (y + 1) * 128], 0.0
                    ).astype(bf16)


def exact_dot(value, choice):
    high, low = split(value)
    return dot(high, choice) + dot(low, choice)


def second_local_kernel(
    state_ref, base_ref, velocity_ref, neigh_ref, send_ref, yz, lift, extract, cross, *refs
):
    shared_refs, map_refs = refs[:-10], refs[-10:-7] + refs[-4:]
    out_ref, added_ref, picked_ref = refs[-7:-4]
    fill_maps(*map_refs)
    elements = neigh_ref.shape[1]
    table = shared_table(shared_refs, elements).astype(bf16)
    keys = remote_keys(elements)
    picked = pick_faces(column(neigh_ref), keys)
    picked_ref[...] = picked
    terms = lift_rows(picked, table, lift[...], elements)
    first = rows_of(base_ref) + (time_step * penalty) * terms
    first_table = face_table(first + remainder(rows_of(state_ref)), extract[...])
    rate = local_rate(
        first, velocity_ref, neigh_ref, first_table, *split(yz[...]), lift[...]
    )
    second = 0.5 * (rows_of(state_ref) + first + time_step * rate)
    out_ref[...] = second.reshape(out_ref.shape)
    own = pick_rows(column(send_ref), local_key(elements))
    added_ref[:elements, :] = dot(own, first_table)
    names = jnp.concatenate([ref[-8:, :].T[:elements] for ref in shared_refs[1:]], axis=0)
    count = names.shape[0]
    pairs = facing_pairs(pick_faces(names, keys), table, count)
    face = names[:, 6:7]
    half = low_half((count, 128))
    same = half != ((face == 1) | (face == 3) | (face == 5))
    for c in range(FIELDS):
        faces = dot(pairs[c * count : (c + 1) * count], cross[...])
        added = jnp.where(face >= 2, faces[:, 128:256], faces[:, :128])
        added = jnp.where(face >= 4, faces[:, 256:], added)
        added = jnp.where(same, added, pltpu.roll(added, 64, 1))
        added_ref[elements:, c * 128 : (c + 1) * 128] = (time_step * penalty) * added


def exchange_plan(size):
    straight = [m for m in range(size // 2, 3 * size // 4) if m & 1]
    relayed = [m for m in range(size - 1, 1, -2) if m not in straight]
    return relayed, [m for m in range(size) if m not in relayed]


def sample_kernel(
    base_ref, picked_ref, added_ref, lift, radial_ref, axial_ref, high_ref, low_ref, *refs
):
    sectors = high_ref.shape[1] // (PB * TB * 8)
    shares = lax.axis_size("ax") - 1
    shared_refs = refs[:shares]
    new_ref, out_refs = refs[shares], refs[shares + 1 : -2]
    turned_ref, parts_ref = refs[-2:]
    elements = base_ref.shape[1]
    added = added_ref[elements:, :] + shared_table(shared_refs, elements)
    table = jnp.concatenate([added_ref[:elements, :], added], axis=0).astype(bf16)
    terms = lift_rows(picked_ref[...], table, lift[...], elements)
    new_state = rows_of(base_ref) + (0.5 * time_step * penalty) * terms
    new_ref[...] = new_state.reshape(new_ref.shape)
    gap = jnp.zeros((64 - elements, 128), f32)
    for c in range(FIELDS):
        for j in range(4):
            part = new_state[c * elements : (c + 1) * elements, j * 128 : (j + 1) * 128]
            after = pltpu.roll(part, 120, 1)
            turned_ref[c, j] = jnp.concatenate([part, gap, after, gap], axis=0).T
    radial = radial_ref[...]
    axial = axial_ref[...]
    theta_lanes = high_ref.shape[1] // PB
    groups = sectors // PB
    rows = 64 // groups
    for pair in range(2):
        tiles = []
        for yy in (2 * pair, 2 * pair + 1):
            values = []
            for c in range(FIELDS):
                inputs = []
                for x in range(8):
                    start = (x % 2) * 64 + 16 * yy
                    value = axial[0:8, :] * turned_ref[c, x // 2, start : start + 1, :]
                    for z in range(1, 8):
                        row = turned_ref[c, x // 2, start + z : start + z + 1, :]
                        value = value + axial[8 * z : 8 * z + 8, :] * row
                    inputs.append(value)
                for r in range(8):
                    value = radial_ref[8 * r : 8 * r + 1, :] * inputs[0]
                    for x in range(1, 8):
                        value = value + radial_ref[8 * r + x : 8 * r + x + 1, :] * inputs[x]
                    values.append(value)
            tiles.append(jnp.concatenate(values, axis=0))
        mapped_high, mapped_low = split(jnp.concatenate(tiles, axis=1))
        depth = slice(256 * pair, 256 * pair + 256)
        weight_high = high_ref[depth, :]
        part = (
            dot(mapped_high, weight_high)
            + dot(mapped_low, weight_high)
            + dot(mapped_high, low_ref[depth, :])
        )
        total = part if pair == 0 else total + part
    for pb in range(PB):
        for g in range(groups):
            for c in range(FIELDS):
                start = c * 64 + g * rows
                parts_ref[pb * groups + g, c * rows : (c + 1) * rows, :] = total[
                    start : start + rows, pb * theta_lanes : (pb + 1) * theta_lanes
                ]
    owner = lax.axis_index("az")
    relayed, kept = exchange_plan(sectors)
    for i, m in enumerate(relayed):
        out_refs[0][i] = parts_ref[owner ^ m]
    for i, m in enumerate(kept):
        out_refs[1 + i][...] = parts_ref[owner ^ m]


def fourier_kernel(table_ref, *refs):
    out_ref = refs[-1]
    total = refs[0][...]
    for ref in refs[1:-1]:
        total = total + ref[...]
    high, low = split(total)
    weight, weight_low = split(table_ref[...])
    coeffs = dot(high, weight) + dot(low, weight) + dot(high, weight_low)
    width = total.shape[1]
    rows = total.shape[0] // FIELDS
    for k in range(2):
        for c in range(FIELDS):
            out_ref[k, c] = coeffs[c * rows : (c + 1) * rows, k * width : (k + 1) * width]


def join_kernel(got_ref, *refs):
    count = len(refs) // 2
    for i in range(count - 1):
        refs[count + i][...] = refs[i][...] + got_ref[i]
    refs[-1][...] = refs[count - 1][...]


def store_kernel(new_ref, out_ref, sem):
    copy = pltpu.make_async_copy(new_ref, out_ref, sem)
    copy.start()
    copy.wait()


def shape(dims, dtype=f32):
    return jax.ShapeDtypeStruct(dims, dtype)


def call(kernel, outs, *args, scratch=(), flops=0, in_space=pltpu.VMEM, out_space=pltpu.VMEM, aliases={}):
    size = sum(math.prod(a.shape) * a.dtype.itemsize for a in list(args) + list(outs))
    return pl.pallas_call(
        kernel,
        out_shape=outs,
        in_specs=[pl.BlockSpec(memory_space=in_space)] * len(args),
        out_specs=tuple([pl.BlockSpec(memory_space=out_space)] * len(outs)),
        scratch_shapes=list(scratch),
        input_output_aliases=aliases,
        cost_estimate=pl.CostEstimate(flops=flops, bytes_accessed=size, transcendentals=0),
        compiler_params=pltpu.CompilerParams(vmem_limit_bytes=48 * 1024 * 1024),
    )(*args)


def exchange(value, axis):
    size = lax.axis_size(axis)
    return [value] + [
        lax.ppermute(value, axis, [(i, i ^ m) for i in range(size)]) for m in range(size - 1, 0, -1)
    ][::-1]


def per_device(state, velocity, interp_maps, neighbours, send_faces, owner_device, owner_block):
    elements = state.shape[0]
    sectors = lax.axis_size("az")
    inputs = (
        state.transpose(1, 0, 2),
        send_faces.reshape(1, elements),
        velocity.T,
        neighbours.T,
        interp_maps.transpose(1, 2, 3, 0).reshape(3, 64, elements),
        owner_device.reshape(1, elements),
        owner_block.reshape(1, elements),
    )
    yz_table = jnp.asarray(tile_tables(), f32)
    face_rows = shape((6 * elements, FIELDS * 128), bf16)
    travel = FIELDS * elements // 2
    sources = inputs + (yz_table,)
    sources = tuple(pltpu.with_memory_space_constraint(a, pltpu.HBM) for a in sources)
    loaded = call(
        load_kernel,
        tuple(shape(a.shape, a.dtype) for a in sources)
        + (shape((512, 512), bf16), shape((256, 512), bf16), shape((384, 384), bf16))
        + (face_rows, shape((travel + 8, 128))),
        *sources,
        scratch=(pltpu.SemaphoreType.DMA((len(sources) - 1 + FIELDS,)),),
        flops=400_000_000,
        in_space=pltpu.HBM,
    )
    fields, sends, speed, names, maps, places, blocks, yz, extract, lift, cross, table, shared = loaded
    cube = shape(fields.shape)
    others = exchange(shared, "ax")
    base, shared = call(
        first_local_kernel, (cube, shape((travel, 128))),
        fields, speed, names, sends, table, yz, lift, extract,
        flops=1_000_000_000,
    )
    firsts = exchange(shared, "ax")
    lanes = sectors * TB * 8
    weights = shape((512, PB * lanes), bf16)
    base, added, picked, radial, axial, weight_high, weight_low = call(
        second_local_kernel,
        (cube, shape((lax.axis_size("ax") * elements, FIELDS * 128)))
        + (shape((6 * elements, lax.axis_size("ax") * elements), bf16), shape((64, 128)), shape((64, 128)), weights, weights),
        fields, base, speed, names, sends, yz, lift, extract, cross, *others, maps, places, blocks,
        flops=1_500_000_000,
    )
    rows = FIELDS * 64 * PB // sectors
    piece = shape((rows, lanes))
    relayed, kept = exchange_plan(sectors)
    sampled = call(
        sample_kernel, (cube, shape((len(relayed), rows, lanes))) + (piece,) * len(kept),
        base, picked, added, lift, radial, axial, weight_high, weight_low, *firsts[1:],
        scratch=(
            pltpu.VMEM((FIELDS, 4, 128, 128), f32),
            pltpu.VMEM((sectors, rows, lanes), f32),
        ),
        flops=800_000_000,
    )
    new_state, bundle, pieces = sampled[0], sampled[1], dict(zip(kept, sampled[2:]))
    stored = call(
        store_kernel, (cube,), new_state, scratch=(pltpu.SemaphoreType.DMA,), out_space=pltpu.HBM
    )[0]

    def swap(value, mask):
        return lax.ppermute(value, "az", [(i, i ^ mask) for i in range(sectors)])

    bundle = swap(bundle, 1)
    joined = [m - 1 for m in relayed] + [1]
    arrived = [swap(pieces[m], m) for m in kept if m and m not in joined]
    sums = call(join_kernel, (piece,) * len(joined), bundle, *[pieces[m] for m in joined])
    arrived += [swap(value, m) for m, value in zip(joined, sums)]
    arrived.append(pieces[0])
    angle = 2.0 * np.pi / lanes * (np.outer(np.arange(lanes), np.arange(lanes)) % lanes)
    table = np.concatenate([np.cos(angle), -np.sin(angle)], axis=1) * lanes**-0.5
    spectrum = call(
        fourier_kernel, (shape((2, FIELDS, rows // FIELDS, lanes)),),
        jnp.asarray(table, f32), *arrived,
        flops=100_000_000,
    )[0]
    return stored.transpose(1, 0, 2), spectrum


def solution(mesh):
    return jax.shard_map(
        per_device,
        mesh=mesh,
        in_specs=(
            P(("az", "ax"), None, None),
            P(("az", "ax"), None),
            P(("az", "ax"), None, None, None),
            P(("az", "ax"), None),
            P(("az", "ax")),
            P(("az", "ax"), None),
            P(("az", "ax")),
        ),
        out_specs=(P(("az", "ax"), None, None), P(None, None, ("az", "ax"), None)),
        check_vma=False,
    )
```

```python
import functools
import math

import jax
import jax.numpy as jnp
import numpy as np
from jax import lax
from jax.experimental import pallas as pl
from jax.experimental.pallas import tpu as pltpu
from jax.sharding import PartitionSpec as P

TB = 2
PB = 4
FIELDS = 5
time_step = 0.02
penalty = 5.0
highest = lax.Precision.HIGHEST
f32 = jnp.float32
bf16 = jnp.bfloat16


def spectral_derivative():
    points = np.cos(np.pi * np.arange(8) / 7.0)
    ends = (np.arange(8) == 0) | (np.arange(8) == 7)
    scales = np.where(ends, 2.0, 1.0)
    signs = np.where(np.arange(8) % 2 == 0, 1.0, -1.0)
    differ = points[:, None] - points[None, :]
    offdiag = (
        scales[:, None]
        / scales[None, :]
        * signs[:, None]
        * signs[None, :]
        / np.where(np.eye(8) > 0, 1.0, differ)
    )
    inner = -points / (2.0 * np.where(ends, 1.0, 1.0 - points * points))
    corner = (2.0 * 49.0 + 1.0) / 6.0
    diagonal = np.where(np.arange(8) == 0, corner, np.where(np.arange(8) == 7, -corner, inner))
    return np.where(np.eye(8) > 0, diagonal[:, None], offdiag)


def tile_tables():
    deriv = spectral_derivative()
    along_y = np.kron(np.eye(2), np.kron(deriv, np.eye(8))).T
    along_z = np.kron(np.eye(16), deriv).T
    return np.concatenate([along_y, along_z], axis=1)


def face_node(face, position):
    first, second = position >> 3, position & 7
    if face < 2:
        return 448 * face + position
    if face < 4:
        return 56 * (face - 2) + 64 * first + second
    return 7 * (face - 4) + 64 * first + 8 * second


def iota(dims, axis):
    return lax.broadcasted_iota(jnp.int32, dims, axis)


def face_counts():
    node = iota((1, 512), 1)
    count = jnp.zeros((1, 512), f32)
    for coordinate in (node >> 6, (node >> 3) & 7, node & 7):
        count = count + jnp.where((coordinate == 0) | (coordinate == 7), 1.0, 0.0)
    return count


def split(value):
    high = value.astype(bf16)
    return high, (value - high.astype(f32)).astype(bf16)


def remainder(value):
    return value - value.astype(bf16).astype(f32)


def dot(a, b):
    return jnp.dot(a, b, preferred_element_type=f32)


def low_half(shape):
    return lax.broadcasted_iota(jnp.int32, shape, len(shape) - 1) < 64


def local_key(elements):
    lane = lax.broadcasted_iota(jnp.int32, (1, 6 * elements), 1)
    face = jnp.zeros_like(lane)
    for f in range(1, 6):
        face = face + (lane >= f * elements).astype(jnp.int32)
    return 6 * (lane - face * elements) + face


def column(row_ref):
    return row_ref[...].astype(f32).T


def pick_rows(names, keys):
    return jnp.where(names == keys.astype(f32), 1.0, 0.0).astype(bf16)


def face_table(fields, extract):
    elements = fields.shape[0] // FIELDS
    faces = dot(fields.astype(bf16), extract).astype(bf16)
    half = low_half((fields.shape[0], 128))
    ends = [fields[:, :128], fields[:, 384:]]
    turned = [pltpu.roll(end, 64, 1) for end in ends]
    ends = [jnp.where(half, ends[0], turned[0]), jnp.where(half, turned[1], ends[1])]
    blocks = [end.astype(bf16) for end in ends] + [
        faces[:, f * 128 : (f + 1) * 128] for f in range(4)
    ]
    rows = [
        jnp.concatenate(
            [block[c * elements : (c + 1) * elements] for c in range(FIELDS)], axis=1
        )
        for block in blocks
    ]
    return jnp.concatenate(rows, axis=0)


def share_rows(table, picked, out_ref):
    elements = picked.shape[0]
    rows = dot(picked, table)
    field = [rows[:, c * 128 : (c + 1) * 128] for c in range(FIELDS)]
    half = low_half((elements, 128))
    out_ref[0:elements, :] = jnp.where(half, field[0], field[1])
    out_ref[elements : 2 * elements, :] = jnp.where(half, field[2], field[3])
    middle = elements // 2
    out_ref[2 * elements : 2 * elements + middle, :] = jnp.where(
        half[:middle], field[4][:middle], field[4][middle:]
    )


def unpack_rows(ref, elements):
    half = low_half((elements, 128))
    middle = elements // 2
    fields = []
    for first in range(2):
        both = ref[first * elements : (first + 1) * elements, :]
        turned = pltpu.roll(both, 64, 1)
        fields.append(jnp.where(half, both, turned))
        fields.append(jnp.where(half, turned, both))
    both = ref[2 * elements : 2 * elements + middle, :]
    turned = pltpu.roll(both, 64, 1)
    fields.append(
        jnp.concatenate(
            [jnp.where(half[:middle], both, turned), jnp.where(half[:middle], turned, both)],
            axis=0,
        )
    )
    return jnp.concatenate(fields, axis=1)


def share_names(names_ref, send_ref, out_ref):
    elements = send_ref.shape[1]
    sends = send_ref[...].astype(f32)
    element = jnp.floor((sends + 0.5) * (1.0 / 6.0))
    chosen = (iota((elements, elements), 0).astype(f32) == element).astype(f32).astype(bf16)
    names = jnp.concatenate([names_ref[...].astype(f32), jnp.zeros((2, elements), f32)], axis=0)
    out_ref[-8:, :] = jnp.zeros((8, 128), f32)
    out_ref[-8:, :elements] = exact_dot(names, chosen)
    out_ref[-2:-1, :elements] = sends - 6.0 * element


def facing_pairs(picked, table, elements):
    half = low_half((elements, 128))
    facing = dot(picked, table)
    field_rows = []
    for c in range(FIELDS):
        blocks = [
            facing[f * elements : (f + 1) * elements, c * 128 : (c + 1) * 128] for f in range(6)
        ]
        pairs = [jnp.where(half, blocks[f], blocks[f + 1]) for f in range(0, 6, 2)]
        field_rows.append(jnp.concatenate(pairs, axis=1))
    return jnp.concatenate(field_rows, axis=0).astype(bf16)


def lift_rows(picked, table, lift, elements):
    half = low_half((elements, 128))
    facing = dot(picked, table)
    ends, inner = [], []
    for c in range(FIELDS):
        blocks = [
            facing[f * elements : (f + 1) * elements, c * 128 : (c + 1) * 128] for f in range(6)
        ]
        ends.append((jnp.where(half, blocks[0], 0.0), jnp.where(half, 0.0, blocks[1])))
        pairs = [jnp.where(half, blocks[f], blocks[f + 1]) for f in (2, 4)]
        inner.append(jnp.concatenate(pairs, axis=1))
    lifted = dot(jnp.concatenate(inner, axis=0).astype(bf16), lift)
    rows = []
    for c in range(FIELDS):
        part = lifted[c * elements : (c + 1) * elements]
        rows.append(
            jnp.concatenate(
                [part[:, :128] + ends[c][0], part[:, 128:384], part[:, 384:] + ends[c][1]], axis=1
            )
        )
    return jnp.concatenate(rows, axis=0)


def x_derivative(fields):
    deriv = spectral_derivative()
    half = low_half((1, 128))
    tiles = [fields[:, 128 * i : 128 * i + 128] for i in range(4)]
    turned = [pltpu.roll(tile, 64, 1) for tile in tiles]
    out = []
    for j in range(4):
        total = None
        for i in range(4):
            same = jnp.where(half, float(deriv[2 * j, 2 * i]), float(deriv[2 * j + 1, 2 * i + 1]))
            cross = jnp.where(half, float(deriv[2 * j, 2 * i + 1]), float(deriv[2 * j + 1, 2 * i]))
            part = same * tiles[i] + cross * turned[i]
            total = part if total is None else total + part
        out.append(total)
    return out


def local_rate(fields, velocity_ref, neigh_ref, table, yz_high, yz_low, lift):
    elements = neigh_ref.shape[1]
    high, low = split(fields)
    speed = velocity_ref[...].T
    speeds = [jnp.broadcast_to(speed[:, d : d + 1], (elements, 128)) for d in range(3)]
    yz_twice = jnp.concatenate([yz_high, yz_high], axis=0)
    both = []
    for j in range(4):
        lanes = slice(j * 128, (j + 1) * 128)
        parts = jnp.concatenate([high[:, lanes], low[:, lanes]], axis=1)
        both.append(dot(parts, yz_twice) + dot(high[:, lanes], yz_low))
    chunk = elements // 2
    rows = []
    for c in range(FIELDS):
        for part in range(2):
            begin = c * elements + part * chunk
            along_x = x_derivative(fields[begin : begin + chunk])
            here = [speed_rows[part * chunk : (part + 1) * chunk] for speed_rows in speeds]
            tiles = [
                here[0] * along_x[j]
                + here[1] * both[j][begin : begin + chunk, :128]
                + here[2] * both[j][begin : begin + chunk, 128:]
                for j in range(4)
            ]
            rows.append(jnp.concatenate(tiles, axis=1))
    picked = pick_faces(column(neigh_ref), local_key(elements))
    lifted = lift_rows(picked, table, lift, elements)
    return penalty * (lifted - face_counts() * fields) - jnp.concatenate(rows, axis=0)


def pick_faces(names, keys):
    return jnp.concatenate([pick_rows(names[:, f : f + 1], keys) for f in range(6)], axis=0)


def remote_keys(elements):
    me = lax.axis_index("ax")
    lane = iota((1, elements), 1)
    return jnp.concatenate(
        [6 * elements + (me ^ m) * elements + lane for m in range(lax.axis_size("ax"))], axis=1
    )


def shared_table(refs, elements):
    return jnp.concatenate([unpack_rows(ref, elements) for ref in refs], axis=0)


def rows_of(ref):
    fields, elements, nodes = ref.shape
    return ref[...].reshape(fields * elements, nodes)


def load_kernel(*refs):
    count = 8
    sources, loaded = refs[:count], refs[count : 2 * count]
    extract_ref, lift_ref, cross_ref, table_ref, shared_ref, sems = refs[2 * count :]
    pairs = list(zip(sources, loaded))
    fields = [(pairs[0][0].at[c], pairs[0][1].at[c]) for c in range(FIELDS)]
    copies = [
        pltpu.make_async_copy(source, target, sems.at[i])
        for i, (source, target) in enumerate(pairs[1:2] + pairs[3:4] + fields + pairs[2:3] + pairs[4:])
    ]
    for copy in copies:
        copy.start()
    row, lane = iota((512, 128), 0), iota((512, 128), 1)
    for f in range(4):
        here = row == face_node(f + 2, lane & 63)
        extract_ref[:, f * 128 : (f + 1) * 128] = jnp.where(here, 1.0, 0.0).astype(bf16)
    for copy in copies[:2]:
        copy.wait()
    picked = pick_rows(column(loaded[1]), local_key(loaded[1].shape[1]))
    share_names(loaded[3], loaded[1], shared_ref)
    row, lane = iota((64, 512), 0), iota((64, 512), 1)
    for f in range(4):
        here = face_node(f + 2, row) == lane
        lift_ref[f * 64 : (f + 1) * 64, :] = jnp.where(here, 1.0, 0.0).astype(bf16)
    row, lane = iota((64, 128), 0), iota((64, 128), 1)
    for f in range(6):
        for g in range(0, 6, 2):
            node = jnp.where(lane < 64, face_node(g, lane & 63), face_node(g + 1, lane & 63))
            cross_ref[f * 64 : (f + 1) * 64, g * 64 : (g + 2) * 64] = jnp.where(
                face_node(f, row) == node, 1.0, 0.0
            ).astype(bf16)
    for copy in copies[2 : 2 + FIELDS]:
        copy.wait()
    table = face_table(rows_of(loaded[0]), extract_ref[...])
    table_ref[...] = table
    share_rows(table, picked, shared_ref)
    for copy in copies[2 + FIELDS :]:
        copy.wait()


def first_local_kernel(
    state_ref, velocity_ref, neigh_ref, send_ref, table_ref, yz, lift, extract,
    maps_ref, device_ref, block_ref, out_ref, shared_ref, *map_refs
):
    fields = rows_of(state_ref)
    rate = local_rate(
        fields, velocity_ref, neigh_ref, table_ref[...], *split(yz[...]), lift[...]
    )
    base = fields + time_step * rate
    out_ref[...] = base.reshape(out_ref.shape)
    picked = pick_rows(column(send_ref), local_key(send_ref.shape[1]))
    share_rows(face_table(base + remainder(fields), extract[...]), picked, shared_ref)
    fill_maps(maps_ref, device_ref, block_ref, *map_refs)


def fill_maps(
    maps_ref, device_ref, block_ref, radial_ref, axial_ref, high_ref, low_ref
):
    elements = maps_ref.shape[2]
    row, lane = iota((elements, 128), 0), iota((elements, 128), 1)
    twice = ((lane & 63) == row).astype(f32).astype(bf16)
    radial_ref[...] = exact_dot(maps_ref[1], twice)
    swap = ((iota((64, 64), 0) >> 3) + 8 * (iota((64, 64), 0) & 7) == iota((64, 64), 1)).astype(f32)
    axial = [dot(swap.astype(bf16), part).astype(bf16) for part in split(maps_ref[2])]
    axial_ref[...] = dot(axial[0], twice) + dot(axial[1], twice)
    tile_row, tile_lane = iota((64, 1024), 0), iota((64, 1024), 1)
    tile = ((tile_row >> 3) == (tile_lane & 7)) & ((tile_row & 7) == (tile_lane >> 7))
    tile = jnp.where(tile, 1.0, 0.0).astype(bf16)
    values = [dot(part, tile) for part in split(maps_ref[0].T)]
    places = device_ref[...].astype(f32).T
    blocks = block_ref[...].astype(f32).T
    theta_lanes = high_ref.shape[1] // PB
    upper = (blocks >= PB).astype(f32)
    sector_key = places * TB + upper
    plane_key = blocks - PB * upper
    gap = jnp.zeros((64 - elements, high_ref.shape[1]), bf16)
    for y in range(8):
        start = y * 64
        high_ref[start + elements : start + 64, :] = gap
        low_ref[start + elements : start + 64, :] = gap
    for pb in range(PB):
        for tile_at in range(theta_lanes // 128):
            here = ((lane + tile_at * 128) >> 3).astype(f32)
            mine = (sector_key == here) & (plane_key == pb)
            begin = pb * theta_lanes + tile_at * 128
            for ref, value in zip((high_ref, low_ref), values):
                for y in range(8):
                    ref[y * 64 : y * 64 + elements, begin : begin + 128] = jnp.where(
                        mine, value[:, y * 128 : (y + 1) * 128], 0.0
                    ).astype(bf16)


def exact_dot(value, choice):
    high, low = split(value)
    return dot(high, choice) + dot(low, choice)


def second_local_kernel(
    state_ref, base_ref, velocity_ref, neigh_ref, send_ref, yz, lift, extract, cross, *refs
):
    shared_refs, (out_ref, added_ref, picked_ref) = refs[:-3], refs[-3:]
    elements = neigh_ref.shape[1]
    table = shared_table(shared_refs, elements).astype(bf16)
    keys = remote_keys(elements)
    picked = pick_faces(column(neigh_ref), keys)
    picked_ref[...] = picked
    terms = lift_rows(picked, table, lift[...], elements)
    first = rows_of(base_ref) + (time_step * penalty) * terms
    first_table = face_table(first + remainder(rows_of(state_ref)), extract[...])
    rate = local_rate(
        first, velocity_ref, neigh_ref, first_table, *split(yz[...]), lift[...]
    )
    second = 0.5 * (rows_of(state_ref) + first + time_step * rate)
    out_ref[...] = second.reshape(out_ref.shape)
    own = pick_rows(column(send_ref), local_key(elements))
    added_ref[:elements, :] = dot(own, first_table)
    names = jnp.concatenate([ref[-8:, :].T[:elements] for ref in shared_refs[1:]], axis=0)
    count = names.shape[0]
    pairs = facing_pairs(pick_faces(names, keys), table, count)
    face = names[:, 6:7]
    half = low_half((count, 128))
    same = half != ((face == 1) | (face == 3) | (face == 5))
    for c in range(FIELDS):
        faces = dot(pairs[c * count : (c + 1) * count], cross[...])
        added = jnp.where(face >= 2, faces[:, 128:256], faces[:, :128])
        added = jnp.where(face >= 4, faces[:, 256:], added)
        added = jnp.where(same, added, pltpu.roll(added, 64, 1))
        added_ref[elements:, c * 128 : (c + 1) * 128] = (time_step * penalty) * added


def exchange_plan(size):
    straight = [m for m in range(size // 2, 3 * size // 4) if m & 1]
    relayed = [m for m in range(size - 1, 1, -2) if m not in straight]
    return relayed, [m for m in range(size) if m not in relayed]


def sample_kernel(
    base_ref, picked_ref, added_ref, lift, radial_ref, axial_ref, high_ref, low_ref, *refs
):
    sectors = high_ref.shape[1] // (PB * TB * 8)
    shares = lax.axis_size("ax") - 1
    shared_refs = refs[:shares]
    new_ref, out_refs = refs[shares], refs[shares + 1 : -2]
    turned_ref, parts_ref = refs[-2:]
    elements = base_ref.shape[1]
    added = added_ref[elements:, :] + shared_table(shared_refs, elements)
    table = jnp.concatenate([added_ref[:elements, :], added], axis=0).astype(bf16)
    terms = lift_rows(picked_ref[...], table, lift[...], elements)
    new_state = rows_of(base_ref) + (0.5 * time_step * penalty) * terms
    new_ref[...] = new_state.reshape(new_ref.shape)
    gap = jnp.zeros((64 - elements, 128), f32)
    for c in range(FIELDS):
        for j in range(4):
            part = new_state[c * elements : (c + 1) * elements, j * 128 : (j + 1) * 128]
            after = pltpu.roll(part, 120, 1)
            turned_ref[c, j] = jnp.concatenate([part, gap, after, gap], axis=0).T
    radial = radial_ref[...]
    axial = axial_ref[...]
    theta_lanes = high_ref.shape[1] // PB
    groups = sectors // PB
    rows = 64 // groups
    for pair in range(2):
        tiles = []
        for yy in (2 * pair, 2 * pair + 1):
            values = []
            for c in range(FIELDS):
                inputs = []
                for x in range(8):
                    start = (x % 2) * 64 + 16 * yy
                    value = axial[0:8, :] * turned_ref[c, x // 2, start : start + 1, :]
                    for z in range(1, 8):
                        row = turned_ref[c, x // 2, start + z : start + z + 1, :]
                        value = value + axial[8 * z : 8 * z + 8, :] * row
                    inputs.append(value)
                for r in range(8):
                    value = radial_ref[8 * r : 8 * r + 1, :] * inputs[0]
                    for x in range(1, 8):
                        value = value + radial_ref[8 * r + x : 8 * r + x + 1, :] * inputs[x]
                    values.append(value)
            tiles.append(jnp.concatenate(values, axis=0))
        mapped_high, mapped_low = split(jnp.concatenate(tiles, axis=1))
        depth = slice(256 * pair, 256 * pair + 256)
        weight_high = high_ref[depth, :]
        part = (
            dot(mapped_high, weight_high)
            + dot(mapped_low, weight_high)
            + dot(mapped_high, low_ref[depth, :])
        )
        total = part if pair == 0 else total + part
    for pb in range(PB):
        for g in range(groups):
            for c in range(FIELDS):
                start = c * 64 + g * rows
                parts_ref[pb * groups + g, c * rows : (c + 1) * rows, :] = total[
                    start : start + rows, pb * theta_lanes : (pb + 1) * theta_lanes
                ]
    owner = lax.axis_index("az")
    relayed, kept = exchange_plan(sectors)
    for i, m in enumerate(relayed):
        out_refs[0][i] = parts_ref[owner ^ m]
    for i, m in enumerate(kept):
        out_refs[1 + i][...] = parts_ref[owner ^ m]


def fourier_kernel(table_ref, *refs):
    out_ref = refs[-1]
    total = refs[0][...]
    for ref in refs[1:-1]:
        total = total + ref[...]
    high, low = split(total)
    weight, weight_low = split(table_ref[...])
    coeffs = dot(
        jnp.concatenate([high, low], axis=1), jnp.concatenate([weight, weight], axis=0)
    ) + dot(high, weight_low)
    width = total.shape[1]
    rows = total.shape[0] // FIELDS
    for k in range(2):
        for c in range(FIELDS):
            out_ref[k, c] = coeffs[c * rows : (c + 1) * rows, k * width : (k + 1) * width]


def join_kernel(got_ref, *refs):
    count = len(refs) // 2
    for i in range(count - 1):
        refs[count + i][...] = refs[i][...] + got_ref[i]
    refs[-1][...] = refs[count - 1][...]


def store_kernel(new_ref, out_ref, sem):
    copy = pltpu.make_async_copy(new_ref, out_ref, sem)
    copy.start()
    copy.wait()


def shape(dims, dtype=f32):
    return jax.ShapeDtypeStruct(dims, dtype)


def call(kernel, outs, *args, scratch=(), flops=0, in_space=pltpu.VMEM, out_space=pltpu.VMEM, aliases={}):
    size = sum(math.prod(a.shape) * a.dtype.itemsize for a in list(args) + list(outs))
    return pl.pallas_call(
        kernel,
        out_shape=outs,
        in_specs=[pl.BlockSpec(memory_space=in_space)] * len(args),
        out_specs=tuple([pl.BlockSpec(memory_space=out_space)] * len(outs)),
        scratch_shapes=list(scratch),
        input_output_aliases=aliases,
        cost_estimate=pl.CostEstimate(flops=flops, bytes_accessed=size, transcendentals=0),
        compiler_params=pltpu.CompilerParams(vmem_limit_bytes=48 * 1024 * 1024),
    )(*args)


def exchange(value, axis):
    size = lax.axis_size(axis)
    return [value] + [
        lax.ppermute(value, axis, [(i, i ^ m) for i in range(size)]) for m in range(size - 1, 0, -1)
    ][::-1]


def per_device(state, velocity, interp_maps, neighbours, send_faces, owner_device, owner_block):
    elements = state.shape[0]
    sectors = lax.axis_size("az")
    inputs = (
        state.transpose(1, 0, 2),
        send_faces.reshape(1, elements),
        velocity.T,
        neighbours.T,
        interp_maps.transpose(1, 2, 3, 0).reshape(3, 64, elements),
        owner_device.reshape(1, elements),
        owner_block.reshape(1, elements),
    )
    yz_table = jnp.asarray(tile_tables(), f32)
    face_rows = shape((6 * elements, FIELDS * 128), bf16)
    travel = FIELDS * elements // 2
    sources = inputs + (yz_table,)
    sources = tuple(pltpu.with_memory_space_constraint(a, pltpu.HBM) for a in sources)
    loaded = call(
        load_kernel,
        tuple(shape(a.shape, a.dtype) for a in sources)
        + (shape((512, 512), bf16), shape((256, 512), bf16), shape((384, 384), bf16))
        + (face_rows, shape((travel + 8, 128))),
        *sources,
        scratch=(pltpu.SemaphoreType.DMA((len(sources) - 1 + FIELDS,)),),
        flops=400_000_000,
        in_space=pltpu.HBM,
    )
    fields, sends, speed, names, maps, places, blocks, yz, extract, lift, cross, table, shared = loaded
    cube = shape(fields.shape)
    others = exchange(shared, "ax")
    lanes = sectors * TB * 8
    weights = shape((512, PB * lanes), bf16)
    base, shared, radial, axial, weight_high, weight_low = call(
        first_local_kernel,
        (cube, shape((travel, 128)), shape((64, 128)), shape((64, 128)), weights, weights),
        fields, speed, names, sends, table, yz, lift, extract, maps, places, blocks,
        flops=1_000_000_000,
    )
    firsts = exchange(shared, "ax")
    shares = lax.axis_size("ax") * elements
    base, added, picked = call(
        second_local_kernel,
        (cube, shape((shares, FIELDS * 128)), shape((6 * elements, shares), bf16)),
        fields, base, speed, names, sends, yz, lift, extract, cross, *others,
        flops=1_500_000_000,
    )
    rows = FIELDS * 64 * PB // sectors
    piece = shape((rows, lanes))
    relayed, kept = exchange_plan(sectors)
    sampled = call(
        sample_kernel, (cube, shape((len(relayed), rows, lanes))) + (piece,) * len(kept),
        base, picked, added, lift, radial, axial, weight_high, weight_low, *firsts[1:],
        scratch=(
            pltpu.VMEM((FIELDS, 4, 128, 128), f32),
            pltpu.VMEM((sectors, rows, lanes), f32),
        ),
        flops=800_000_000,
    )
    new_state, bundle, pieces = sampled[0], sampled[1], dict(zip(kept, sampled[2:]))
    stored = call(
        store_kernel, (cube,), new_state, scratch=(pltpu.SemaphoreType.DMA,), out_space=pltpu.HBM
    )[0]

    def swap(value, mask):
        return lax.ppermute(value, "az", [(i, i ^ mask) for i in range(sectors)])

    bundle = swap(bundle, 1)
    joined = [m - 1 for m in relayed] + [1]
    arrived = [swap(pieces[m], m) for m in kept if m and m not in joined]
    sums = call(join_kernel, (piece,) * len(joined), bundle, *[pieces[m] for m in joined])
    arrived += [swap(value, m) for m, value in zip(joined, sums)]
    arrived.append(pieces[0])
    angle = 2.0 * np.pi / lanes * (np.outer(np.arange(lanes), np.arange(lanes)) % lanes)
    table = np.concatenate([np.cos(angle), -np.sin(angle)], axis=1) * lanes**-0.5
    spectrum = call(
        fourier_kernel, (shape((2, FIELDS, rows // FIELDS, lanes)),),
        jnp.asarray(table, f32), *arrived,
        flops=100_000_000,
    )[0]
    return stored.transpose(1, 0, 2), spectrum


def solution(mesh):
    return jax.shard_map(
        per_device,
        mesh=mesh,
        in_specs=(
            P(("az", "ax"), None, None),
            P(("az", "ax"), None),
            P(("az", "ax"), None, None, None),
            P(("az", "ax"), None),
            P(("az", "ax")),
            P(("az", "ax"), None),
            P(("az", "ax")),
        ),
        out_specs=(P(("az", "ax"), None, None), P(None, None, ("az", "ax"), None)),
        check_vma=False,
    )
```
